32 devices in a mesh: dp: 8 (over z, y), mp: 4 (over x, core).
Axes of the slice: x: 2, y: 2, z: 4, core: 2. Of those that a mesh axis runs over, the one named last changes fastest.
Arguments:
- patches: bfloat16 [32768, 768], P(('dp', 'mp')), may hold values from -6 to 6
- patch_pos: int32 [32768], P(('dp', 'mp')), may hold values from 0 to 127
- owner: int32 [32768, 1], P(('dp', 'mp')), may hold values from 0 to 3; in each aligned block of 1024 rows (0 to 1023, 1024 to 2047, ...) at most 384 rows name the same one
- local_row: int32 [32768], P(('dp', 'mp')), may hold values from 0 to 8255
- counts: int32 [32, 3], replicated, may hold values from 1 to 1023, as said below
- task: int32 [32], replicated, may hold values from 0 to 31
- table: float32 [33024, 768], P(('mp', 'dp'))
- table_mom: float32 [33024, 768], P(('mp', 'dp')), may hold values from -1.9073486e-05 to 1.9073486e-05
- table_avg: float32 [33024, 768], P(('mp', 'dp')), may hold values from -0.21875 to 0.21875
- patch_w: float32 [896, 768], P(('dp', 'mp')), may hold values from -0.21875 to 0.21875
- patch_mom: float32 [896, 768], P(('dp', 'mp')), may hold values from -1.9073486e-05 to 1.9073486e-05
- patch_avg: float32 [896, 768], P(('dp', 'mp')), may hold values from -0.21875 to 0.21875
- attn_w: float32 [768, 3072], P(('dp', 'mp'))
- attn_mom: float32 [768, 3072], P(('dp', 'mp')), may hold values from -1.9073486e-05 to 1.9073486e-05
- attn_avg: float32 [768, 3072], P(('dp', 'mp')), may hold values from -0.21875 to 0.21875
- up_w: float32 [768, 3072], P(('dp', 'mp')), may hold values from -0.21875 to 0.21875
- up_mom: float32 [768, 3072], P(('dp', 'mp')), may hold values from -1.9073486e-05 to 1.9073486e-05
- up_avg: float32 [768, 3072], P(('dp', 'mp')), may hold values from -0.21875 to 0.21875
- down_w: float32 [3072, 768], P(('dp', 'mp')), may hold values from -0.109375 to 0.109375
- down_mom: float32 [3072, 768], P(('dp', 'mp')), may hold values from -1.9073486e-05 to 1.9073486e-05
- down_avg: float32 [3072, 768], P(('dp', 'mp')), may hold values from -0.109375 to 0.109375
- gains: float32 [3, 768], P(None, ('dp', 'mp'))
- gain_mom: float32 [3, 768], P(None, ('dp', 'mp')), may hold values from -7.6293945e-05 to 7.6293945e-05
- gain_avg: float32 [3, 768], P(None, ('dp', 'mp')), may hold values from 0.5 to 1.5
Outputs:
- table_new: float32 [33024, 768], P(('mp', 'dp'))
- table_mom_new: float32 [33024, 768], P(('mp', 'dp'))
- table_avg_new: float32 [33024, 768], P(('mp', 'dp'))
- table_half: bfloat16 [33024, 768], P(('mp', 'dp'))
- patch_new: float32 [896, 768], P(('dp', 'mp'))
- patch_mom_new: float32 [896, 768], P(('dp', 'mp'))
- patch_avg_new: float32 [896, 768], P(('dp', 'mp'))
- patch_half: bfloat16 [896, 768], P(('dp', 'mp'))
- attn_new: float32 [768, 3072], P(('dp', 'mp'))
- attn_mom_new: float32 [768, 3072], P(('dp', 'mp'))
- attn_avg_new: float32 [768, 3072], P(('dp', 'mp'))
- attn_half: bfloat16 [768, 3072], P(('dp', 'mp'))
- up_new: float32 [768, 3072], P(('dp', 'mp'))
- up_mom_new: float32 [768, 3072], P(('dp', 'mp'))
- up_avg_new: float32 [768, 3072], P(('dp', 'mp'))
- up_half: bfloat16 [768, 3072], P(('dp', 'mp'))
- down_new: float32 [3072, 768], P(('dp', 'mp'))
- down_mom_new: float32 [3072, 768], P(('dp', 'mp'))
- down_avg_new: float32 [3072, 768], P(('dp', 'mp'))
- down_half: bfloat16 [3072, 768], P(('dp', 'mp'))
- gains_new: float32 [3, 768], P(None, ('dp', 'mp'))
- gain_mom_new: float32 [3, 768], P(None, ('dp', 'mp'))
- gain_avg_new: float32 [3, 768], P(None, ('dp', 'mp'))
- loss_sum: float32 [], replicated
- loss_count: float32 [], replicated
- clip_norm: float32 [], replicated
- rms_stats: float32 [4], replicated
The draws below stay inside these ranges and needn't reach their ends.
Inputs may be any that keep to these rules, and one draw needn't show every extreme that they name: In the rows of one device no owner is named more than 384 times; some owner exactly 384 times. `counts`: column 0 (patch tokens) is 1 to 768; column 1 (table tokens) is 256 or more, with columns 0 and 1 summing to 1024 at most; column 2 (scored tokens) is 1 to 256, reached.
All inputs are finite; a program needn't handle non-finite values.
Results may differ from the reference program's by a relative error of at most 0.013.
The reference program's roundings to bfloat16 on the way count: a program that leaves them out, or rounds other values in their place, can miss the bound.
Values may be sent and summed in bfloat16 or wider, within the bound.
No kernel may reach another device: no remote copies, remote signals or barrier semaphores. Data moves between devices by JAX's collectives and lax.ppermute only.
A program may use at most 512 MiB of HBM per device.

```python
import math
import jax
import jax.numpy as jnp
import numpy as np
from jax import lax

D = 768
HEADS = 24
HDIM = 32
FF = 3072
V = 33024
PIX = 768
POSN = 128
SEQ_LEN = 1024
SEQ_DEV = 1
LOSS = 256
TASKS = 32
OWNERS = 4
GROUPS = 8
TOK_DEV = 1024
SEQS = 32
TOKENS = 32768
VSH = 8256
CAP = 384


def draw_counts(key, part):
    key = jax.random.fold_in(key, 5)
    key_list = jax.random.split(key, 6)
    sequence = jnp.arange(SEQS, dtype=jnp.int32)
    device = sequence // SEQ_DEV
    across = device % OWNERS
    downward = device // OWNERS
    rising = downward * (OWNERS - 1) + across * (GROUPS - 1)
    span_total = 2 * (GROUPS - 1) * (OWNERS - 1)
    base_count = LOSS // 3 + (LOSS - LOSS // 3) * rising // span_total
    shrink = jax.random.randint(key_list[0], (SEQS,), 3, 5)
    scored = jnp.maximum(base_count * shrink // 4, 1)
    upper = SEQ_LEN - LOSS
    level_draw = jax.random.randint(key_list[1], (SEQS,), 0, 4)
    raw_patch = jax.random.randint(key_list[2], (SEQS,), upper // 2, upper + 1)
    patch_count = jnp.maximum(jnp.right_shift(raw_patch, 2 * level_draw), 1)
    chosen = jax.random.randint(key_list[3], (), 0, SEQS)
    other_seq = (chosen + 1 + jax.random.randint(key_list[4], (), 0, SEQS - 1)) % SEQS
    patch_count = jnp.where(sequence == chosen, upper, patch_count)
    patch_count = jnp.where(sequence == other_seq, 1, patch_count)
    room = SEQ_LEN - patch_count - LOSS
    pad_draw = jax.random.randint(key_list[5], (SEQS,), 0, 1 << 20)
    padding = pad_draw % (room // 4 + 1)
    padding = jnp.where(sequence == other_seq, 0, padding)
    table_count = SEQ_LEN - patch_count - padding
    scored = jnp.where(sequence == other_seq, LOSS, scored)
    return jnp.stack([patch_count, table_count, scored], 1).astype(jnp.int32)


def draw_table(key, part):
    key = jax.random.fold_in(key, 11)
    ramp = jnp.arange(V, dtype=jnp.float32)[:, None] / V
    jitter = jnp.clip(jax.random.normal(key, (V, D), jnp.float32), -6.0, 6.0)
    scale = 0.8 + 1.6 * ramp
    return jitter * scale * D ** (-0.5)


def draw_attn_w(key, part):
    key = jax.random.fold_in(key, 9)
    column = jnp.arange(4 * D)
    scale = jnp.where(column < 3 * D, 1.0, 8.0) * D ** (-0.5)
    jitter = jnp.clip(jax.random.normal(key, (D, 4 * D), jnp.float32), -6.0, 6.0)
    return jitter * scale[None, :]


def draw_gains(key, part):
    key = jax.random.fold_in(key, 7)
    ramp = 0.6 + 1.2 * jnp.arange(D, dtype=jnp.float32) / D
    jitter = jnp.clip(1.0 + 0.1 * jax.random.normal(key, (3, D), jnp.float32), 0.7, 1.3)
    return ramp[None, :] * jitter


def set_ends(values, rng, low, largest):
    index_at = [jax.random.randint(jax.random.fold_in(rng, axis), (), 0, length) for axis, length in enumerate(values.shape)]
    main_axis = values.shape.index(max(values.shape))
    beside = index_at[:main_axis] + [(index_at[main_axis] + 1) % values.shape[main_axis]] + index_at[main_axis + 1:]
    return values.at[tuple(index_at)].set(low).at[tuple(beside)].set(largest)


def block_levels(rng, shape, cuts, least, high):
    factor_of = 1.0
    for axis_at, parts in cuts:
        steps = jax.random.uniform(jax.random.fold_in(jax.random.fold_in(rng, 6), axis_at), (parts,), jnp.float32, least / len(cuts), high / len(cuts))
        factor_of = factor_of * jnp.repeat(jnp.exp(steps), shape[axis_at] // parts).reshape((-1,) + (1,) * (len(shape) - 1 - axis_at))
    return factor_of


def rank_bounds(amount, skew):
    loads = [(1 << 20) // math.isqrt(grade ** skew) + 1 for grade in range(1, amount + 1)]
    scale = 1 + sum(loads) // (1 << 30)
    return np.cumsum(np.array([max(1, weight // scale) for weight in loads]))


def skewed_ids(rng, dims, amount, slope):
    grid = rank_bounds(amount, slope)
    ticket = jax.random.randint(jax.random.fold_in(rng, 1), dims, 0, int(grid[amount - 1]))
    rank = jnp.searchsorted(jnp.asarray(grid, jnp.int32), ticket, side="right")
    return jax.random.permutation(jax.random.fold_in(rng, 2), amount)[rank].astype(jnp.int32)


def deal_out(key, own, number, rows, number_of, top, limit, slope):
    ranking = jax.random.permutation(key, number_of)
    crowded, usual = portions_of(number_of, rows * top, limit, slope, True), portions_of(number_of, rows * top, limit, slope, False)
    places = jnp.arange(number_of)

    def named(sizes, offset_by):
        used = int((sizes > 0).sum())
        fixed = max(1, used // 4)
        shifted = fixed + (places - fixed + offset_by * (used - fixed)) % max(1, number_of - fixed)
        return jnp.zeros((number_of,), jnp.int32).at[ranking[jnp.where(places < fixed, places, shifted)]].set(jnp.asarray(sizes, jnp.int32))

    sizes = jnp.where(number % 4 == 0, named(crowded, number // 4), named(usual, number - number // 4 - 1))
    mixed = jax.random.permutation(jax.random.fold_in(own, 3), number_of)
    source_of, taker = mixed[0:number_of // 2 * 2:2], mixed[1:number_of // 2 * 2:2]
    margin = jnp.minimum(sizes[source_of] - 1, limit - sizes[taker]) // 2
    margin = jnp.where((source_of == ranking[0]) | (taker == ranking[0]) | (sizes[taker] == 0), 0, jnp.maximum(margin, 0))
    shifted = jax.random.randint(jax.random.fold_in(own, 4), (number_of // 2,), 0, 1 << 20) % (margin + 1)
    sizes = sizes.at[source_of].add(-shifted).at[taker].add(shifted)
    labels = jnp.searchsorted(jnp.cumsum(sizes), jnp.arange(rows * top), side="right").astype(jnp.int32)
    grid = labels.reshape(top, rows).T
    grid = grid[jax.random.permutation(jax.random.fold_in(own, 1), rows)]
    offset_by = jax.random.randint(jax.random.fold_in(own, 2), (rows, 1), 0, top)
    return jnp.take_along_axis(grid, (jnp.arange(top)[None, :] + offset_by) % top, axis=1)


def portions_of(count, total, most, skew, full):
    portions = [(1 << 20) // math.isqrt(standing ** skew) + 1 for standing in range(1, count + 1)]
    largest = most if full else min(most, max(-(-total // count), total * portions[0] // sum(portions)))
    least = 1 if total - largest >= count - 1 else 0
    given, surplus = [largest] + [least] * (count - 1), total - largest - least * (count - 1)
    while surplus > 0:
        candidates = [i for i in range(1, count) if given[i] < largest] or [i for i in range(1, count) if given[i] < most]
        whole, budget = sum([portions[i] for i in candidates]), surplus
        for i in candidates:
            extra = min(most - given[i], max(1, budget * portions[i] // whole), surplus)
            given[i] = given[i] + extra
            surplus = surplus - extra
    return np.array(given)


def bell_draw(key, dims, scale, bound, cuts=(), held_as=jnp.bfloat16):
    drawn = jax.random.normal(key, dims, jnp.float32) * scale
    if len(cuts) > 0:
        drawn = block_levels(key, dims, cuts, -0.22, 0.18) * drawn
    return jnp.clip(drawn, min=-bound, max=bound).astype(held_as)


def setup_inputs(seed: int = 0) -> dict:
    key_of = jax.random.split(jax.random.key(seed), 25)
    patches = bell_draw(key_of[0], (TOKENS, PIX), 1.0, 6.0, ((0, 32),))
    patch_pos = set_ends(jax.random.randint(key_of[1], (TOKENS,), 0, POSN), jax.random.fold_in(key_of[1], 1), 0, POSN - 1).astype(jnp.int32)
    owner_keys = jax.random.split(jax.random.fold_in(key_of[2], 1), TOKENS // TOK_DEV)
    owner_turns = jax.random.permutation(jax.random.fold_in(key_of[2], 3), TOKENS // TOK_DEV)
    owner = jax.vmap(lambda own, number: deal_out(jax.random.fold_in(key_of[2], 2), own, number, TOK_DEV, OWNERS, 1, CAP, 2))(owner_keys, owner_turns).reshape((TOKENS, 1))
    local_row = set_ends(skewed_ids(key_of[3], (TOKENS,), VSH, 2), jax.random.fold_in(key_of[3], 3), 0, VSH - 1).astype(jnp.int32)
    counts = draw_counts(jax.random.fold_in(key_of[24], 71), 0)
    task = set_ends(jax.random.randint(key_of[5], (SEQS,), 0, TASKS), jax.random.fold_in(key_of[5], 1), 0, TASKS - 1).astype(jnp.int32)
    table = draw_table(jax.random.fold_in(key_of[24], 71), 0)
    table_mom = bell_draw(key_of[7], (V, D), (0.02 * (V * D + (PIX + POSN) * D + 6 * D * D + 2 * D * FF + 3 * D) ** -0.5), 1.9073486328125e-05, ((0, 32),), jnp.float32)
    table_avg = bell_draw(key_of[8], (V, D), D ** -0.5, 0.21875, ((0, 32),), jnp.float32)
    patch_w = bell_draw(key_of[9], (PIX + POSN, D), PIX ** -0.5, 0.21875, ((0, 32),), jnp.float32)
    patch_mom = bell_draw(key_of[10], (PIX + POSN, D), (0.02 * (V * D + (PIX + POSN) * D + 6 * D * D + 2 * D * FF + 3 * D) ** -0.5), 1.9073486328125e-05, ((0, 32),), jnp.float32)
    patch_avg = bell_draw(key_of[11], (PIX + POSN, D), PIX ** -0.5, 0.21875, ((0, 32),), jnp.float32)
    attn_w = draw_attn_w(jax.random.fold_in(key_of[24], 71), 0)
    attn_mom = bell_draw(key_of[13], (D, 4 * D), (0.02 * (V * D + (PIX + POSN) * D + 6 * D * D + 2 * D * FF + 3 * D) ** -0.5), 1.9073486328125e-05, ((0, 32),), jnp.float32)
    attn_avg = bell_draw(key_of[14], (D, 4 * D), D ** -0.5, 0.21875, ((0, 32),), jnp.float32)
    up_w = bell_draw(key_of[15], (D, FF), D ** -0.5, 0.21875, ((0, 32),), jnp.float32)
    up_mom = bell_draw(key_of[16], (D, FF), (0.02 * (V * D + (PIX + POSN) * D + 6 * D * D + 2 * D * FF + 3 * D) ** -0.5), 1.9073486328125e-05, ((0, 32),), jnp.float32)
    up_avg = bell_draw(key_of[17], (D, FF), D ** -0.5, 0.21875, ((0, 32),), jnp.float32)
    down_w = bell_draw(key_of[18], (FF, D), FF ** -0.5, 0.109375, ((0, 32),), jnp.float32)
    down_mom = bell_draw(key_of[19], (FF, D), (0.02 * (V * D + (PIX + POSN) * D + 6 * D * D + 2 * D * FF + 3 * D) ** -0.5), 1.9073486328125e-05, ((0, 32),), jnp.float32)
    down_avg = bell_draw(key_of[20], (FF, D), FF ** -0.5, 0.109375, ((0, 32),), jnp.float32)
    gains = draw_gains(jax.random.fold_in(key_of[24], 71), 0)
    gain_mom = bell_draw(key_of[22], (3, D), (0.08 * (V * D + (PIX + POSN) * D + 6 * D * D + 2 * D * FF + 3 * D) ** -0.5), 7.62939453125e-05, ((1, 32),), jnp.float32)
    gain_avg = jnp.clip(1.0 + 0.1 * jax.random.normal(key_of[23], (3, D), jnp.float32), 0.5, 1.5)
    return dict(patches=patches, patch_pos=patch_pos, owner=owner, local_row=local_row, counts=counts, task=task, table=table, table_mom=table_mom, table_avg=table_avg, patch_w=patch_w, patch_mom=patch_mom, patch_avg=patch_avg, attn_w=attn_w, attn_mom=attn_mom, attn_avg=attn_avg, up_w=up_w, up_mom=up_mom, up_avg=up_avg, down_w=down_w, down_mom=down_mom, down_avg=down_avg, gains=gains, gain_mom=gain_mom, gain_avg=gain_avg)


NORM_EPS = 1e-05
STEP_RATE = 5000.0
MOMENTUM = 0.5
AVERAGE_DECAY = 0.5
CLIP_LIMIT = 0.02
HIGHEST = lax.Precision.HIGHEST

@jax.custom_vjp
def low(v):
    return lax.optimization_barrier(v.astype(jnp.bfloat16)).astype(jnp.float32)

@jax.custom_vjp
def low_back(v):
    return v

def low_keep(v):
    return (low(v), None)

def low_pass(kept, grad):
    return (grad,)

def back_keep(v):
    return (v, None)

def back_low(kept, grad):
    return (low(grad),)
low.defvjp(low_keep, low_pass)
low_back.defvjp(back_keep, back_low)

def product(left, right):
    return jnp.dot(left, right, precision=HIGHEST, preferred_element_type=jnp.float32)

def layer_norm(values, gain):
    row_mean = lax.optimization_barrier(jnp.mean(values, -1, keepdims=True))
    centred = values - row_mean
    spread = lax.optimization_barrier(jnp.mean(centred * centred, -1, keepdims=True))
    return centred * lax.rsqrt(spread + NORM_EPS) * gain

def square_sum(values, valid):
    return jnp.sum(jnp.where(valid, lax.optimization_barrier(jnp.mean(values * values, -1, keepdims=True)), 0.0))

def sequence_loss(weights_low, inputs_seq):
    table_low, patch_low, attn_low, up_low, down_low, gain_low = weights_low
    patch_in, token_ids, patch_count, live_count, scored_count, inverse_weight = inputs_seq
    positions = jnp.arange(SEQ_LEN, dtype=jnp.int32)
    is_patch = (positions < patch_count)[:, None]
    is_token = ((positions >= patch_count) & (positions < patch_count + live_count))[:, None]
    looked = low_back(table_low[token_ids])
    from_patch = low_back(product(patch_in, patch_low))
    embedded = jnp.where(is_patch, from_patch, 0.0) + jnp.where(is_token, math.sqrt(D) * looked, 0.0)
    normed_first = low(layer_norm(embedded, gain_low[0]))
    projected = low(low_back(product(normed_first, attn_low[:, :3 * D])))
    query_rows = projected[:, :D].reshape(SEQ_LEN, HEADS, HDIM)
    key_rows = projected[:, D:2 * D].reshape(SEQ_LEN, HEADS, HDIM)
    value_rows = projected[:, 2 * D:].reshape(SEQ_LEN, HEADS, HDIM)
    scores = low_back(jnp.einsum('qhd,khd->hqk', query_rows, key_rows, precision=HIGHEST) * HDIM ** (-0.5))
    allowed = positions[None, :] <= positions[:, None]
    scores = jnp.where(allowed[None], scores, -1e+30)
    row_top = lax.optimization_barrier(jnp.max(scores, -1, keepdims=True))
    exponent = jnp.exp(scores - row_top)
    probability = low(exponent / lax.optimization_barrier(jnp.sum(exponent, -1, keepdims=True)))
    attended = jnp.einsum('hqk,khd->qhd', probability, value_rows, precision=HIGHEST).reshape(SEQ_LEN, D)
    attended = low(low_back(attended))
    branch = low_back(product(attended, attn_low[:, 3 * D:]))
    middle = embedded + branch
    normed_second = low(layer_norm(middle, gain_low[1]))
    hidden = low_back(product(normed_second, up_low))
    active = low(jax.nn.gelu(hidden, approximate=True))
    second = low_back(product(active, down_low))
    result = middle + second
    final_rows = layer_norm(result, gain_low[2])
    head_rows = low(lax.dynamic_slice_in_dim(final_rows, (patch_count - 1).astype(jnp.int32), LOSS, 0))
    target_rows = lax.dynamic_slice_in_dim(looked, patch_count.astype(jnp.int32), LOSS, 0)
    logits = low_back(product(head_rows, table_low.T))
    logit_top = lax.optimization_barrier(jnp.max(logits, -1, keepdims=True))
    log_total = logit_top[:, 0] + jnp.log(lax.optimization_barrier(jnp.sum(jnp.exp(logits - logit_top), -1)))
    picked = lax.optimization_barrier(jnp.sum(head_rows * target_rows, -1))
    row_weight = (jnp.arange(LOSS) < scored_count).astype(jnp.float32) * inverse_weight
    loss_part = jnp.sum(row_weight * (log_total - picked))
    valid = (positions < patch_count + live_count)[:, None]
    stat_sums = jnp.stack([square_sum(embedded, valid), square_sum(branch, valid), square_sum(second, valid), square_sum(result, valid)])
    return (loss_part, stat_sums)

def renew(weight, moment, average, gradient, factor):
    clipped = gradient * factor
    moment_new = MOMENTUM * moment + clipped
    weight_new = weight - STEP_RATE * (clipped + MOMENTUM * moment_new)
    average_new = AVERAGE_DECAY * average + (1.0 - AVERAGE_DECAY) * weight_new
    return (weight_new, moment_new, average_new)

def reference(patches, patch_pos, owner, local_row, counts, task, table, table_mom, table_avg, patch_w, patch_mom, patch_avg, attn_w, attn_mom, attn_avg, up_w, up_mom, up_avg, down_w, down_mom, down_avg, gains, gain_mom, gain_avg):
    token_ids = (owner[:, 0] * VSH + local_row).astype(jnp.int32).reshape(SEQS, SEQ_LEN)
    onehot = (patch_pos[:, None] == jnp.arange(POSN)[None, :]).astype(jnp.float32)
    patch_in = jnp.concatenate([patches.astype(jnp.float32), onehot], 1).reshape(SEQS, SEQ_LEN, PIX + POSN)
    scored = counts[:, 2].astype(jnp.float32)
    per_task = (task[:, None] == jnp.arange(TASKS)[None, :]).astype(jnp.float32)
    task_total = lax.optimization_barrier(jnp.sum(per_task * scored[:, None], 0))
    present = jnp.sum((task_total > 0).astype(jnp.float32))
    inverse_seq = lax.optimization_barrier(jnp.sum(per_task / jnp.maximum(task_total, 1.0)[None, :], 1))
    weights_all = (table, patch_w, attn_w, up_w, down_w, gains)

    def whole_loss(weights_now):
        weights_low = tuple((low(matrix) for matrix in weights_now))

        def seq_step(accum, inputs_seq):
            loss_part, stat_sums = jax.checkpoint(sequence_loss)(weights_low, inputs_seq)
            return ((accum[0] + loss_part, accum[1] + stat_sums), None)
        start = (jnp.zeros((), jnp.float32), jnp.zeros((4,), jnp.float32))
        (loss_total, stat_total), _ = lax.scan(seq_step, start, (patch_in, token_ids, counts[:, 0], counts[:, 1], counts[:, 2], inverse_seq))
        return (loss_total / present, (loss_total, stat_total))
    _, pullback, (loss_total, stat_total) = jax.vjp(whole_loss, weights_all, has_aux=True)
    gradient_list, = pullback(jnp.ones((), jnp.float32))
    squares = sum((jnp.sum(gradient * gradient) for gradient in gradient_list))
    clip_norm = jnp.sqrt(squares)
    factor = jnp.minimum(1.0, CLIP_LIMIT / clip_norm)
    states = ((table, table_mom, table_avg), (patch_w, patch_mom, patch_avg), (attn_w, attn_mom, attn_avg), (up_w, up_mom, up_avg), (down_w, down_mom, down_avg), (gains, gain_mom, gain_avg))
    renewed = [renew(state[0], state[1], state[2], gradient, factor) for state, gradient in zip(states, gradient_list)]
    valid_total = jnp.sum(counts[:, :2].astype(jnp.float32))
    rms_stats = jnp.sqrt(stat_total / valid_total)
    table_out, patch_out, attn_out, up_out, down_out, gain_out = renewed
    return (table_out[0], table_out[1], table_out[2], table_out[0].astype(jnp.bfloat16), patch_out[0], patch_out[1], patch_out[2], patch_out[0].astype(jnp.bfloat16), attn_out[0], attn_out[1], attn_out[2], attn_out[0].astype(jnp.bfloat16), up_out[0], up_out[1], up_out[2], up_out[0].astype(jnp.bfloat16), down_out[0], down_out[1], down_out[2], down_out[0].astype(jnp.bfloat16), gain_out[0], gain_out[1], gain_out[2], loss_total, present, clip_norm, rms_stats)
```

```python
import math

import jax
import jax.numpy as jnp
from jax import lax
from jax.experimental import pallas as pl
from jax.experimental.pallas import tpu as pltpu
from jax.sharding import PartitionSpec as P

D = 768
HEADS = 24
HDIM = 32
POSN = 128
SEQ_LEN = 1024
LOSS = 256
TASKS = 32

NORM_EPS = 1e-05
STEP_RATE = 5000.0
MOMENTUM = 0.5
AVERAGE_DECAY = 0.5
CLIP_LIMIT = 0.02

AXES = ("dp", "mp")
LANES = 128
GROUP = LANES // HDIM
TILES = D // LANES
SCALE = HDIM ** (-0.5)
SCALE_LOG2 = SCALE * math.log2(math.e)
VMEM = 56 * 2**20
bf16 = jnp.bfloat16
f32 = jnp.float32


def contract(left, right, left_dim, right_dim):
    return lax.dot_general(
        left, right, (((left_dim,), (right_dim,)), ((), ())), preferred_element_type=f32
    )


def nn(left, right):
    return contract(left, right, 1, 0)


def nt(left, right):
    return contract(left, right, 1, 1)


def tn(left, right):
    return contract(left, right, 0, 0)


def layer_norm(values, gain):
    row_mean = jnp.mean(values, -1, keepdims=True)
    centred = values - row_mean
    spread = jnp.mean(centred * centred, -1, keepdims=True)
    return centred * lax.rsqrt(spread + NORM_EPS) * gain


def gelu_tanh(values):
    return jax.nn.gelu(values, approximate=True)


def head_masks():
    lane = lax.broadcasted_iota(jnp.int32, (1, LANES), 1) // HDIM
    return [lane == head for head in range(GROUP)]


def only(mask, block):
    return jnp.where(mask, block, jnp.zeros((), block.dtype))


def attention_all_kernel(q_ref, k_ref, v_ref, o_ref, *, block):
    length = q_ref.shape[0]
    masks = head_masks()
    row = lax.broadcasted_iota(jnp.int32, (block, block), 0)
    col = lax.broadcasted_iota(jnp.int32, (block, block), 1)
    triangle = col <= row
    for index in range(length // block):
        start, end = index * block, (index + 1) * block
        q = q_ref[start:end, :]
        k, v = k_ref[0:end, :], v_ref[0:end, :]
        joined = jnp.zeros((block, LANES), f32)
        for mask in masks:
            scores = nt(only(mask, q), k)
            diagonal = jnp.where(triangle, scores[:, start:], -1e30)
            scores = jnp.concatenate([scores[:, :start], diagonal], 1) if index else diagonal
            top = jnp.max(scores, 1, keepdims=True) * SCALE_LOG2
            power = jnp.exp2(scores * SCALE_LOG2 - top)
            total = jnp.sum(power, 1, keepdims=True)
            joined = jnp.where(mask, nn(power.astype(bf16), v) / total, joined)
        o_ref[start:end, :] = joined.astype(bf16)


def attention_all(queries, key_values):
    length = queries.shape[0]
    return pl.pallas_call(
        lambda *refs: attention_all_kernel(*refs, block=512),
        grid=(TILES,),
        in_specs=[
            pl.BlockSpec((length, LANES), lambda g: (0, g)),
            pl.BlockSpec((length, LANES), lambda g: (0, g)),
            pl.BlockSpec((length, LANES), lambda g: (0, TILES + g)),
        ],
        out_specs=pl.BlockSpec((length, LANES), lambda g: (0, g)),
        out_shape=jax.ShapeDtypeStruct((length, D), bf16),
        compiler_params=pltpu.CompilerParams(vmem_limit_bytes=VMEM),
        cost_estimate=pl.CostEstimate(
            flops=2 * 2 * HEADS * length * length * LANES, bytes_accessed=8 * length * D,
            transcendentals=HEADS * length * length,
        ),
        name="attention_all",
    )(queries, key_values, key_values)


def attention_pick_kernel(first_ref, q_ref, k_ref, v_ref, o_ref, lse_ref):
    rows, length = q_ref.shape[0], k_ref.shape[0]
    masks = head_masks()
    row = lax.broadcasted_iota(jnp.int32, (rows, length), 0)
    col = lax.broadcasted_iota(jnp.int32, (rows, length), 1)
    allowed = col <= row + first_ref[0]
    lane = lax.broadcasted_iota(jnp.int32, (1, LANES), 1)
    q, k, v = q_ref[...], k_ref[...], v_ref[...]
    joined = jnp.zeros((rows, LANES), f32)
    stat = jnp.zeros((rows, LANES), f32)
    for head, mask in enumerate(masks):
        scores = jnp.where(allowed, nt(only(mask, q), k), -1e30)
        top = jnp.max(scores, 1, keepdims=True) * SCALE_LOG2
        power = jnp.exp2(scores * SCALE_LOG2 - top)
        total = jnp.sum(power, 1, keepdims=True)
        joined = jnp.where(mask, nn(power.astype(bf16), v) / total, joined)
        stat = jnp.where(lane == head, top + jnp.log2(total), stat)
    o_ref[...] = joined.astype(bf16)
    lse_ref[0] = stat.T[0:8, :]


def attention_pick(first, queries, key_values):
    rows, length = queries.shape[0], key_values.shape[0]
    return pl.pallas_call(
        attention_pick_kernel,
        grid_spec=pltpu.PrefetchScalarGridSpec(
            num_scalar_prefetch=1,
            grid=(TILES,),
            in_specs=[
                pl.BlockSpec((rows, LANES), lambda g, s: (0, g)),
                pl.BlockSpec((length, LANES), lambda g, s: (0, g)),
                pl.BlockSpec((length, LANES), lambda g, s: (0, TILES + g)),
            ],
            out_specs=[
                pl.BlockSpec((rows, LANES), lambda g, s: (0, g)),
                pl.BlockSpec((1, 8, rows), lambda g, s: (g, 0, 0)),
            ],
        ),
        out_shape=[
            jax.ShapeDtypeStruct((rows, D), bf16),
            jax.ShapeDtypeStruct((TILES, 8, rows), f32),
        ],
        compiler_params=pltpu.CompilerParams(vmem_limit_bytes=VMEM),
        cost_estimate=pl.CostEstimate(
            flops=2 * 2 * HEADS * rows * length * LANES, bytes_accessed=6 * length * D,
            transcendentals=HEADS * rows * length,
        ),
        name="attention_pick",
    )(first, queries, key_values, key_values)


def attention_back_kernel(
    first_ref, q_ref, k_ref, v_ref, o_ref, do_ref, lse_ref, dq_ref, dk_ref, dv_ref
):
    rows, length = q_ref.shape[0], k_ref.shape[0]
    masks = head_masks()
    key = lax.broadcasted_iota(jnp.int32, (length, rows), 0)
    query = lax.broadcasted_iota(jnp.int32, (length, rows), 1)
    allowed = key <= query + first_ref[0]
    q, k, v, do = q_ref[...], k_ref[...], v_ref[...], do_ref[...]
    share = (
        lax.broadcasted_iota(jnp.int32, (8, LANES), 0)
        == lax.broadcasted_iota(jnp.int32, (8, LANES), 1) // HDIM
    ).astype(f32)
    inner = lax.dot_general(
        share, do.astype(f32) * o_ref[...].astype(f32), (((1,), (1,)), ((), ())),
        preferred_element_type=f32, precision=lax.Precision.HIGHEST,
    )
    lse = lse_ref[0]
    dq = jnp.zeros((rows, LANES), f32)
    dk = jnp.zeros((length, LANES), f32)
    dv = jnp.zeros((length, LANES), f32)
    for head, mask in enumerate(masks):
        k_head = only(mask, k)
        scores = nt(k_head, q)
        chance = jnp.where(
            allowed, jnp.exp2(scores * SCALE_LOG2 - lse[head : head + 1, :]), 0.0
        )
        d_chance = nt(only(mask, v), do)
        d_scores = (chance * (d_chance - inner[head : head + 1, :])).astype(bf16)
        dv = jnp.where(mask, nn(chance.astype(bf16), do), dv)
        dk = jnp.where(mask, nn(d_scores, q), dk)
        dq = dq + tn(d_scores, k_head)
    dq_ref[...] = (dq * SCALE).astype(bf16)
    dk_ref[...] = (dk * SCALE).astype(bf16)
    dv_ref[...] = dv.astype(bf16)


def attention_back(first, queries, key_values, attended, grad_attended, lse):
    rows, length = queries.shape[0], key_values.shape[0]
    rows_spec = pl.BlockSpec((rows, LANES), lambda g, s: (0, g))
    all_spec = pl.BlockSpec((length, LANES), lambda g, s: (0, g))
    return pl.pallas_call(
        attention_back_kernel,
        grid_spec=pltpu.PrefetchScalarGridSpec(
            num_scalar_prefetch=1,
            grid=(TILES,),
            in_specs=[
                rows_spec,
                all_spec,
                pl.BlockSpec((length, LANES), lambda g, s: (0, TILES + g)),
                rows_spec,
                rows_spec,
                pl.BlockSpec((1, 8, rows), lambda g, s: (g, 0, 0)),
            ],
            out_specs=[rows_spec, all_spec, all_spec],
        ),
        out_shape=[
            jax.ShapeDtypeStruct((rows, D), bf16),
            jax.ShapeDtypeStruct((length, D), bf16),
            jax.ShapeDtypeStruct((length, D), bf16),
        ],
        compiler_params=pltpu.CompilerParams(vmem_limit_bytes=VMEM),
        cost_estimate=pl.CostEstimate(
            flops=5 * 2 * HEADS * rows * length * LANES, bytes_accessed=10 * length * D,
            transcendentals=HEADS * rows * length,
        ),
        name="attention_back",
    )(first, queries, key_values, key_values, attended, grad_attended, lse)


def split_high(values):
    high = lax.reduce_precision(values, 8, 7)
    return high, values - high


def with_lse(packed):
    lse = packed[..., D : D + 3].astype(f32)
    return packed[..., :D].astype(f32), lse[..., 0:1] + lse[..., 1:2] + lse[..., 2:3]


def pack_lse(mean, lse):
    high, low = split_high(lse)
    low, rest = split_high(low)
    return jnp.concatenate(
        [mean, high, low, rest, jnp.zeros(mean.shape[:-1] + (LANES - 3,), f32)], -1
    ).astype(bf16)


def merge(first, second):
    joint = jnp.logaddexp(first[1], second[1])
    mean = first[0] * jnp.exp(first[1] - joint) + second[0] * jnp.exp(second[1] - joint)
    return mean, joint


def head_scan_kernel(rows_ref, *refs, carried, last):
    split = len(refs) - (1 if last else 2)
    refs, outs = refs[:split], refs[split:]
    rows = rows_ref[...]
    top = total = mixed = None
    if carried:
        mixed, top = refs[0][...].astype(f32), refs[1][...]
        total = jnp.ones_like(top)
        refs = refs[2:]
    for at in range(0, len(refs), 2):
        chunk = refs[at][...]
        if at + 1 < len(refs):
            chunk = jnp.concatenate([chunk, refs[at + 1][...]], 0)
        logits = nt(rows, chunk)
        here = jnp.max(logits, 1, keepdims=True)
        if top is None:
            top = here
            power = jnp.exp(logits - top)
            total = jnp.sum(power, 1, keepdims=True)
            mixed = nn(power.astype(bf16), chunk)
        else:
            joint = jnp.maximum(top, here)
            shrink = jnp.exp(top - joint)
            power = jnp.exp(logits - joint)
            total = total * shrink + jnp.sum(power, 1, keepdims=True)
            mixed = mixed * shrink + nn(power.astype(bf16), chunk)
            top = joint
    lse = top + jnp.log(total)
    if len(outs) == 2:
        outs[0][...], outs[1][...] = mixed / total, lse
    else:
        outs[0][:, :D] = (mixed / total).astype(bf16)
        high = lse.astype(bf16).astype(f32)
        low = (lse - high).astype(bf16).astype(f32)
        rest = lse - high - low
        lane = lax.broadcasted_iota(jnp.int32, (1, LANES), 1)
        tail = jnp.where(lane == 0, high, jnp.where(lane == 1, low, jnp.where(lane == 2, rest, 0.0)))
        outs[0][:, D:] = tail.astype(bf16)


def head_scan(rows, chunks, carry=(), last=True):
    count, block = rows.shape[0], 512
    vocab = sum(chunk.shape[0] for chunk in chunks)
    wide = pl.BlockSpec((block, D), lambda i: (i, 0))
    thin = pl.BlockSpec((block, 1), lambda i: (i, 0))
    if last:
        out_specs = [pl.BlockSpec((block, D + LANES), lambda i: (i, 0))]
        out_shape = [jax.ShapeDtypeStruct((count, D + LANES), bf16)]
    else:
        out_specs = [wide, thin]
        out_shape = [jax.ShapeDtypeStruct((count, D), f32), jax.ShapeDtypeStruct((count, 1), f32)]
    return pl.pallas_call(
        lambda *refs: head_scan_kernel(*refs, carried=bool(carry), last=last),
        grid=(count // block,),
        in_specs=[wide]
        + [wide, thin][: len(carry)]
        + [
            pl.BlockSpec(chunk.shape, lambda i: (0, 0), pipeline_mode=pl.Buffered(1))
            for chunk in chunks
        ],
        out_specs=out_specs,
        out_shape=out_shape,
        compiler_params=pltpu.CompilerParams(vmem_limit_bytes=VMEM),
        cost_estimate=pl.CostEstimate(
            flops=4 * count * vocab * D, bytes_accessed=2 * vocab * D + 4 * count * D,
            transcendentals=count * vocab,
        ),
        name="head_scan",
    )(rows, *carry, *chunks)


def head_grad_kernel(table_ref, rows_ref, weight_ref, out_ref):
    rows = rows_ref[:, :D]
    tail = rows_ref[:, D:].astype(f32).T
    logits = nt(table_ref[...], rows)
    lse = tail[0:1] + tail[1:2] + tail[2:3]
    grad = (jnp.exp(logits - lse) * weight_ref[0]).astype(bf16)
    part = nn(grad, rows)

    @pl.when(pl.program_id(0) == 0)
    def _():
        out_ref[...] = part

    @pl.when(pl.program_id(0) > 0)
    def _():
        out_ref[...] += part


def head_grad(table_low, rows, weight):
    vocab, count, block = table_low.shape[0], rows.shape[0], 2048
    steps = count // block
    return pl.pallas_call(
        head_grad_kernel,
        grid=(steps,),
        in_specs=[
            pl.BlockSpec((vocab, D), lambda i: (0, 0)),
            pl.BlockSpec((block, D + LANES), lambda i: (i, 0)),
            pl.BlockSpec((1, 1, block), lambda i: (i, 0, 0)),
        ],
        out_specs=pl.BlockSpec((vocab, D), lambda i: (0, 0)),
        out_shape=jax.ShapeDtypeStruct((vocab, D), f32),
        compiler_params=pltpu.CompilerParams(vmem_limit_bytes=VMEM),
        cost_estimate=pl.CostEstimate(
            flops=4 * count * vocab * D, bytes_accessed=2 * count * D + 6 * vocab * D,
            transcendentals=count * vocab,
        ),
        name="head_grad",
    )(table_low, rows, weight.reshape(steps, 1, block))


def permute(value, axis, target):
    return lax.ppermute(value, axis, [(i, target(i)) for i in range(lax.axis_size(axis))])


def other_core(value):
    return permute(value, "mp", lambda i: i ^ 1)


def along_x(value, step):
    chips = lax.axis_size("mp") // 2
    return permute(value, "mp", lambda i: (i // 2 + step) % chips * 2 + i % 2)


def ring_order(count):
    return list(range(0, count, 2)) + list(range(count - 1, 0, -2))


def after(value, *others):
    return lax.optimization_barrier((value, *others))[0]


def ring_hop(upward, downward):
    count = lax.axis_size("dp")
    order = ring_order(count)
    spot = [order.index(i) for i in range(count)]
    return (
        permute(upward, "dp", lambda i: order[(spot[i] + 1) % count]),
        permute(downward, "dp", lambda i: order[(spot[i] - 1) % count]),
    )


def ring_rest(first, gates):
    count = lax.axis_size("dp")
    upward, downward = first
    pieces = []
    for step in range(2, count // 2 + 1):
        upward, downward, _ = lax.optimization_barrier(
            (upward, downward, gates[min(step - 2, len(gates) - 1)])
        )
        if 2 * step == count:
            half = upward.shape[0] // 32 * 16
            upward, downward = upward[:half], downward[half:]
        upward, downward = ring_hop(upward, downward)
        pieces += [upward, downward]
    return pieces


def sum_everywhere(values):
    world = lax.axis_size(AXES)
    row = jnp.pad(values, (0, LANES - values.shape[0]))
    spread = jnp.broadcast_to(row[None, :], (world, LANES))
    return jnp.sum(lax.all_to_all(spread, AXES, 0, 0, tiled=True), 0)[: values.shape[0]]


def one_hot(index, count):
    return (index[:, None] == jnp.arange(count, dtype=jnp.int32)[None, :]).astype(bf16)


def placed(index, values, count):
    hit = index[None, :] == jnp.arange(count, dtype=jnp.int32)[:, None]
    return jnp.max(jnp.where(hit, values[None, :], -1), 1)


def rank_before(choice):
    count = choice.shape[0]
    earlier = (
        jnp.arange(count)[None, :] < jnp.arange(count)[:, None]
    ).astype(bf16)
    return jnp.dot(earlier, choice.astype(bf16), preferred_element_type=f32)


def unblocks(packed, rows):
    return jnp.concatenate(
        [packed[j : j + rows] for j in range(0, packed.shape[0], rows)], 1
    )


def grad_pack_kernel(core_ref, *refs, plan, rows_of, world):
    refs = dict(enumerate(refs))
    for left, right, held in plan:
        refs[held][...] = tn(refs[left][...], refs[right][...])
    mine_ref, theirs_ref = refs[rows_of[-1][0]], refs[rows_of[-1][0] + 1]
    second = core_ref[0] == 1
    total = mine_ref.shape[1]
    for j in range(world // 2):
        mine, theirs, filled = [], [], 0
        for held, rows, column in rows_of[:-1]:
            low = refs[held][2 * j * rows : (2 * j + 1) * rows, column : column + D]
            high = refs[held][(2 * j + 1) * rows : (2 * j + 2) * rows, column : column + D]
            mine.append(jnp.where(second, high, low))
            theirs.append(jnp.where(second, low, high))
            filled += rows
        if filled < total:
            mine.append(jnp.zeros((total - filled, D), f32))
            theirs.append(mine[-1])
        mine_ref[j] = jnp.concatenate(mine, 0).astype(bf16)
        theirs_ref[j] = jnp.concatenate(theirs, 0).astype(bf16)


def grad_pack(products, rows, world):
    core = jnp.reshape(lax.axis_index("mp") % 2, (1,)).astype(jnp.int32)
    operands = [value for product in products for value in product] + list(rows)
    inputs, count = len(operands), len(products)
    plan = [(2 * i, 2 * i + 1, inputs + 2 + i) for i in range(count)]
    pieces, scratch, flops = [], [], 0
    for i, (left, right) in enumerate(products):
        flops += 2 * left.shape[0] * left.shape[1] * right.shape[1]
        scratch.append(pltpu.VMEM((left.shape[1], right.shape[1]), f32))
        for column in range(0, right.shape[1], D):
            pieces.append((inputs + 2 + i, left.shape[1] // world, column))
    for i, value in enumerate(rows):
        pieces.append((2 * count + i, value.shape[0] // world, 0))
    total = -(-sum(piece[1] for piece in pieces) // 16) * 16
    pieces.append((inputs, 0, 0))
    shape = jax.ShapeDtypeStruct((world // 2, total, D), bf16)
    return pl.pallas_call(
        lambda *refs: grad_pack_kernel(*refs, plan=plan, rows_of=pieces, world=world),
        in_specs=[pl.BlockSpec(memory_space=pltpu.SMEM)]
        + [pl.BlockSpec(memory_space=pltpu.VMEM)] * inputs,
        out_specs=[pl.BlockSpec(memory_space=pltpu.VMEM)] * 2,
        out_shape=[shape, shape],
        scratch_shapes=scratch,
        compiler_params=pltpu.CompilerParams(vmem_limit_bytes=VMEM),
        cost_estimate=pl.CostEstimate(
            flops=flops, bytes_accessed=4 * world // 2 * total * D, transcendentals=0
        ),
        name="grad_pack",
    )(core, *operands)


class RingSum:

    def __init__(self, mine, theirs):
        self.count = lax.axis_size("dp")
        self.chips = lax.axis_size("mp") // 2
        shape = (self.count, self.chips, -1, D)
        self.got = other_core(theirs).reshape(shape)
        self.mine = mine.reshape(shape)
        self.order = ring_order(self.count)
        spot = [self.order.index(i) for i in range(self.count)]
        self.here = jnp.asarray(spot, jnp.int32)[lax.axis_index("dp")]
        self.up_steps, self.down_steps = self.count // 2, (self.count - 1) // 2
        self.upward = self.part(self.up_steps).astype(bf16)
        self.downward = self.part(-self.down_steps).astype(bf16)
        self.step = 0

    def part(self, step):
        at = jnp.asarray(self.order, jnp.int32)[(self.here + step) % self.count]
        return lax.dynamic_index_in_dim(self.mine, at, 0, keepdims=False).astype(f32) + (
            lax.dynamic_index_in_dim(self.got, at, 0, keepdims=False).astype(f32)
        )

    def hop(self):
        self.step += 1
        step, down = self.step, self.downward
        self.upward, down = ring_hop(self.upward, down)
        if step <= self.down_steps:
            self.downward = down
        if step < self.up_steps:
            self.upward = (self.upward.astype(f32) + self.part(self.up_steps - step)).astype(bf16)
        if step < self.down_steps:
            self.downward = (self.downward.astype(f32) + self.part(step - self.down_steps)).astype(
                bf16
            )

    def before(self, value):
        return lax.optimization_barrier((value, self.upward, self.downward))[0]

    def total(self, gate=None):
        while self.step < self.up_steps:
            self.hop()
        line = (
            self.part(0) + self.upward.astype(f32) + self.downward.astype(f32)
        ).astype(bf16)
        if gate is not None:
            line = after(line, gate)
        chip = lax.axis_index("mp") // 2
        total = lax.dynamic_index_in_dim(line, chip, 0, keepdims=False).astype(f32)
        for step in range(1, self.chips):
            going = lax.dynamic_index_in_dim(line, (chip + step) % self.chips, 0, keepdims=False)
            total = total + along_x(going, step).astype(f32)
        return total


def renew(weight, moment, average, gradient, factor):
    clipped = gradient * factor
    moment_new = MOMENTUM * moment + clipped
    weight_new = weight - STEP_RATE * (clipped + MOMENTUM * moment_new)
    average_new = AVERAGE_DECAY * average + (1.0 - AVERAGE_DECAY) * weight_new
    return (weight_new, moment_new, average_new)


def shards(
    patches,
    patch_pos,
    owner,
    local_row,
    counts,
    task,
    table,
    table_mom,
    table_avg,
    patch_w,
    patch_mom,
    patch_avg,
    attn_w,
    attn_mom,
    attn_avg,
    up_w,
    up_mom,
    up_avg,
    down_w,
    down_mom,
    down_avg,
    gains,
    gain_mom,
    gain_avg,
):
    groups, owners = lax.axis_size("dp"), lax.axis_size("mp")
    world = groups * owners
    tokens_here = patches.shape[0]
    rows_own = table.shape[0]
    rows_attn, rows_patch, rows_down = attn_w.shape[0], patch_w.shape[0], down_w.shape[0]
    cols_gain = gains.shape[1]
    place = lax.axis_index("dp") * owners + lax.axis_index("mp")

    table_low = table.astype(bf16)
    gain_row = jnp.pad(gains.astype(bf16).reshape(1, 3 * cols_gain), ((0, 0), (0, 4 * D - 3 * cols_gain)))
    patch_rows = jnp.pad(patch_w.astype(bf16), ((0, -rows_patch % 4), (0, 0)))
    early = jnp.concatenate([attn_w.astype(bf16), patch_rows.reshape(-1, 4 * D), gain_row], 0)
    late = jnp.concatenate(
        [
            up_w.astype(bf16),
            jnp.concatenate(
                [down_w[j : j + rows_attn] for j in range(0, rows_down, rows_attn)], 1
            ).astype(bf16),
        ],
        0,
    )
    early_all, late_all = (
        lax.all_gather(jnp.pad(w, ((0, -w.shape[0] % 8), (0, 0))), AXES, axis=0, tiled=False)
        for w in (early, late)
    )
    first_pieces = ring_hop(table_low, table_low)

    my_counts = lax.dynamic_slice_in_dim(counts, place, 1, 0)
    first_tok, alive = my_counts[0, 0], my_counts[0, 1]
    positions = jnp.arange(tokens_here, dtype=jnp.int32)
    is_patch = (positions < first_tok)[:, None]
    is_token = (positions >= first_tok) & (positions < first_tok + alive)
    is_valid = (positions < first_tok + alive)[:, None]
    target_owner = owner[:, 0]

    share = -(-3 * tokens_here // (2 * world) // 16) * 16
    identity = target_owner * (rows_own * groups) + local_row
    same = (identity[:, None] == identity[None, :]) & is_token[None, :]
    first_same = jnp.min(jnp.where(same, positions[None, :], tokens_here), 1)
    leads = is_token & (first_same == positions)
    dest = identity // rows_own
    leads_to = (dest[:, None] == jnp.arange(world)[None, :]) & leads[:, None]
    lead_rank = jnp.sum(jnp.where(leads_to, rank_before(leads_to), 0.0), 1).astype(jnp.int32)
    far_rank = jnp.max(
        jnp.where(first_same[:, None] == positions[None, :], lead_rank[None, :], 0), 1
    )
    far_row = identity - dest * rows_own
    most = jnp.max(jnp.sum(leads_to.astype(jnp.int32), 0))

    def far_slots(start, share):
        within = far_rank - start
        fits = is_token & (within >= 0) & (within < share)
        return jnp.where(fits, dest * share + within, -1)

    def far_ids(slots, extra, share):
        ids = placed(slots, far_row, world * share).reshape(world, share)
        ids = jnp.concatenate([ids, jnp.full((world, 1), extra, jnp.int32)], 1)
        return lax.all_to_all(ids, ("mp", "dp"), split_axis=0, concat_axis=0, tiled=True)

    first_slots = far_slots(0, share)
    first_ids = far_ids(first_slots, most, share)
    few = 16
    turns = (jnp.max(first_ids[:, share]) - share + few - 1) // few

    def far_fetch(slots, ids, share):
        spread = one_hot(ids[:, :share].reshape(-1), rows_own)
        rows = jnp.dot(spread, table_low, preferred_element_type=f32).astype(bf16)
        rows = lax.optimization_barrier((rows, *first_pieces))[0]
        arrived = lax.all_to_all(
            rows.reshape(world, share, D), ("mp", "dp"), split_axis=0, concat_axis=0, tiled=True
        ).reshape(world * share, D)
        return arrived, jnp.dot(one_hot(slots, world * share), arrived, preferred_element_type=f32)

    def far_pack(slots, values, share):
        return jnp.dot(
            one_hot(slots, world * share).T, values, preferred_element_type=f32
        ).astype(bf16)

    def far_send(packed, share):
        return lax.all_to_all(
            packed.reshape(world, share, D),
            ("mp", "dp"), split_axis=0, concat_axis=0, tiled=True,
        ).reshape(world * share, D)

    def far_add(arrived, ids, share):
        spread = one_hot(ids[:, :share].reshape(-1), rows_own)
        return tn(spread, arrived)

    arrived, looked = far_fetch(first_slots, first_ids, share)

    def fetch_turn(turn, total):
        slots = far_slots(share + turn * few, few)
        return total + far_fetch(slots, far_ids(slots, 0, few), few)[1]

    looked = lax.fori_loop(0, turns, fetch_turn, looked)

    def columns(gathered, low, high):
        return gathered[:, :rows_attn, low * D : high * D].reshape(-1, (high - low) * D)

    w_q, w_kv, w_out = columns(early_all, 0, 1), columns(early_all, 1, 3), columns(early_all, 3, 4)
    gain_at = rows_attn + patch_rows.shape[0] // 4
    w_patch = (
        early_all[:, rows_attn:gain_at].reshape(world, -1, D)[:, :rows_patch].reshape(-1, D)
    )
    gain_all = (
        early_all[:, gain_at, : 3 * cols_gain]
        .reshape(world, 3, cols_gain).transpose(1, 0, 2).reshape(3, D).astype(f32)
    )
    w_up = columns(late_all, 0, 4)
    w_down = jnp.concatenate(
        [late_all[:, rows_attn : 2 * rows_attn, j : j + D] for j in range(0, 4 * D, D)], 1
    ).reshape(world * rows_down, D)

    position_code = (patch_pos[:, None] == jnp.arange(POSN)[None, :]).astype(bf16)
    patch_in = jnp.concatenate([patches, position_code], 1)
    from_patch = jnp.dot(patch_in, w_patch, preferred_element_type=f32)
    embed_scale = math.sqrt(D)
    embedded = jnp.where(is_patch, from_patch, 0.0) + embed_scale * looked
    normed_first, first_back = jax.vjp(layer_norm, embedded, gain_all[0])
    normed_first = normed_first.astype(bf16)
    key_values = jnp.dot(normed_first, w_kv, preferred_element_type=f32).astype(bf16)

    pick = first_tok - 1
    pick_at = jnp.reshape(pick, (1,))

    def picked_rows(values, start=pick):
        return lax.dynamic_slice_in_dim(values, start, LOSS, 0)

    normed_pick = picked_rows(normed_first)
    query_pick = jnp.dot(normed_pick, w_q, preferred_element_type=f32).astype(bf16)
    attended_pick, lse_pick = attention_pick(pick_at, query_pick, key_values)
    branch_pick = jnp.dot(attended_pick, w_out, preferred_element_type=f32)
    middle_pick = picked_rows(embedded) + branch_pick
    normed_mid, mid_back = jax.vjp(layer_norm, middle_pick, gain_all[1])
    normed_mid = normed_mid.astype(bf16)
    query_all = jnp.dot(normed_first, w_q, preferred_element_type=f32).astype(bf16)
    attended = attention_all(query_all, key_values)
    normed_mid = after(normed_mid, attended)
    hidden_pick = jnp.dot(normed_mid, w_up, preferred_element_type=f32)
    active_f32, gelu_back = jax.vjp(gelu_tanh, hidden_pick)
    active_pick = active_f32.astype(bf16)
    result_pick = middle_pick + jnp.dot(active_pick, w_down, preferred_element_type=f32)
    final_rows, final_back = jax.vjp(layer_norm, result_pick, gain_all[2])
    own_rows = final_rows.astype(bf16)
    pieces = ring_rest(first_pieces, (arrived, attended, own_rows))
    chunks = [table_low, *first_pieces, *pieces]
    target_rows = picked_rows(looked, first_tok)

    chips = owners // 2
    line = jnp.stack([own_rows] + [along_x(own_rows, step) for step in range(1, chips)])
    group_rows = jnp.stack([line, other_core(line)])
    group_rows = group_rows.reshape(-1, D)
    near = 5
    carry = head_scan(group_rows, chunks[:near], last=False)
    (scanned,) = head_scan(group_rows, chunks[near:], carry)
    scanned = scanned.reshape(2, chips, LOSS, D + LANES)
    there = other_core(scanned[1])
    line = pack_lse(*merge(with_lse(scanned[0]), with_lse(there)))
    own = with_lse(line[0])
    for step in range(1, chips):
        own = merge(own, with_lse(along_x(line[step], -step)))
    mean_own, own_total = own[0], own[1][:, 0]

    picked = jnp.sum(own_rows.astype(f32) * target_rows, 1)
    scored_all = counts[:, 2].astype(f32)
    per_task = (task[:, None] == jnp.arange(TASKS)[None, :]).astype(f32)
    task_total = jnp.sum(per_task * scored_all[:, None], 0)
    present = jnp.sum((task_total > 0).astype(f32))
    inverse_seq = jnp.sum(per_task / jnp.maximum(task_total, 1.0)[None, :], 1)
    row_live = (jnp.arange(LOSS)[None, :] < counts[:, 2:3]).astype(f32) * inverse_seq[:, None]
    own_weight = lax.dynamic_slice_in_dim(row_live, place, 1, 0)[0]
    loss_part = jnp.sum(own_weight * (own_total - picked))

    rows_all = lax.all_gather(
        pack_lse(own_rows.astype(f32), own_total[:, None]), AXES, axis=0, tiled=True
    )

    scaled_weight = (own_weight / present)[:, None]
    grad_rows = scaled_weight * (mean_own - target_rows)
    grad_result, grad_gain_last = final_back(grad_rows)
    grad_second = grad_result.astype(bf16)
    grad_hidden = gelu_back(nt(grad_second, w_down))[0].astype(bf16)
    grad_middle, grad_gain_mid = mid_back(nt(grad_hidden, w_up))
    grad_middle = grad_result + grad_middle
    grad_branch = grad_middle.astype(bf16)
    late_mine, late_theirs = grad_pack(
        [(normed_mid, grad_hidden), (active_pick, grad_second), (attended_pick, grad_branch)],
        [], world,
    )
    late_sum = RingSum(late_mine, late_theirs)
    grad_attended = late_sum.before(nt(grad_branch, w_out).astype(bf16))
    late_sum.hop()
    grad_q, grad_k, grad_v = attention_back(
        pick_at, query_pick, key_values, attended_pick, grad_attended, lse_pick
    )
    grad_kv = late_sum.before(jnp.concatenate([grad_k, grad_v], 1))
    late_sum.hop()
    def back_in_place(rows, start):
        whole = jnp.zeros((tokens_here, D), f32)
        return lax.dynamic_update_slice_in_dim(whole, rows, start, 0)

    grad_normed = nt(grad_kv, w_kv) + back_in_place(nt(grad_q, w_q), pick)
    grad_normed = late_sum.before(grad_normed)
    late_sum.hop()
    grad_embedded, grad_gain_first = first_back(grad_normed)
    grad_embedded = grad_embedded + back_in_place(grad_middle, pick)
    grad_looked = (
        embed_scale * grad_embedded
        + back_in_place(-scaled_weight * own_rows.astype(f32), first_tok)
    ).astype(bf16)
    grad_looked = late_sum.before(grad_looked)
    packed = far_pack(first_slots, grad_looked, share)
    grad_patch_rows = jnp.where(is_patch, grad_embedded, 0.0).astype(bf16)
    grad_gain = jnp.stack([grad_gain_first, grad_gain_mid, grad_gain_last])
    gain_part = grad_gain.reshape(3, world, cols_gain).transpose(1, 0, 2)
    gain_part = jnp.pad(gain_part.reshape(world, 3 * cols_gain), ((0, 0), (0, D - 3 * cols_gain)))
    early_mine, early_theirs = grad_pack(
        [
            (normed_pick, grad_q),
            (normed_first, grad_k),
            (normed_first, grad_v),
            (patch_in, after(grad_patch_rows, packed)),
        ],
        [gain_part], world,
    )
    table_head = head_grad(table_low, after(rows_all, early_theirs), row_live / present)
    grad_arrived = far_send(packed, share)
    summed_early = RingSum(early_mine, early_theirs).total()
    summed_late = late_sum.total(grad_arrived)
    grad_table = table_head + far_add(grad_arrived, first_ids, share)

    def next_turn(turn, total):
        slots = far_slots(share + turn * few, few)
        return total + far_add(
            far_send(far_pack(slots, grad_looked, few), few), far_ids(slots, 0, few), few
        )

    grad_table = lax.fori_loop(0, turns, next_turn, grad_table)

    attended = after(attended, late_theirs)
    branch = jnp.dot(attended, w_out, preferred_element_type=f32)
    middle = embedded + branch
    normed_second = layer_norm(middle, gain_all[1]).astype(bf16)
    hidden = jnp.dot(normed_second, w_up, preferred_element_type=f32)
    second = jnp.dot(gelu_tanh(hidden).astype(bf16), w_down, preferred_element_type=f32)
    result = middle + second

    def square_sum(values):
        return jnp.sum(jnp.where(is_valid, jnp.mean(values * values, 1, keepdims=True), 0.0))

    edge = 3 * rows_attn
    summed_up = unblocks(summed_late[: 4 * rows_attn], rows_attn)
    summed_down = summed_late[4 * rows_attn : 4 * rows_attn + rows_down]
    out_at = 4 * rows_attn + rows_down
    summed_attn = jnp.concatenate(
        [unblocks(summed_early[:edge], rows_attn), summed_late[out_at : out_at + rows_attn]], 1
    )
    summed_patch = summed_early[edge : edge + rows_patch]
    summed_gain = summed_early[edge + rows_patch, : 3 * cols_gain].reshape(3, cols_gain)
    gradient_list = (grad_table, summed_patch, summed_attn, summed_up, summed_down, summed_gain)
    squares = sum((jnp.sum(gradient * gradient) for gradient in gradient_list))
    totals = sum_everywhere(
        jnp.stack(
            [
                squares,
                loss_part,
                square_sum(embedded),
                square_sum(branch),
                square_sum(second),
                square_sum(result),
            ]
        )
    )
    clip_norm = jnp.sqrt(totals[0])
    loss_total = totals[1]
    factor = jnp.minimum(1.0, CLIP_LIMIT / clip_norm)
    states = (
        (table, table_mom, table_avg),
        (patch_w, patch_mom, patch_avg),
        (attn_w, attn_mom, attn_avg),
        (up_w, up_mom, up_avg),
        (down_w, down_mom, down_avg),
        (gains, gain_mom, gain_avg),
    )
    renewed = [
        renew(state[0], state[1], state[2], gradient, factor)
        for state, gradient in zip(states, gradient_list)
    ]
    valid_total = jnp.sum(counts[:, :2].astype(f32))
    rms_stats = jnp.sqrt(totals[2:6] / valid_total)
    outputs = []
    for state in renewed[:-1]:
        outputs.extend([state[0], state[1], state[2], state[0].astype(bf16)])
    outputs.extend(renewed[-1])
    return (*outputs, loss_total, present, clip_norm, rms_stats)


def solution(mesh):
    whole, split = P(), P(AXES)
    rows, vocab, columns = P(AXES, None), P(("mp", "dp"), None), P(None, AXES)
    in_specs = (rows, split, rows, split, whole, whole) + (vocab,) * 3 + (rows,) * 12 + (columns,) * 3
    out_specs = (vocab,) * 4 + (rows,) * 16 + (columns,) * 3 + (whole,) * 4
    return jax.shard_map(shards, mesh=mesh, in_specs=in_specs, out_specs=out_specs, check_vma=False)
```

```python
import math

import jax
import jax.numpy as jnp
from jax import lax
from jax.experimental import pallas as pl
from jax.experimental.pallas import tpu as pltpu
from jax.sharding import PartitionSpec as P

D = 768
HEADS = 24
HDIM = 32
POSN = 128
SEQ_LEN = 1024
LOSS = 256
TASKS = 32

NORM_EPS = 1e-05
STEP_RATE = 5000.0
MOMENTUM = 0.5
AVERAGE_DECAY = 0.5
CLIP_LIMIT = 0.02

AXES = ("dp", "mp")
LANES = 128
GROUP = LANES // HDIM
TILES = D // LANES
SCALE = HDIM ** (-0.5)
SCALE_LOG2 = SCALE * math.log2(math.e)
VMEM = 56 * 2**20
HEAD_BLOCK = 2048
bf16 = jnp.bfloat16
f32 = jnp.float32


def contract(left, right, left_dim, right_dim):
    return lax.dot_general(
        left, right, (((left_dim,), (right_dim,)), ((), ())), preferred_element_type=f32
    )


def nn(left, right):
    return contract(left, right, 1, 0)


def nt(left, right):
    return contract(left, right, 1, 1)


def tn(left, right):
    return contract(left, right, 0, 0)


def layer_norm(values, gain):
    row_mean = jnp.mean(values, -1, keepdims=True)
    centred = values - row_mean
    spread = jnp.mean(centred * centred, -1, keepdims=True)
    return centred * lax.rsqrt(spread + NORM_EPS) * gain


def gelu_tanh(values):
    return jax.nn.gelu(values, approximate=True)


def head_masks():
    lane = lax.broadcasted_iota(jnp.int32, (1, LANES), 1) // HDIM
    return [lane == head for head in range(GROUP)]


def only(mask, block):
    return jnp.where(mask, block, jnp.zeros((), block.dtype))


def attention_all_kernel(q_ref, k_ref, v_ref, o_ref, *, block):
    length = q_ref.shape[0]
    masks = head_masks()
    row = lax.broadcasted_iota(jnp.int32, (block, block), 0)
    col = lax.broadcasted_iota(jnp.int32, (block, block), 1)
    triangle = col <= row
    for index in range(length // block):
        start, end = index * block, (index + 1) * block
        q = q_ref[start:end, :]
        k, v = k_ref[0:end, :], v_ref[0:end, :]
        joined = jnp.zeros((block, LANES), f32)
        for mask in masks:
            scores = nt(only(mask, q), k)
            diagonal = jnp.where(triangle, scores[:, start:], -1e30)
            scores = jnp.concatenate([scores[:, :start], diagonal], 1) if index else diagonal
            top = jnp.max(scores, 1, keepdims=True) * SCALE_LOG2
            power = jnp.exp2(scores * SCALE_LOG2 - top)
            total = jnp.sum(power, 1, keepdims=True)
            joined = jnp.where(mask, nn(power.astype(bf16), v) / total, joined)
        o_ref[start:end, :] = joined.astype(bf16)


def attention_all(queries, key_values):
    length = queries.shape[0]
    return pl.pallas_call(
        lambda *refs: attention_all_kernel(*refs, block=512),
        grid=(TILES,),
        in_specs=[
            pl.BlockSpec((length, LANES), lambda g: (0, g)),
            pl.BlockSpec((length, LANES), lambda g: (0, g)),
            pl.BlockSpec((length, LANES), lambda g: (0, TILES + g)),
        ],
        out_specs=pl.BlockSpec((length, LANES), lambda g: (0, g)),
        out_shape=jax.ShapeDtypeStruct((length, D), bf16),
        compiler_params=pltpu.CompilerParams(vmem_limit_bytes=VMEM),
        cost_estimate=pl.CostEstimate(
            flops=2 * 2 * HEADS * length * length * LANES, bytes_accessed=8 * length * D,
            transcendentals=HEADS * length * length,
        ),
        name="attention_all",
    )(queries, key_values, key_values)


def attention_pick_kernel(first_ref, q_ref, k_ref, v_ref, o_ref, lse_ref):
    rows, length = q_ref.shape[0], k_ref.shape[0]
    masks = head_masks()
    row = lax.broadcasted_iota(jnp.int32, (rows, length), 0)
    col = lax.broadcasted_iota(jnp.int32, (rows, length), 1)
    allowed = col <= row + first_ref[0]
    lane = lax.broadcasted_iota(jnp.int32, (1, LANES), 1)
    q, k, v = q_ref[...], k_ref[...], v_ref[...]
    joined = jnp.zeros((rows, LANES), f32)
    stat = jnp.zeros((rows, LANES), f32)
    for head, mask in enumerate(masks):
        scores = jnp.where(allowed, nt(only(mask, q), k), -1e30)
        top = jnp.max(scores, 1, keepdims=True) * SCALE_LOG2
        power = jnp.exp2(scores * SCALE_LOG2 - top)
        total = jnp.sum(power, 1, keepdims=True)
        joined = jnp.where(mask, nn(power.astype(bf16), v) / total, joined)
        stat = jnp.where(lane == head, top + jnp.log2(total), stat)
    o_ref[...] = joined.astype(bf16)
    lse_ref[0] = stat.T[0:8, :]


def attention_pick(first, queries, key_values):
    rows, length = queries.shape[0], key_values.shape[0]
    return pl.pallas_call(
        attention_pick_kernel,
        grid_spec=pltpu.PrefetchScalarGridSpec(
            num_scalar_prefetch=1,
            grid=(TILES,),
            in_specs=[
                pl.BlockSpec((rows, LANES), lambda g, s: (0, g)),
                pl.BlockSpec((length, LANES), lambda g, s: (0, g)),
                pl.BlockSpec((length, LANES), lambda g, s: (0, TILES + g)),
            ],
            out_specs=[
                pl.BlockSpec((rows, LANES), lambda g, s: (0, g)),
                pl.BlockSpec((1, 8, rows), lambda g, s: (g, 0, 0)),
            ],
        ),
        out_shape=[
            jax.ShapeDtypeStruct((rows, D), bf16),
            jax.ShapeDtypeStruct((TILES, 8, rows), f32),
        ],
        compiler_params=pltpu.CompilerParams(vmem_limit_bytes=VMEM),
        cost_estimate=pl.CostEstimate(
            flops=2 * 2 * HEADS * rows * length * LANES, bytes_accessed=6 * length * D,
            transcendentals=HEADS * rows * length,
        ),
        name="attention_pick",
    )(first, queries, key_values, key_values)


def attention_back_kernel(
    first_ref, q_ref, k_ref, v_ref, o_ref, do_ref, lse_ref, dq_ref, dk_ref, dv_ref
):
    rows, length = q_ref.shape[0], k_ref.shape[0]
    masks = head_masks()
    key = lax.broadcasted_iota(jnp.int32, (length, rows), 0)
    query = lax.broadcasted_iota(jnp.int32, (length, rows), 1)
    allowed = key <= query + first_ref[0]
    q, k, v, do = q_ref[...], k_ref[...], v_ref[...], do_ref[...]
    share = (
        lax.broadcasted_iota(jnp.int32, (8, LANES), 0)
        == lax.broadcasted_iota(jnp.int32, (8, LANES), 1) // HDIM
    ).astype(f32)
    inner = lax.dot_general(
        share, do.astype(f32) * o_ref[...].astype(f32), (((1,), (1,)), ((), ())),
        preferred_element_type=f32, precision=lax.Precision.HIGHEST,
    )
    lse = lse_ref[0]
    dq = jnp.zeros((rows, LANES), f32)
    dk = jnp.zeros((length, LANES), f32)
    dv = jnp.zeros((length, LANES), f32)
    for head, mask in enumerate(masks):
        k_head = only(mask, k)
        scores = nt(k_head, q)
        chance = jnp.where(
            allowed, jnp.exp2(scores * SCALE_LOG2 - lse[head : head + 1, :]), 0.0
        )
        d_chance = nt(only(mask, v), do)
        d_scores = (chance * (d_chance - inner[head : head + 1, :])).astype(bf16)
        dv = jnp.where(mask, nn(chance.astype(bf16), do), dv)
        dk = jnp.where(mask, nn(d_scores, q), dk)
        dq = dq + tn(d_scores, k_head)
    dq_ref[...] = (dq * SCALE).astype(bf16)
    dk_ref[...] = (dk * SCALE).astype(bf16)
    dv_ref[...] = dv.astype(bf16)


def attention_back(first, queries, key_values, attended, grad_attended, lse):
    rows, length = queries.shape[0], key_values.shape[0]
    rows_spec = pl.BlockSpec((rows, LANES), lambda g, s: (0, g))
    all_spec = pl.BlockSpec((length, LANES), lambda g, s: (0, g))
    return pl.pallas_call(
        attention_back_kernel,
        grid_spec=pltpu.PrefetchScalarGridSpec(
            num_scalar_prefetch=1,
            grid=(TILES,),
            in_specs=[
                rows_spec,
                all_spec,
                pl.BlockSpec((length, LANES), lambda g, s: (0, TILES + g)),
                rows_spec,
                rows_spec,
                pl.BlockSpec((1, 8, rows), lambda g, s: (g, 0, 0)),
            ],
            out_specs=[rows_spec, all_spec, all_spec],
        ),
        out_shape=[
            jax.ShapeDtypeStruct((rows, D), bf16),
            jax.ShapeDtypeStruct((length, D), bf16),
            jax.ShapeDtypeStruct((length, D), bf16),
        ],
        compiler_params=pltpu.CompilerParams(vmem_limit_bytes=VMEM),
        cost_estimate=pl.CostEstimate(
            flops=5 * 2 * HEADS * rows * length * LANES, bytes_accessed=10 * length * D,
            transcendentals=HEADS * rows * length,
        ),
        name="attention_back",
    )(first, queries, key_values, key_values, attended, grad_attended, lse)


def first_back_kernel(
    bounds_ref, k_ref, v_ref, wkv_ref, q_ref, wq_ref, x_ref, gain_ref, middle_ref, target_ref,
    patch_ref, looked_ref, dgain_ref, normed, residual, pulled,
):
    length, block = x_ref.shape[0], 128
    first = bounds_ref[0]
    normed[0:length, :] = nt(k_ref[...], wkv_ref[:, :D]) + nt(v_ref[...], wkv_ref[:, D:])
    residual[...] = jnp.zeros_like(residual)
    pulled[...] = jnp.zeros_like(pulled)

    def place(ref, rows, start):
        base = pl.multiple_of(start // 8 * 8, 8)
        padded = jnp.concatenate([rows, jnp.zeros((8, D), f32)], 0)
        turned = pltpu.roll(padded, start - base, 0)
        at = pl.ds(base, rows.shape[0] + 8)
        ref[at, :] = ref[at, :] + turned

    place(normed, nt(q_ref[...], wq_ref[...]), first - 1)
    place(residual, middle_ref[...], first - 1)
    place(pulled, target_ref[...], first)
    gain = gain_ref[...]
    dgain = jnp.zeros((1, D), f32)
    for start in range(0, length, block):
        at = slice(start, start + block)
        x, grad = x_ref[at, :], normed[at, :]
        centred = x - jnp.mean(x, 1, keepdims=True)
        spread = lax.rsqrt(jnp.mean(centred * centred, 1, keepdims=True) + NORM_EPS)
        unit = centred * spread
        dgain = dgain + jnp.sum(grad * unit, 0, keepdims=True)
        scaled = grad * gain
        inner = jnp.mean(scaled * unit, 1, keepdims=True)
        back = spread * (scaled - jnp.mean(scaled, 1, keepdims=True) - unit * inner)
        back = back + residual[at, :]
        row = start + lax.broadcasted_iota(jnp.int32, (block, 1), 0)
        patch_ref[at, :] = jnp.where(row < first, back, 0.0).astype(bf16)
        looked_ref[at, :] = (math.sqrt(D) * back + pulled[at, :]).astype(bf16)
    dgain_ref[...] = dgain


def first_back(first, grad_k, grad_v, w_kv, grad_q, w_q, embedded, gain, middle, target):
    length = embedded.shape[0]
    wide = jax.ShapeDtypeStruct((length, D), bf16)
    return pl.pallas_call(
        first_back_kernel,
        in_specs=[pl.BlockSpec(memory_space=pltpu.SMEM)]
        + [pl.BlockSpec(memory_space=pltpu.VMEM)] * 9,
        out_specs=[pl.BlockSpec(memory_space=pltpu.VMEM)] * 3,
        out_shape=[wide, wide, jax.ShapeDtypeStruct((1, D), f32)],
        scratch_shapes=[pltpu.VMEM((length + 16, D), f32)] * 3,
        compiler_params=pltpu.CompilerParams(vmem_limit_bytes=VMEM),
        cost_estimate=pl.CostEstimate(
            flops=2 * length * 2 * D * D, bytes_accessed=16 * length * D, transcendentals=0
        ),
        name="first_back",
    )(first, grad_k, grad_v, w_kv, grad_q, w_q, embedded, gain, middle, target)


def write_with_lse(ref, mean, lse):
    ref[:, :D] = mean.astype(bf16)
    high = lse.astype(bf16).astype(f32)
    low = (lse - high).astype(bf16).astype(f32)
    rest = lse - high - low
    lane = lax.broadcasted_iota(jnp.int32, (1, LANES), 1)
    tail = jnp.where(lane == 0, high, jnp.where(lane == 1, low, jnp.where(lane == 2, rest, 0.0)))
    ref[:, D:] = tail.astype(bf16)


def merge_kernel(*refs, count, last):
    means, sums = [], []
    for ref in refs[:count]:
        means.append(ref[:, :D].astype(f32))
        tail = ref[:, D:].astype(f32)
        sums.append(tail[:, 0:1] + tail[:, 1:2] + tail[:, 2:3])
    top = sums[0]
    for value in sums[1:]:
        top = jnp.maximum(top, value)
    powers = [jnp.exp(value - top) for value in sums]
    total = sum(powers[1:], powers[0])
    mean = sum((m * p for m, p in zip(means[1:], powers[1:])), means[0] * powers[0]) / total
    lse = top + jnp.log(total)
    if last:
        refs[count][...], refs[count + 1][...] = mean, lse
    else:
        write_with_lse(refs[count], mean, lse)


def merge(parts, last=False):
    rows = parts[0].shape[0]
    shapes = [jax.ShapeDtypeStruct((rows, D + LANES), bf16)]
    if last:
        shapes = [jax.ShapeDtypeStruct((rows, D), f32), jax.ShapeDtypeStruct((rows, 1), f32)]
    return pl.pallas_call(
        lambda *refs: merge_kernel(*refs, count=len(parts), last=last),
        in_specs=[pl.BlockSpec(memory_space=pltpu.VMEM)] * len(parts),
        out_specs=[pl.BlockSpec(memory_space=pltpu.VMEM)] * len(shapes),
        out_shape=shapes,
        compiler_params=pltpu.CompilerParams(vmem_limit_bytes=VMEM),
        name="merge",
    )(*parts)


def head_scan_kernel(rows_ref, *refs, carried, last):
    refs, outs = refs[:-2], refs[-2:]
    rows = rows_ref[...]
    top = total = mixed = None
    if carried:
        mixed, top = refs[0][...].astype(f32), refs[1][...]
        total = jnp.ones_like(top)
        refs = refs[2:]
    for at in range(0, len(refs), 2):
        chunk = refs[at][...]
        if at + 1 < len(refs):
            chunk = jnp.concatenate([chunk, refs[at + 1][...]], 0)
        logits = nt(rows, chunk)
        here = jnp.max(logits, 1, keepdims=True)
        if top is None:
            top = here
            power = jnp.exp(logits - top)
            total = jnp.sum(power, 1, keepdims=True)
            mixed = nn(power.astype(bf16), chunk)
        else:
            joint = jnp.maximum(top, here)
            shrink = jnp.exp(top - joint)
            power = jnp.exp(logits - joint)
            total = total * shrink + jnp.sum(power, 1, keepdims=True)
            mixed = mixed * shrink + nn(power.astype(bf16), chunk)
            top = joint
    lse = top + jnp.log(total)
    if not last:
        outs[0][...], outs[1][...] = mixed / total, lse
    else:
        for part in range(2):

            @pl.when(pl.program_id(0) == part)
            def _():
                write_with_lse(outs[part], mixed / total, lse)


def head_scan(rows, chunks, carry=(), last=True):
    count, block = rows.shape[0], rows.shape[0] // 2
    vocab = sum(chunk.shape[0] for chunk in chunks)
    wide = pl.BlockSpec((block, D), lambda i: (i, 0))
    thin = pl.BlockSpec((block, 1), lambda i: (i, 0))
    if last:
        out_specs = [pl.BlockSpec((block, D + LANES), lambda i: (0, 0))] * 2
        out_shape = [jax.ShapeDtypeStruct((block, D + LANES), bf16)] * 2
    else:
        out_specs = [wide, thin]
        out_shape = [jax.ShapeDtypeStruct((count, D), f32), jax.ShapeDtypeStruct((count, 1), f32)]
    return pl.pallas_call(
        lambda *refs: head_scan_kernel(*refs, carried=bool(carry), last=last),
        grid=(count // block,),
        in_specs=[wide]
        + [wide, thin][: len(carry)]
        + [
            pl.BlockSpec(chunk.shape, lambda i: (0, 0), pipeline_mode=pl.Buffered(1))
            for chunk in chunks
        ],
        out_specs=out_specs,
        out_shape=out_shape,
        compiler_params=pltpu.CompilerParams(vmem_limit_bytes=VMEM),
        cost_estimate=pl.CostEstimate(
            flops=4 * count * vocab * D, bytes_accessed=2 * vocab * D + 4 * count * D,
            transcendentals=count * vocab,
        ),
        name="head_scan",
    )(rows, *carry, *chunks)


def head_grad_kernel(table_ref, rows_ref, lse_ref, weight_ref, *refs):
    out_ref = refs[-1]
    rows = rows_ref[...]
    logits = nt(table_ref[...], rows)
    grad = (jnp.exp(logits - lse_ref[0]) * weight_ref[0]).astype(bf16)
    part = nn(grad, rows)

    @pl.when(pl.program_id(0) == 0)
    def _():
        out_ref[...] = part if len(refs) == 1 else refs[0][...] + part

    @pl.when(pl.program_id(0) > 0)
    def _():
        out_ref[...] += part


def head_grad(table_low, rows, lse, weight, half, carry=()):
    vocab, count, block = table_low.shape[0], rows.shape[0], HEAD_BLOCK
    steps = count // block
    part = steps // 2
    stat = pl.BlockSpec((1, 1, block), lambda i: (i + half * part, 0, 0))
    whole = pl.BlockSpec((vocab, D), lambda i: (0, 0))
    return pl.pallas_call(
        head_grad_kernel,
        grid=(part,),
        in_specs=[whole, pl.BlockSpec((block, D), lambda i: (i + half * part, 0)), stat, stat]
        + [whole] * len(carry),
        out_specs=whole,
        out_shape=jax.ShapeDtypeStruct((vocab, D), f32),
        compiler_params=pltpu.CompilerParams(vmem_limit_bytes=VMEM),
        cost_estimate=pl.CostEstimate(
            flops=2 * count * vocab * D, bytes_accessed=count * D + 6 * vocab * D,
            transcendentals=count * vocab // 2,
        ),
        name="head_grad",
    )(table_low, rows, lse.reshape(steps, 1, block), weight, *carry)


def permute(value, axis, target):
    return lax.ppermute(value, axis, [(i, target(i)) for i in range(lax.axis_size(axis))])


def other_core(value):
    return permute(value, "mp", lambda i: i ^ 1)


def along_x(value, step):
    chips = lax.axis_size("mp") // 2
    return permute(value, "mp", lambda i: (i // 2 + step) % chips * 2 + i % 2)


def ring_order(count):
    return list(range(0, count, 2)) + list(range(count - 1, 0, -2))


def after(value, *others):
    return lax.optimization_barrier((value, *others))[0]


def ring_hop(upward, downward):
    count = lax.axis_size("dp")
    order = ring_order(count)
    spot = [order.index(i) for i in range(count)]
    return (
        permute(upward, "dp", lambda i: order[(spot[i] + 1) % count]),
        permute(downward, "dp", lambda i: order[(spot[i] - 1) % count]),
    )


def ring_middle(first, gates):
    upward, downward = first
    pieces = []
    for step in range(2, lax.axis_size("dp") // 2):
        upward, downward, _ = lax.optimization_barrier(
            (upward, downward, gates[min(step - 2, len(gates) - 1)])
        )
        upward, downward = ring_hop(upward, downward)
        pieces += [upward, downward]
    return pieces


def one_hot(index, count):
    return (index[:, None] == jnp.arange(count, dtype=jnp.int32)[None, :]).astype(bf16)


def placed(index, values, count):
    hit = index[None, :] == jnp.arange(count, dtype=jnp.int32)[:, None]
    return jnp.max(jnp.where(hit, values[None, :], -1), 1)


def rank_before(choice):
    count = choice.shape[0]
    earlier = (
        jnp.arange(count)[None, :] < jnp.arange(count)[:, None]
    ).astype(bf16)
    return jnp.dot(earlier, choice.astype(bf16), preferred_element_type=f32)


def grad_pack_kernel(core_ref, *refs, plan, rows_of, world):
    refs = dict(enumerate(refs))
    for left, right, held in plan:
        refs[held][...] = tn(refs[left][...], refs[right][...])
    mine_ref, theirs_ref = refs[rows_of[-1][0]], refs[rows_of[-1][0] + 1]
    second = core_ref[0] == 1
    total = mine_ref.shape[1]
    for j in range(world // 2):
        mine, theirs, filled = [], [], 0
        for held, rows, column in rows_of[:-1]:
            if column is None:
                mine.append(refs[held][...])
                theirs.append(mine[-1])
                filled += rows
                continue
            low = refs[held][2 * j * rows : (2 * j + 1) * rows, column : column + D]
            high = refs[held][(2 * j + 1) * rows : (2 * j + 2) * rows, column : column + D]
            mine.append(jnp.where(second, high, low))
            theirs.append(jnp.where(second, low, high))
            filled += rows
        if filled < total:
            mine.append(jnp.zeros((total - filled, D), f32))
            theirs.append(mine[-1])
        mine_ref[j] = jnp.concatenate(mine, 0).astype(bf16)
        theirs_ref[j] = jnp.concatenate(theirs, 0).astype(bf16)


def grad_pack(products, rows, world):
    core = jnp.reshape(lax.axis_index("mp") % 2, (1,)).astype(jnp.int32)
    operands = [value for product in products for value in product] + list(rows)
    inputs, count = len(operands), len(products)
    plan = [(2 * i, 2 * i + 1, inputs + 2 + i) for i in range(count)]
    pieces, scratch, flops = [], [], 0
    for i, (left, right) in enumerate(products):
        flops += 2 * left.shape[0] * left.shape[1] * right.shape[1]
        scratch.append(pltpu.VMEM((left.shape[1], right.shape[1]), f32))
        for column in range(0, right.shape[1], D):
            pieces.append((inputs + 2 + i, left.shape[1] // world, column))
    for i, value in enumerate(rows):
        pieces.append((2 * count + i, value.shape[0], None))
    total = -(-sum(piece[1] for piece in pieces) // 16) * 16
    pieces.append((inputs, 0, 0))
    shape = jax.ShapeDtypeStruct((world // 2, total, D), bf16)
    return pl.pallas_call(
        lambda *refs: grad_pack_kernel(*refs, plan=plan, rows_of=pieces, world=world),
        in_specs=[pl.BlockSpec(memory_space=pltpu.SMEM)]
        + [pl.BlockSpec(memory_space=pltpu.VMEM)] * inputs,
        out_specs=[pl.BlockSpec(memory_space=pltpu.VMEM)] * 2,
        out_shape=[shape, shape],
        scratch_shapes=scratch,
        compiler_params=pltpu.CompilerParams(vmem_limit_bytes=VMEM),
        cost_estimate=pl.CostEstimate(
            flops=flops, bytes_accessed=4 * world // 2 * total * D, transcendentals=0
        ),
        name="grad_pack",
    )(core, *operands)


class RingSum:

    def __init__(self, mine, theirs, x_first=False, gate=None):
        self.count = lax.axis_size("dp")
        self.chips = lax.axis_size("mp") // 2
        self.x_first = x_first
        shape = (self.count, self.chips, -1, D)
        got = other_core(theirs)
        got = (got if gate is None else after(got, gate)).reshape(shape)
        self.terms = [mine.reshape(shape), got]
        if x_first:
            chip = lax.axis_index("mp") // 2

            def for_chip(index):
                return sum(
                    lax.dynamic_index_in_dim(term, index, 1, keepdims=False).astype(f32)
                    for term in self.terms
                ).astype(bf16)

            self.terms = [for_chip(chip)] + [
                along_x(for_chip((chip + step) % self.chips), step)
                for step in range(1, self.chips)
            ]
        side, at = lax.axis_index("dp") % 2, lax.axis_index("dp") // 2
        self.here = jnp.where(side == 0, at, self.count - 1 - at)
        self.up_steps, self.down_steps = self.count // 2, (self.count - 1) // 2
        self.upward = self.downward = None
        self.step = 0

    def ready(self, *gates):
        if gates:
            self.terms[-1] = after(self.terms[-1], *gates)
        self.upward = self.part(self.up_steps).astype(bf16)
        self.downward = self.part(-self.down_steps).astype(bf16)

    def part(self, step):
        spot = lax.rem(self.here + step + self.count, self.count)
        at = jnp.where(2 * spot < self.count, 2 * spot, 2 * (self.count - 1 - spot) + 1)
        return sum(
            lax.dynamic_index_in_dim(term, at, 0, keepdims=False).astype(f32)
            for term in self.terms
        )

    def hop(self, gate=None):
        self.step += 1
        step, down = self.step, self.downward
        self.upward, down = ring_hop(self.upward, down)
        if gate is not None:
            self.upward, down, _ = lax.optimization_barrier((self.upward, down, gate))
        if step <= self.down_steps:
            self.downward = down
        if step < self.up_steps:
            self.upward = (self.upward.astype(f32) + self.part(self.up_steps - step)).astype(bf16)
        if step < self.down_steps:
            self.downward = (self.downward.astype(f32) + self.part(step - self.down_steps)).astype(
                bf16
            )

    def wait(self, gate):
        self.upward, self.downward, _ = lax.optimization_barrier((self.upward, self.downward, gate))

    def total(self):
        while self.step < self.up_steps:
            self.hop()
        line = self.part(0) + self.upward.astype(f32) + self.downward.astype(f32)
        if self.x_first:
            return [line]
        line = line.astype(bf16)
        chip = lax.axis_index("mp") // 2
        terms = [lax.dynamic_index_in_dim(line, chip, 0, keepdims=False)]
        for step in range(1, self.chips):
            going = lax.dynamic_index_in_dim(line, (chip + step) % self.chips, 0, keepdims=False)
            terms.append(along_x(going, step))
        return terms


def renew(weight, moment, average, gradient, factor):
    clipped = gradient * factor
    moment_new = MOMENTUM * moment + clipped
    weight_new = weight - STEP_RATE * (clipped + MOMENTUM * moment_new)
    average_new = AVERAGE_DECAY * average + (1.0 - AVERAGE_DECAY) * weight_new
    return (weight_new, moment_new, average_new)


def finish_sum_kernel(row_ref, *refs):
    terms, (total_ref, spread_ref) = refs[:-2], refs[-2:]
    total = sum((term[...].astype(f32) for term in terms[1:]), terms[0][...].astype(f32))
    total_ref[...] = total
    squares = jnp.sum(jnp.sum(total * total, 0, keepdims=True), 1, keepdims=True)
    lane = lax.broadcasted_iota(jnp.int32, (1, LANES), 1)
    row = row_ref[...] + jnp.where(lane == 0, squares, 0.0)
    spread_ref[...] = jnp.broadcast_to(row, spread_ref.shape)


def finish_sum(terms, row, world):
    vmem = pl.BlockSpec(memory_space=pltpu.VMEM)
    return pl.pallas_call(
        finish_sum_kernel,
        in_specs=[vmem] * (1 + len(terms)),
        out_specs=[vmem] * 2,
        out_shape=[
            jax.ShapeDtypeStruct(terms[0].shape, f32),
            jax.ShapeDtypeStruct((world, LANES), f32),
        ],
        compiler_params=pltpu.CompilerParams(vmem_limit_bytes=VMEM),
        name="finish_sum",
    )(row, *terms)


def clip_factor(totals):
    return jnp.minimum(1.0, CLIP_LIMIT / jnp.sqrt(totals[:, 0:1]))


def renew_kernel(spread_ref, early_ref, late_ref, *refs):
    states, outs = [refs[i : i + 3] for i in range(0, 12, 3)], refs[12:]
    totals = jnp.sum(spread_ref[...], 0, keepdims=True)
    outs[-1][...] = totals
    factor = clip_factor(totals)
    rows = states[1][0].shape[0]
    rows_patch, rows_down = states[0][0].shape[0], states[3][0].shape[0]
    attn = [(early_ref, j * rows, rows) for j in range(3)]
    attn.append((late_ref, 4 * rows + rows_down, rows))
    pieces = (
        [(early_ref, 3 * rows, rows_patch)],
        attn,
        [(late_ref, j * rows, rows) for j in range(4)],
        [(late_ref, 4 * rows, rows_down)],
    )
    for index, (state, parts) in enumerate(zip(states, pieces)):
        new = outs[4 * index : 4 * index + 4]
        for j, (ref, start, count) in enumerate(parts):
            at = slice(j * D, (j + 1) * D)
            gradient = ref[start : start + count, :]
            results = renew(
                state[0][:, at], state[1][:, at], state[2][:, at], gradient, factor
            )
            for out, value in zip(new, results):
                out[:, at] = value
            new[3][:, at] = results[0].astype(bf16)


def renew_matrices(spread, early, late, states):
    vmem = pl.BlockSpec(memory_space=pltpu.VMEM)
    shapes = []
    for state in states:
        shape = state[0].shape
        shapes += [jax.ShapeDtypeStruct(shape, f32)] * 3 + [jax.ShapeDtypeStruct(shape, bf16)]
    shapes.append(jax.ShapeDtypeStruct((1, LANES), f32))
    return pl.pallas_call(
        renew_kernel,
        in_specs=[vmem] * 15,
        out_specs=[vmem] * len(shapes),
        out_shape=shapes,
        compiler_params=pltpu.CompilerParams(vmem_limit_bytes=VMEM),
        name="renew_matrices",
    )(spread, early, late, *[value for state in states for value in state])


def shards(
    patches,
    patch_pos,
    owner,
    local_row,
    counts,
    task,
    table,
    table_mom,
    table_avg,
    patch_w,
    patch_mom,
    patch_avg,
    attn_w,
    attn_mom,
    attn_avg,
    up_w,
    up_mom,
    up_avg,
    down_w,
    down_mom,
    down_avg,
    gains,
    gain_mom,
    gain_avg,
):
    groups, owners = lax.axis_size("dp"), lax.axis_size("mp")
    world = groups * owners
    tokens_here = patches.shape[0]
    rows_own = table.shape[0]
    rows_attn, rows_patch, rows_down = attn_w.shape[0], patch_w.shape[0], down_w.shape[0]
    cols_gain = gains.shape[1]
    place = lax.axis_index("dp") * owners + lax.axis_index("mp")

    table_low = table.astype(bf16)
    gain_row = jnp.pad(gains.astype(bf16).reshape(1, 3 * cols_gain), ((0, 0), (0, 4 * D - 3 * cols_gain)))
    patch_rows = jnp.pad(patch_w.astype(bf16), ((0, -rows_patch % 4), (0, 0)))
    early = jnp.concatenate([attn_w.astype(bf16), patch_rows.reshape(-1, 4 * D), gain_row], 0)
    late = jnp.concatenate(
        [
            up_w.astype(bf16),
            jnp.concatenate(
                [down_w[j : j + rows_attn] for j in range(0, rows_down, rows_attn)], 1
            ).astype(bf16),
        ],
        0,
    )
    early_all, late_all = (
        lax.all_gather(jnp.pad(w, ((0, -w.shape[0] % 8), (0, 0))), AXES, axis=0, tiled=False)
        for w in (early, late)
    )

    first_pieces = ring_hop(table_low, table_low)

    my_counts = lax.dynamic_slice_in_dim(counts, place, 1, 0)
    first_tok, alive = my_counts[0, 0], my_counts[0, 1]
    positions = jnp.arange(tokens_here, dtype=jnp.int32)
    is_patch = (positions < first_tok)[:, None]
    is_token = (positions >= first_tok) & (positions < first_tok + alive)
    is_valid = (positions < first_tok + alive)[:, None]
    target_owner = owner[:, 0]

    share = -(-3 * tokens_here // (2 * world) // 16) * 16
    identity = target_owner * (rows_own * groups) + local_row
    same = (identity[:, None] == identity[None, :]) & is_token[None, :]
    first_same = jnp.min(jnp.where(same, positions[None, :], tokens_here), 1)
    leads = is_token & (first_same == positions)
    dest = identity // rows_own
    leads_to = (dest[:, None] == jnp.arange(world)[None, :]) & leads[:, None]
    lead_rank = jnp.sum(jnp.where(leads_to, rank_before(leads_to), 0.0), 1).astype(jnp.int32)
    far_rank = jnp.max(
        jnp.where(first_same[:, None] == positions[None, :], lead_rank[None, :], 0), 1
    )
    far_row = identity - dest * rows_own
    most = jnp.max(jnp.sum(leads_to.astype(jnp.int32), 0))

    def far_slots(start, share, limit):
        within = far_rank - start
        fits = is_token & (within >= 0) & (within < limit)
        return jnp.where(fits, dest * share + within, -1)

    def far_ids(slots, extra, share):
        ids = placed(slots, far_row, world * share).reshape(world, share)
        ids = jnp.concatenate([ids, jnp.full((world, 1), extra, jnp.int32)], 1)
        return lax.all_to_all(ids, ("mp", "dp"), split_axis=0, concat_axis=0, tiled=True)

    first_slots = far_slots(0, share, share - 1)
    first_ids = far_ids(first_slots, most, share)
    few = 16
    turns = (jnp.max(first_ids[:, share]) - (share - 1) + few - 1) // few

    def far_fetch(slots, ids, share):
        spread = one_hot(ids[:, :share].reshape(-1), rows_own)
        rows = jnp.dot(spread, table_low, preferred_element_type=f32).astype(bf16)
        rows = lax.optimization_barrier((rows, *first_pieces))[0]
        return lax.all_to_all(
            rows.reshape(world, share, D), ("mp", "dp"), split_axis=0, concat_axis=0, tiled=True
        ).reshape(world * share, D)

    def far_spread(slots, arrived, share):
        return jnp.dot(one_hot(slots, world * share), arrived, preferred_element_type=f32)

    def far_pack(slots, values, share, extra=None):
        rows = jnp.dot(one_hot(slots, world * share).T, values, preferred_element_type=f32)
        if extra is not None:
            spare = lax.broadcasted_iota(jnp.int32, (world * share, 1), 0) % share == share - 1
            rows = jnp.where(spare, extra, rows)
        return rows.astype(bf16)

    def far_send(packed, share):
        return lax.all_to_all(
            packed.reshape(world, share, D),
            ("mp", "dp"), split_axis=0, concat_axis=0, tiled=True,
        ).reshape(world * share, D)

    def far_add(arrived, ids, share):
        spread = one_hot(ids[:, :share].reshape(-1), rows_own)
        return tn(spread, arrived)


    def columns(gathered, low, high):
        return gathered[:, :rows_attn, low * D : high * D].reshape(-1, (high - low) * D)

    w_q, w_kv, w_out = columns(early_all, 0, 1), columns(early_all, 1, 3), columns(early_all, 3, 4)
    gain_at = rows_attn + patch_rows.shape[0] // 4
    w_patch = (
        early_all[:, rows_attn:gain_at].reshape(world, -1, D)[:, :rows_patch].reshape(-1, D)
    )
    gain_all = (
        early_all[:, gain_at, : 3 * cols_gain]
        .reshape(world, 3, cols_gain).transpose(1, 0, 2).reshape(3, D).astype(f32)
    )
    scored_all = counts[:, 2].astype(f32)
    per_task = (task[:, None] == jnp.arange(TASKS)[None, :]).astype(f32)
    task_total = jnp.sum(per_task * scored_all[:, None], 0)
    present = jnp.sum((task_total > 0).astype(f32))
    inverse_seq = jnp.sum(per_task / jnp.maximum(task_total, 1.0)[None, :], 1)
    row_live = (jnp.arange(LOSS)[None, :] < counts[:, 2:3]).astype(f32) * inverse_seq[:, None]
    head_weight = (row_live / present).reshape(-1, 1, HEAD_BLOCK)

    arrived = far_fetch(first_slots, first_ids, share)
    arrived, head_weight = lax.optimization_barrier((arrived, head_weight, w_kv, w_q, w_patch))[:2]
    looked = far_spread(first_slots, arrived, share)

    def fetch_turn(turn, total):
        slots = far_slots(share - 1 + turn * few, few, few)
        return total + far_spread(slots, far_fetch(slots, far_ids(slots, 0, few), few), few)

    looked = lax.fori_loop(0, turns, fetch_turn, looked)

    w_up = columns(late_all, 0, 4)
    w_down = jnp.concatenate(
        [late_all[:, rows_attn : 2 * rows_attn, j : j + D] for j in range(0, 4 * D, D)], 1
    ).reshape(world * rows_down, D)

    def patch_rows_of(pixels):
        position_code = (patch_pos[:, None] == jnp.arange(POSN)[None, :]).astype(bf16)
        return jnp.concatenate([pixels, position_code], 1)

    patch_in = patch_rows_of(patches)
    from_patch = jnp.dot(patch_in, w_patch, preferred_element_type=f32)
    embed_scale = math.sqrt(D)
    embedded = jnp.where(is_patch, from_patch, 0.0) + embed_scale * looked
    normed_first = layer_norm(embedded, gain_all[0]).astype(bf16)
    key_values = jnp.dot(normed_first, w_kv, preferred_element_type=f32).astype(bf16)

    pick = first_tok - 1
    pick_at = jnp.reshape(pick, (1,))

    def picked_rows(values, start=pick):
        return lax.dynamic_slice_in_dim(values, start, LOSS, 0)

    normed_pick = picked_rows(normed_first)
    query_pick = jnp.dot(normed_pick, w_q, preferred_element_type=f32).astype(bf16)
    attended_pick, lse_pick = attention_pick(pick_at, query_pick, key_values)
    branch_pick = jnp.dot(attended_pick, w_out, preferred_element_type=f32)
    middle_pick = picked_rows(embedded) + branch_pick
    normed_mid, mid_back = jax.vjp(layer_norm, middle_pick, gain_all[1])
    normed_mid = normed_mid.astype(bf16)
    query_all = jnp.dot(normed_first, w_q, preferred_element_type=f32).astype(bf16)
    attended = attention_all(after(query_all, attended_pick), key_values)
    normed_mid = after(normed_mid, attended)
    hidden_pick = jnp.dot(normed_mid, w_up, preferred_element_type=f32)
    active_f32, gelu_back = jax.vjp(gelu_tanh, hidden_pick)
    active_pick = active_f32.astype(bf16)
    result_pick = middle_pick + jnp.dot(active_pick, w_down, preferred_element_type=f32)
    final_rows, final_back = jax.vjp(layer_norm, result_pick, gain_all[2])
    own_rows = final_rows.astype(bf16)
    chunks = [table_low, *first_pieces, *ring_middle(first_pieces, (arrived, attended))]
    half = rows_own // 32 * 16
    last_up, last_down = after(chunks[-2], own_rows)[:half], after(chunks[-1], own_rows)[half:]
    chunks += ring_hop(last_up, last_down)
    target_rows = picked_rows(looked, first_tok)

    chips = owners // 2
    line = jnp.stack([own_rows] + [along_x(own_rows, step) for step in range(1, chips)])
    group_rows = jnp.stack([line, other_core(line)])
    group_rows = group_rows.reshape(-1, D)
    carry = head_scan(after(group_rows, last_up, last_down), chunks[:5], last=False)
    mine, theirs = head_scan(group_rows, chunks[5:], carry)
    (line,) = merge([mine, other_core(theirs)])
    mean_own, own_total = merge(
        [line[:LOSS]]
        + [along_x(line[step * LOSS : (step + 1) * LOSS], -step) for step in range(1, chips)],
        last=True,
    )
    own_total = own_total[:, 0]

    picked = jnp.sum(own_rows.astype(f32) * target_rows, 1)
    own_weight = lax.dynamic_slice_in_dim(row_live, place, 1, 0)[0]
    loss_part = jnp.sum(own_weight * (own_total - picked))

    rows_all = lax.all_gather(after(own_rows, mean_own), AXES, axis=0, tiled=True)
    high = lax.reduce_precision(own_total, 8, 7)
    low = lax.reduce_precision(own_total - high, 8, 7)
    total_row = jnp.concatenate([high, low, own_total - high - low])[None, :]

    scaled_weight = (own_weight / present)[:, None]
    grad_rows = scaled_weight * (mean_own - target_rows)
    grad_result, grad_gain_last = final_back(grad_rows)
    grad_second = grad_result.astype(bf16)
    grad_hidden = gelu_back(nt(grad_second, w_down))[0].astype(bf16)
    grad_middle, grad_gain_mid = mid_back(nt(grad_hidden, w_up))
    grad_middle = grad_result + grad_middle
    grad_branch = grad_middle.astype(bf16)
    grad_attended = nt(grad_branch, w_out).astype(bf16)
    grad_q, grad_k, grad_v = attention_back(
        pick_at, query_pick, key_values, attended_pick, grad_attended, lse_pick
    )
    grad_patch_rows, grad_looked, grad_gain_first = first_back(
        jnp.reshape(first_tok, (1,)), grad_k, grad_v, w_kv, grad_q, w_q, embedded,
        gain_all[0:1], grad_middle, -scaled_weight * own_rows.astype(f32),
    )
    packed = far_pack(first_slots, grad_looked, share, total_row)
    grad_arrived = far_send(packed, share)
    grad_gain = jnp.stack([grad_gain_first[0], grad_gain_mid, grad_gain_last])
    early_mine, early_theirs = grad_pack(
        [
            (normed_pick, grad_q),
            (normed_first, grad_k),
            (normed_first, grad_v),
            (patch_rows_of(after(patches, packed)), after(grad_patch_rows, packed)),
        ],
        [grad_gain], world,
    )
    late_mine, late_theirs = grad_pack(
        [
            (normed_mid, after(grad_hidden, early_theirs)),
            (active_pick, grad_second),
            (attended_pick, grad_branch),
        ],
        [], world,
    )
    early_sum = RingSum(early_mine, early_theirs, True)
    late_sum = RingSum(late_mine, late_theirs)
    late_sum.ready()

    branch = jnp.dot(after(attended, late_sum.upward), w_out, preferred_element_type=f32)
    middle = embedded + branch
    normed_second = layer_norm(middle, gain_all[1]).astype(bf16)
    hidden = jnp.dot(normed_second, w_up, preferred_element_type=f32)
    second = jnp.dot(gelu_tanh(hidden).astype(bf16), w_down, preferred_element_type=f32)
    result = middle + second

    grad_arrived = after(grad_arrived, normed_second)
    spare_rows = grad_arrived.reshape(owners, groups, share, D)[:, :, share - 1].astype(f32)
    total_all = spare_rows[..., :LOSS] + spare_rows[..., LOSS : 2 * LOSS] + spare_rows[..., 2 * LOSS :]
    total_all = total_all.transpose(1, 0, 2)
    late_sum.hop(grad_arrived)
    early_sum.ready(late_sum.upward)
    head_first = head_grad(
        table_low, after(rows_all, late_sum.upward, early_sum.upward), total_all, head_weight, 0
    )
    late_sum.hop(head_first)
    early_sum.hop(late_sum.upward)
    table_head = head_grad(
        table_low, after(rows_all, late_sum.upward, early_sum.upward), total_all, head_weight, 1,
        (head_first,),
    )
    late_sum.hop(table_head)
    early_sum.hop(late_sum.upward)
    grad_table = table_head + far_add(
        after(grad_arrived, late_sum.upward, early_sum.upward), first_ids, share
    )
    late_terms = late_sum.total()
    (summed_early,) = early_sum.total()

    def next_turn(turn, total):
        slots = far_slots(share - 1 + turn * few, few, few)
        return total + far_add(
            far_send(far_pack(slots, grad_looked, few), few), far_ids(slots, 0, few), few
        )

    grad_table = lax.fori_loop(0, turns, next_turn, grad_table)

    def square_sum(values):
        return jnp.sum(jnp.where(is_valid, jnp.mean(values * values, 1, keepdims=True), 0.0))

    edge = 3 * rows_attn + rows_patch
    summed_gain = lax.dynamic_slice_in_dim(
        summed_early[edge : edge + 3], place * cols_gain, cols_gain, 1
    )
    squares = (
        jnp.sum(grad_table * grad_table)
        + jnp.sum(summed_early[:edge] * summed_early[:edge])
        + jnp.sum(summed_gain * summed_gain)
    )
    row = jnp.zeros((1, LANES), f32)
    lane = lax.broadcasted_iota(jnp.int32, (1, LANES), 1)
    scalars = (
        squares, loss_part, square_sum(embedded), square_sum(branch), square_sum(second),
        square_sum(result),
    )
    for at, value in enumerate(scalars):
        row = jnp.where(lane == at, value, row)
    summed_late, spread = finish_sum(late_terms, row, world)
    spread = lax.all_to_all(spread, AXES, 0, 0, tiled=True)
    *matrices, totals = renew_matrices(
        spread, summed_early, summed_late,
        (
            (patch_w, patch_mom, patch_avg),
            (attn_w, attn_mom, attn_avg),
            (up_w, up_mom, up_avg),
            (down_w, down_mom, down_avg),
        ),
    )
    factor = clip_factor(jnp.sum(spread, 0, keepdims=True))[0, 0]
    table_new = renew(table, table_mom, table_avg, grad_table, factor)
    gains_new = renew(gains, gain_mom, gain_avg, summed_gain, factor)
    clip_norm = jnp.sqrt(totals[0, 0])
    loss_total = totals[0, 1]
    valid_total = jnp.sum(counts[:, :2].astype(f32))
    rms_stats = jnp.sqrt(totals[0, 2:6] / valid_total)
    return (
        *table_new, table_new[0].astype(bf16), *matrices, *gains_new,
        loss_total, present, clip_norm, rms_stats,
    )


def solution(mesh):
    whole, split = P(), P(AXES)
    rows, vocab, columns = P(AXES, None), P(("mp", "dp"), None), P(None, AXES)
    in_specs = (rows, split, rows, split, whole, whole) + (vocab,) * 3 + (rows,) * 12 + (columns,) * 3
    out_specs = (vocab,) * 4 + (rows,) * 16 + (columns,) * 3 + (whole,) * 4
    return jax.shard_map(shards, mesh=mesh, in_specs=in_specs, out_specs=out_specs, check_vma=False)
```

```python
import math

import jax
import jax.numpy as jnp
from jax import lax
from jax.experimental import pallas as pl
from jax.experimental.pallas import tpu as pltpu
from jax.sharding import PartitionSpec as P

D = 768
HEADS = 24
HDIM = 32
POSN = 128
SEQ_LEN = 1024
LOSS = 256
TASKS = 32

NORM_EPS = 1e-05
STEP_RATE = 5000.0
MOMENTUM = 0.5
AVERAGE_DECAY = 0.5
CLIP_LIMIT = 0.02

AXES = ("dp", "mp")
LANES = 128
GROUP = LANES // HDIM
TILES = D // LANES
SCALE = HDIM ** (-0.5)
SCALE_LOG2 = SCALE * math.log2(math.e)
VMEM = 56 * 2**20
HEAD_BLOCK = 2048
SMALL_COST = pl.CostEstimate(flops=1, bytes_accessed=1, transcendentals=0)
bf16 = jnp.bfloat16
f32 = jnp.float32


def contract(left, right, left_dim, right_dim):
    return lax.dot_general(
        left, right, (((left_dim,), (right_dim,)), ((), ())), preferred_element_type=f32
    )


def nn(left, right):
    return contract(left, right, 1, 0)


def nt(left, right):
    return contract(left, right, 1, 1)


def tn(left, right):
    return contract(left, right, 0, 0)


def layer_norm(values, gain):
    row_mean = jnp.mean(values, -1, keepdims=True)
    centred = values - row_mean
    spread = jnp.mean(centred * centred, -1, keepdims=True)
    return centred * lax.rsqrt(spread + NORM_EPS) * gain


def gelu_tanh(values):
    return jax.nn.gelu(values, approximate=True)


def head_masks():
    lane = lax.broadcasted_iota(jnp.int32, (1, LANES), 1) // HDIM
    return [lane == head for head in range(GROUP)]


def only(mask, block):
    return jnp.where(mask, block, jnp.zeros((), block.dtype))


def attention_all_kernel(q_ref, k_ref, v_ref, o_ref, *, block):
    length = q_ref.shape[0]
    masks = head_masks()
    row = lax.broadcasted_iota(jnp.int32, (block, block), 0)
    col = lax.broadcasted_iota(jnp.int32, (block, block), 1)
    triangle = col <= row
    for index in range(length // block):
        start, end = index * block, (index + 1) * block
        q = q_ref[start:end, :]
        k, v = k_ref[0:end, :], v_ref[0:end, :]
        joined = jnp.zeros((block, LANES), f32)
        for mask in masks:
            scores = nt(only(mask, q), k)
            diagonal = jnp.where(triangle, scores[:, start:], -1e30)
            scores = jnp.concatenate([scores[:, :start], diagonal], 1) if index else diagonal
            top = jnp.max(scores, 1, keepdims=True) * SCALE_LOG2
            power = jnp.exp2(scores * SCALE_LOG2 - top)
            total = jnp.sum(power, 1, keepdims=True)
            joined = jnp.where(mask, nn(power.astype(bf16), v) / total, joined)
        o_ref[start:end, :] = joined.astype(bf16)


def attention_all(queries, key_values):
    length = queries.shape[0]
    return pl.pallas_call(
        lambda *refs: attention_all_kernel(*refs, block=512),
        grid=(TILES,),
        in_specs=[
            pl.BlockSpec((length, LANES), lambda g: (0, g)),
            pl.BlockSpec((length, LANES), lambda g: (0, g)),
            pl.BlockSpec((length, LANES), lambda g: (0, TILES + g)),
        ],
        out_specs=pl.BlockSpec((length, LANES), lambda g: (0, g)),
        out_shape=jax.ShapeDtypeStruct((length, D), bf16),
        compiler_params=pltpu.CompilerParams(vmem_limit_bytes=VMEM),
        cost_estimate=pl.CostEstimate(
            flops=2 * 2 * HEADS * length * length * LANES, bytes_accessed=8 * length * D,
            transcendentals=HEADS * length * length,
        ),
        name="attention_all",
    )(queries, key_values, key_values)


def attention_pick_kernel(first_ref, q_ref, k_ref, v_ref, o_ref, lse_ref):
    rows, length = q_ref.shape[0], k_ref.shape[0]
    masks = head_masks()
    row = lax.broadcasted_iota(jnp.int32, (rows, length), 0)
    col = lax.broadcasted_iota(jnp.int32, (rows, length), 1)
    allowed = col <= row + first_ref[0]
    lane = lax.broadcasted_iota(jnp.int32, (1, LANES), 1)
    q, k, v = q_ref[...], k_ref[...], v_ref[...]
    joined = jnp.zeros((rows, LANES), f32)
    stat = jnp.zeros((rows, LANES), f32)
    for head, mask in enumerate(masks):
        scores = jnp.where(allowed, nt(only(mask, q), k), -1e30)
        top = jnp.max(scores, 1, keepdims=True) * SCALE_LOG2
        power = jnp.exp2(scores * SCALE_LOG2 - top)
        total = jnp.sum(power, 1, keepdims=True)
        joined = jnp.where(mask, nn(power.astype(bf16), v) / total, joined)
        stat = jnp.where(lane == head, top + jnp.log2(total), stat)
    o_ref[...] = joined.astype(bf16)
    lse_ref[0] = stat.T[0:8, :]


def attention_pick(first, queries, key_values):
    rows, length = queries.shape[0], key_values.shape[0]
    return pl.pallas_call(
        attention_pick_kernel,
        grid_spec=pltpu.PrefetchScalarGridSpec(
            num_scalar_prefetch=1,
            grid=(TILES,),
            in_specs=[
                pl.BlockSpec((rows, LANES), lambda g, s: (0, g)),
                pl.BlockSpec((length, LANES), lambda g, s: (0, g)),
                pl.BlockSpec((length, LANES), lambda g, s: (0, TILES + g)),
            ],
            out_specs=[
                pl.BlockSpec((rows, LANES), lambda g, s: (0, g)),
                pl.BlockSpec((1, 8, rows), lambda g, s: (g, 0, 0)),
            ],
        ),
        out_shape=[
            jax.ShapeDtypeStruct((rows, D), bf16),
            jax.ShapeDtypeStruct((TILES, 8, rows), f32),
        ],
        compiler_params=pltpu.CompilerParams(vmem_limit_bytes=VMEM),
        cost_estimate=pl.CostEstimate(
            flops=2 * 2 * HEADS * rows * length * LANES, bytes_accessed=6 * length * D,
            transcendentals=HEADS * rows * length,
        ),
        name="attention_pick",
    )(first, queries, key_values, key_values)


def attention_back_kernel(
    first_ref, q_ref, k_ref, v_ref, o_ref, do_ref, lse_ref, dq_ref, dk_ref, dv_ref
):
    rows, length = q_ref.shape[0], k_ref.shape[0]
    masks = head_masks()
    key = lax.broadcasted_iota(jnp.int32, (length, rows), 0)
    query = lax.broadcasted_iota(jnp.int32, (length, rows), 1)
    allowed = key <= query + first_ref[0]
    q, k, v, do = q_ref[...], k_ref[...], v_ref[...], do_ref[...]
    share = (
        lax.broadcasted_iota(jnp.int32, (8, LANES), 0)
        == lax.broadcasted_iota(jnp.int32, (8, LANES), 1) // HDIM
    ).astype(f32)
    inner = lax.dot_general(
        share, do.astype(f32) * o_ref[...].astype(f32), (((1,), (1,)), ((), ())),
        preferred_element_type=f32, precision=lax.Precision.HIGHEST,
    )
    lse = lse_ref[0]
    dq = jnp.zeros((rows, LANES), f32)
    dk = jnp.zeros((length, LANES), f32)
    dv = jnp.zeros((length, LANES), f32)
    for head, mask in enumerate(masks):
        k_head = only(mask, k)
        scores = nt(k_head, q)
        chance = jnp.where(
            allowed, jnp.exp2(scores * SCALE_LOG2 - lse[head : head + 1, :]), 0.0
        )
        d_chance = nt(only(mask, v), do)
        d_scores = (chance * (d_chance - inner[head : head + 1, :])).astype(bf16)
        dv = jnp.where(mask, nn(chance.astype(bf16), do), dv)
        dk = jnp.where(mask, nn(d_scores, q), dk)
        dq = dq + tn(d_scores, k_head)
    dq_ref[...] = (dq * SCALE).astype(bf16)
    dk_ref[...] = (dk * SCALE).astype(bf16)
    dv_ref[...] = dv.astype(bf16)


def attention_back(first, queries, key_values, attended, grad_attended, lse):
    rows, length = queries.shape[0], key_values.shape[0]
    rows_spec = pl.BlockSpec((rows, LANES), lambda g, s: (0, g))
    all_spec = pl.BlockSpec((length, LANES), lambda g, s: (0, g))
    return pl.pallas_call(
        attention_back_kernel,
        grid_spec=pltpu.PrefetchScalarGridSpec(
            num_scalar_prefetch=1,
            grid=(TILES,),
            in_specs=[
                rows_spec,
                all_spec,
                pl.BlockSpec((length, LANES), lambda g, s: (0, TILES + g)),
                rows_spec,
                rows_spec,
                pl.BlockSpec((1, 8, rows), lambda g, s: (g, 0, 0)),
            ],
            out_specs=[rows_spec, all_spec, all_spec],
        ),
        out_shape=[
            jax.ShapeDtypeStruct((rows, D), bf16),
            jax.ShapeDtypeStruct((length, D), bf16),
            jax.ShapeDtypeStruct((length, D), bf16),
        ],
        compiler_params=pltpu.CompilerParams(vmem_limit_bytes=VMEM),
        cost_estimate=pl.CostEstimate(
            flops=5 * 2 * HEADS * rows * length * LANES, bytes_accessed=10 * length * D,
            transcendentals=HEADS * rows * length,
        ),
        name="attention_back",
    )(first, queries, key_values, key_values, attended, grad_attended, lse)


def layer_stats_kernel(
    valid_ref, attended_ref, x_ref, wout_ref, wup_ref, wdown_ref, gain_ref, row_ref, out_ref
):
    block = x_ref.shape[0]
    step = pl.program_id(0)
    embedded = x_ref[...]
    branch = nn(attended_ref[...], wout_ref[...])
    middle = embedded + branch
    normed = layer_norm(middle, gain_ref[...]).astype(bf16)
    active = gelu_tanh(nn(normed, wup_ref[...])).astype(bf16)
    second = nn(active, wdown_ref[...])
    valid = step * block + lax.broadcasted_iota(jnp.int32, (block, 1), 0) < valid_ref[0]
    lane = lax.broadcasted_iota(jnp.int32, (1, LANES), 1)
    sums = jnp.zeros((1, LANES), f32)
    for at, values in enumerate((embedded, branch, second, middle + second)):
        mean = jnp.where(valid, jnp.mean(values * values, 1, keepdims=True), 0.0)
        sums = jnp.where(lane == at + 2, jnp.sum(mean, 0, keepdims=True), sums)

    @pl.when(step == 0)
    def _():
        out_ref[...] = row_ref[...] + sums

    @pl.when(step > 0)
    def _():
        out_ref[...] += sums


def layer_stats(valid, attended, embedded, w_out, w_up, w_down, gain, row):
    length, block = embedded.shape[0], 256
    blocked = pl.BlockSpec((block, D), lambda i, s: (i, 0))

    def whole(value):
        return pl.BlockSpec(value.shape, lambda i, s: (0, 0), pipeline_mode=pl.Buffered(1))

    return pl.pallas_call(
        layer_stats_kernel,
        grid_spec=pltpu.PrefetchScalarGridSpec(
            num_scalar_prefetch=1,
            grid=(length // block,),
            in_specs=[blocked, blocked] + [whole(v) for v in (w_out, w_up, w_down, gain, row)],
            out_specs=pl.BlockSpec((1, LANES), lambda i, s: (0, 0)),
        ),
        out_shape=jax.ShapeDtypeStruct((1, LANES), f32),
        compiler_params=pltpu.CompilerParams(vmem_limit_bytes=VMEM),
        cost_estimate=SMALL_COST,
        name="layer_stats",
    )(valid, attended, embedded, w_out, w_up, w_down, gain, row)


def first_back_kernel(
    bounds_ref, k_ref, v_ref, wkv_ref, q_ref, wq_ref, x_ref, gain_ref, middle_ref, target_ref,
    patch_ref, looked_ref, dgain_ref, normed, residual, pulled,
):
    length, block = x_ref.shape[0], 128
    first = bounds_ref[0]
    normed[0:length, :] = nt(k_ref[...], wkv_ref[:, :D]) + nt(v_ref[...], wkv_ref[:, D:])
    residual[...] = jnp.zeros_like(residual)
    pulled[...] = jnp.zeros_like(pulled)

    def place(ref, rows, start):
        base = pl.multiple_of(start // 8 * 8, 8)
        padded = jnp.concatenate([rows, jnp.zeros((8, D), f32)], 0)
        turned = pltpu.roll(padded, start - base, 0)
        at = pl.ds(base, rows.shape[0] + 8)
        ref[at, :] = ref[at, :] + turned

    place(normed, nt(q_ref[...], wq_ref[...]), first - 1)
    place(residual, middle_ref[...], first - 1)
    place(pulled, target_ref[...], first)
    gain = gain_ref[...]
    dgain = jnp.zeros((1, D), f32)
    for start in range(0, length, block):
        at = slice(start, start + block)
        x, grad = x_ref[at, :], normed[at, :]
        centred = x - jnp.mean(x, 1, keepdims=True)
        spread = lax.rsqrt(jnp.mean(centred * centred, 1, keepdims=True) + NORM_EPS)
        unit = centred * spread
        dgain = dgain + jnp.sum(grad * unit, 0, keepdims=True)
        scaled = grad * gain
        inner = jnp.mean(scaled * unit, 1, keepdims=True)
        back = spread * (scaled - jnp.mean(scaled, 1, keepdims=True) - unit * inner)
        back = back + residual[at, :]
        row = start + lax.broadcasted_iota(jnp.int32, (block, 1), 0)
        patch_ref[at, :] = jnp.where(row < first, back, 0.0).astype(bf16)
        looked_ref[at, :] = (math.sqrt(D) * back + pulled[at, :]).astype(bf16)
    dgain_ref[...] = dgain


def first_back(first, grad_k, grad_v, w_kv, grad_q, w_q, embedded, gain, middle, target):
    length = embedded.shape[0]
    wide = jax.ShapeDtypeStruct((length, D), bf16)
    return pl.pallas_call(
        first_back_kernel,
        in_specs=[pl.BlockSpec(memory_space=pltpu.SMEM)]
        + [pl.BlockSpec(memory_space=pltpu.VMEM)] * 9,
        out_specs=[pl.BlockSpec(memory_space=pltpu.VMEM)] * 3,
        out_shape=[wide, wide, jax.ShapeDtypeStruct((1, D), f32)],
        scratch_shapes=[pltpu.VMEM((length + 16, D), f32)] * 3,
        compiler_params=pltpu.CompilerParams(vmem_limit_bytes=VMEM),
        cost_estimate=pl.CostEstimate(
            flops=2 * length * 2 * D * D, bytes_accessed=16 * length * D, transcendentals=0
        ),
        name="first_back",
    )(first, grad_k, grad_v, w_kv, grad_q, w_q, embedded, gain, middle, target)


def write_with_lse(ref, mean, lse):
    ref[:, :D] = mean.astype(bf16)
    high = lse.astype(bf16).astype(f32)
    low = (lse - high).astype(bf16).astype(f32)
    rest = lse - high - low
    lane = lax.broadcasted_iota(jnp.int32, (1, LANES), 1)
    tail = jnp.where(lane == 0, high, jnp.where(lane == 1, low, jnp.where(lane == 2, rest, 0.0)))
    ref[:, D:] = tail.astype(bf16)


def merge_kernel(*refs, count, last):
    means, sums = [], []
    for ref in refs[:count]:
        means.append(ref[:, :D].astype(f32))
        tail = ref[:, D:].astype(f32)
        sums.append(tail[:, 0:1] + tail[:, 1:2] + tail[:, 2:3])
    top = sums[0]
    for value in sums[1:]:
        top = jnp.maximum(top, value)
    powers = [jnp.exp(value - top) for value in sums]
    total = sum(powers[1:], powers[0])
    mean = sum((m * p for m, p in zip(means[1:], powers[1:])), means[0] * powers[0]) / total
    lse = top + jnp.log(total)
    if last:
        refs[count][...], refs[count + 1][...] = mean, lse
    else:
        write_with_lse(refs[count], mean, lse)


def merge(parts, last=False):
    rows = parts[0].shape[0]
    shapes = [jax.ShapeDtypeStruct((rows, D + LANES), bf16)]
    if last:
        shapes = [jax.ShapeDtypeStruct((rows, D), f32), jax.ShapeDtypeStruct((rows, 1), f32)]
    return pl.pallas_call(
        lambda *refs: merge_kernel(*refs, count=len(parts), last=last),
        in_specs=[pl.BlockSpec(memory_space=pltpu.VMEM)] * len(parts),
        out_specs=[pl.BlockSpec(memory_space=pltpu.VMEM)] * len(shapes),
        out_shape=shapes,
        compiler_params=pltpu.CompilerParams(vmem_limit_bytes=VMEM),
        name="merge",
    )(*parts)


def head_scan_kernel(rows_ref, *refs, carried, last):
    refs, outs = refs[:-2], refs[-2:]
    rows = rows_ref[...]
    top = total = mixed = None
    if carried:
        mixed, top = refs[0][...].astype(f32), refs[1][...]
        total = jnp.ones_like(top)
        refs = refs[2:]
    for at in range(0, len(refs), 2):
        chunk = refs[at][...]
        if at + 1 < len(refs):
            chunk = jnp.concatenate([chunk, refs[at + 1][...]], 0)
        logits = nt(rows, chunk)
        here = jnp.max(logits, 1, keepdims=True)
        if top is None:
            top = here
            power = jnp.exp(logits - top)
            total = jnp.sum(power, 1, keepdims=True)
            mixed = nn(power.astype(bf16), chunk)
        else:
            joint = jnp.maximum(top, here)
            shrink = jnp.exp(top - joint)
            power = jnp.exp(logits - joint)
            total = total * shrink + jnp.sum(power, 1, keepdims=True)
            mixed = mixed * shrink + nn(power.astype(bf16), chunk)
            top = joint
    lse = top + jnp.log(total)
    if not last:
        outs[0][...], outs[1][...] = mixed / total, lse
    else:
        for part in range(2):

            @pl.when(pl.program_id(0) == part)
            def _():
                write_with_lse(outs[part], mixed / total, lse)


def head_scan(rows, chunks, carry=(), last=True):
    count, block = rows.shape[0], rows.shape[0] // 2
    vocab = sum(chunk.shape[0] for chunk in chunks)
    wide = pl.BlockSpec((block, D), lambda i: (i, 0))
    thin = pl.BlockSpec((block, 1), lambda i: (i, 0))
    if last:
        out_specs = [pl.BlockSpec((block, D + LANES), lambda i: (0, 0))] * 2
        out_shape = [jax.ShapeDtypeStruct((block, D + LANES), bf16)] * 2
    else:
        out_specs = [wide, thin]
        out_shape = [jax.ShapeDtypeStruct((count, D), f32), jax.ShapeDtypeStruct((count, 1), f32)]
    return pl.pallas_call(
        lambda *refs: head_scan_kernel(*refs, carried=bool(carry), last=last),
        grid=(count // block,),
        in_specs=[wide]
        + [wide, thin][: len(carry)]
        + [
            pl.BlockSpec(chunk.shape, lambda i: (0, 0), pipeline_mode=pl.Buffered(1))
            for chunk in chunks
        ],
        out_specs=out_specs,
        out_shape=out_shape,
        compiler_params=pltpu.CompilerParams(vmem_limit_bytes=VMEM),
        cost_estimate=pl.CostEstimate(
            flops=4 * count * vocab * D, bytes_accessed=2 * vocab * D + 4 * count * D,
            transcendentals=count * vocab,
        ),
        name="head_scan",
    )(rows, *carry, *chunks)


def head_grad_kernel(table_ref, rows_ref, lse_ref, weight_ref, *refs):
    out_ref = refs[-1]
    rows = rows_ref[...]
    logits = nt(table_ref[...], rows)
    grad = (jnp.exp(logits - lse_ref[0]) * weight_ref[0]).astype(bf16)
    part = nn(grad, rows)

    @pl.when(pl.program_id(0) == 0)
    def _():
        out_ref[...] = part if len(refs) == 1 else refs[0][...] + part

    @pl.when(pl.program_id(0) > 0)
    def _():
        out_ref[...] += part


def head_grad(table_low, rows, lse, weight, half, carry=()):
    vocab, count, block = table_low.shape[0], rows.shape[0], HEAD_BLOCK
    steps = count // block
    part = steps // 2
    stat = pl.BlockSpec((1, 1, block), lambda i: (i + half * part, 0, 0))
    whole = pl.BlockSpec((vocab, D), lambda i: (0, 0))
    return pl.pallas_call(
        head_grad_kernel,
        grid=(part,),
        in_specs=[whole, pl.BlockSpec((block, D), lambda i: (i + half * part, 0)), stat, stat]
        + [whole] * len(carry),
        out_specs=whole,
        out_shape=jax.ShapeDtypeStruct((vocab, D), f32),
        compiler_params=pltpu.CompilerParams(vmem_limit_bytes=VMEM),
        cost_estimate=pl.CostEstimate(
            flops=2 * count * vocab * D, bytes_accessed=count * D + 6 * vocab * D,
            transcendentals=count * vocab // 2,
        ),
        name="head_grad",
    )(table_low, rows, lse.reshape(steps, 1, block), weight, *carry)


def permute(value, axis, target):
    return lax.ppermute(value, axis, [(i, target(i)) for i in range(lax.axis_size(axis))])


def other_core(value):
    return permute(value, "mp", lambda i: i ^ 1)


def along_x(value, step):
    chips = lax.axis_size("mp") // 2
    return permute(value, "mp", lambda i: (i // 2 + step) % chips * 2 + i % 2)


def ring_order(count):
    return list(range(0, count, 2)) + list(range(count - 1, 0, -2))


def after(value, *others):
    return lax.optimization_barrier((value, *others))[0]


def ring_hop(upward, downward):
    count = lax.axis_size("dp")
    order = ring_order(count)
    spot = [order.index(i) for i in range(count)]
    return (
        permute(upward, "dp", lambda i: order[(spot[i] + 1) % count]),
        permute(downward, "dp", lambda i: order[(spot[i] - 1) % count]),
    )


def ring_middle(first, gates):
    upward, downward = first
    pieces = []
    for step in range(2, lax.axis_size("dp") // 2):
        upward, downward, _ = lax.optimization_barrier(
            (upward, downward, gates[min(step - 2, len(gates) - 1)])
        )
        upward, downward = ring_hop(upward, downward)
        pieces += [upward, downward]
    return pieces


def one_hot(index, count):
    return (index[:, None] == jnp.arange(count, dtype=jnp.int32)[None, :]).astype(bf16)


def placed(index, values, count):
    hit = index[None, :] == jnp.arange(count, dtype=jnp.int32)[:, None]
    return jnp.max(jnp.where(hit, values[None, :], -1), 1)


def rank_before(choice):
    count = choice.shape[0]
    earlier = (
        jnp.arange(count)[None, :] < jnp.arange(count)[:, None]
    ).astype(bf16)
    return jnp.dot(earlier, choice.astype(bf16), preferred_element_type=f32)


def grad_pack_kernel(core_ref, *refs, plan, rows_of, world):
    refs = dict(enumerate(refs))
    for left, right, held in plan:
        refs[held][...] = tn(refs[left][...], refs[right][...])
    mine_ref, theirs_ref = refs[rows_of[-1][0]], refs[rows_of[-1][0] + 1]
    second = core_ref[0] == 1
    total = mine_ref.shape[1]
    for j in range(world // 2):
        mine, theirs, filled = [], [], 0
        for held, rows, column in rows_of[:-1]:
            if column is None:
                mine.append(refs[held][...])
                theirs.append(mine[-1])
                filled += rows
                continue
            low = refs[held][2 * j * rows : (2 * j + 1) * rows, column : column + D]
            high = refs[held][(2 * j + 1) * rows : (2 * j + 2) * rows, column : column + D]
            mine.append(jnp.where(second, high, low))
            theirs.append(jnp.where(second, low, high))
            filled += rows
        if filled < total:
            mine.append(jnp.zeros((total - filled, D), f32))
            theirs.append(mine[-1])
        mine_ref[j] = jnp.concatenate(mine, 0).astype(bf16)
        theirs_ref[j] = jnp.concatenate(theirs, 0).astype(bf16)


def grad_pack(products, rows, world):
    core = jnp.reshape(lax.axis_index("mp") % 2, (1,)).astype(jnp.int32)
    operands = [value for product in products for value in product] + list(rows)
    inputs, count = len(operands), len(products)
    plan = [(2 * i, 2 * i + 1, inputs + 2 + i) for i in range(count)]
    pieces, scratch, flops = [], [], 0
    for i, (left, right) in enumerate(products):
        flops += 2 * left.shape[0] * left.shape[1] * right.shape[1]
        scratch.append(pltpu.VMEM((left.shape[1], right.shape[1]), f32))
        for column in range(0, right.shape[1], D):
            pieces.append((inputs + 2 + i, left.shape[1] // world, column))
    for i, value in enumerate(rows):
        pieces.append((2 * count + i, value.shape[0], None))
    total = -(-sum(piece[1] for piece in pieces) // 16) * 16
    pieces.append((inputs, 0, 0))
    shape = jax.ShapeDtypeStruct((world // 2, total, D), bf16)
    return pl.pallas_call(
        lambda *refs: grad_pack_kernel(*refs, plan=plan, rows_of=pieces, world=world),
        in_specs=[pl.BlockSpec(memory_space=pltpu.SMEM)]
        + [pl.BlockSpec(memory_space=pltpu.VMEM)] * inputs,
        out_specs=[pl.BlockSpec(memory_space=pltpu.VMEM)] * 2,
        out_shape=[shape, shape],
        scratch_shapes=scratch,
        compiler_params=pltpu.CompilerParams(vmem_limit_bytes=VMEM),
        cost_estimate=SMALL_COST,
        name="grad_pack",
    )(core, *operands)


class RingSum:

    def __init__(self, mine, theirs, x_first=False, gate=None):
        self.count = lax.axis_size("dp")
        self.chips = lax.axis_size("mp") // 2
        self.x_first = x_first
        shape = (self.count, self.chips, -1, D)
        got = other_core(theirs)
        got = (got if gate is None else after(got, gate)).reshape(shape)
        self.terms = [mine.reshape(shape), got]
        if x_first:
            chip = lax.axis_index("mp") // 2

            def for_chip(index):
                return sum(
                    lax.dynamic_index_in_dim(term, index, 1, keepdims=False).astype(f32)
                    for term in self.terms
                ).astype(bf16)

            self.terms = [for_chip(chip)] + [
                along_x(for_chip((chip + step) % self.chips), step)
                for step in range(1, self.chips)
            ]
        side, at = lax.axis_index("dp") % 2, lax.axis_index("dp") // 2
        self.here = jnp.where(side == 0, at, self.count - 1 - at)
        self.up_steps, self.down_steps = self.count // 2, (self.count - 1) // 2
        self.upward = self.downward = None
        self.step = 0

    def ready(self, *gates):
        if gates:
            self.terms[-1] = after(self.terms[-1], *gates)
        self.upward = self.part(self.up_steps).astype(bf16)
        self.downward = self.part(-self.down_steps).astype(bf16)

    def part(self, step):
        spot = lax.rem(self.here + step + self.count, self.count)
        at = jnp.where(2 * spot < self.count, 2 * spot, 2 * (self.count - 1 - spot) + 1)
        return sum(
            lax.dynamic_index_in_dim(term, at, 0, keepdims=False).astype(f32)
            for term in self.terms
        )

    def hop(self, gate=None):
        self.step += 1
        step, down = self.step, self.downward
        self.upward, down = ring_hop(self.upward, down)
        if gate is not None:
            self.upward, down, _ = lax.optimization_barrier((self.upward, down, gate))
        if step <= self.down_steps:
            self.downward = down
        if step < self.up_steps:
            self.upward = (self.upward.astype(f32) + self.part(self.up_steps - step)).astype(bf16)
        if step < self.down_steps:
            self.downward = (self.downward.astype(f32) + self.part(step - self.down_steps)).astype(
                bf16
            )

    def wait(self, gate):
        self.upward, self.downward, _ = lax.optimization_barrier((self.upward, self.downward, gate))

    def total(self):
        while self.step < self.up_steps:
            self.hop()
        line = self.part(0) + self.upward.astype(f32) + self.downward.astype(f32)
        if self.x_first:
            return [line]
        line = line.astype(bf16)
        chip = lax.axis_index("mp") // 2
        terms = [lax.dynamic_index_in_dim(line, chip, 0, keepdims=False)]
        for step in range(1, self.chips):
            going = lax.dynamic_index_in_dim(line, (chip + step) % self.chips, 0, keepdims=False)
            terms.append(along_x(going, step))
        return terms


def renew(weight, moment, average, gradient, factor):
    clipped = gradient * factor
    moment_new = MOMENTUM * moment + clipped
    weight_new = weight - STEP_RATE * (clipped + MOMENTUM * moment_new)
    average_new = AVERAGE_DECAY * average + (1.0 - AVERAGE_DECAY) * weight_new
    return (weight_new, moment_new, average_new)


def finish_sum_kernel(*refs, count):
    (row_ref, *square_refs), terms, (total_ref, spread_ref) = (
        refs[:count], refs[count:-2], refs[-2:]
    )
    total = sum((term[...].astype(f32) for term in terms[1:]), terms[0][...].astype(f32))
    total_ref[...] = total
    squares = jnp.sum(jnp.sum(total * total, 0, keepdims=True), 1, keepdims=True)
    lane = lax.broadcasted_iota(jnp.int32, (1, LANES), 1)
    for ref in square_refs:
        squares = squares + ref[...]
    row = row_ref[...] + jnp.where(lane == 0, squares, 0.0)
    spread_ref[...] = jnp.broadcast_to(row, spread_ref.shape)


def finish_sum(terms, numbers, world):
    vmem = pl.BlockSpec(memory_space=pltpu.VMEM)
    return pl.pallas_call(
        lambda *refs: finish_sum_kernel(*refs, count=len(numbers)),
        in_specs=[vmem] * (len(numbers) + len(terms)),
        out_specs=[vmem] * 2,
        out_shape=[
            jax.ShapeDtypeStruct(terms[0].shape, f32),
            jax.ShapeDtypeStruct((world, LANES), f32),
        ],
        compiler_params=pltpu.CompilerParams(vmem_limit_bytes=VMEM),
        name="finish_sum",
    )(*numbers, *terms)


def clip_factor(totals):
    return jnp.minimum(1.0, CLIP_LIMIT / jnp.sqrt(totals[:, 0:1]))


def renew_kernel(spread_ref, early_ref, late_ref, *refs):
    states, outs = [refs[i : i + 3] for i in range(0, 12, 3)], refs[12:]
    totals = jnp.sum(spread_ref[...], 0, keepdims=True)
    outs[-1][...] = totals
    factor = clip_factor(totals)
    rows = states[1][0].shape[0]
    rows_patch, rows_down = states[0][0].shape[0], states[3][0].shape[0]
    attn = [(early_ref, j * rows, rows) for j in range(3)]
    attn.append((late_ref, 4 * rows + rows_down, rows))
    pieces = (
        [(early_ref, 3 * rows, rows_patch)],
        attn,
        [(late_ref, j * rows, rows) for j in range(4)],
        [(late_ref, 4 * rows, rows_down)],
    )
    for index, (state, parts) in enumerate(zip(states, pieces)):
        new = outs[4 * index : 4 * index + 4]
        for j, (ref, start, count) in enumerate(parts):
            at = slice(j * D, (j + 1) * D)
            gradient = ref[start : start + count, :]
            results = renew(
                state[0][:, at], state[1][:, at], state[2][:, at], gradient, factor
            )
            for out, value in zip(new, results):
                out[:, at] = value
            new[3][:, at] = results[0].astype(bf16)


def renew_matrices(spread, early, late, states):
    vmem = pl.BlockSpec(memory_space=pltpu.VMEM)
    shapes = []
    for state in states:
        shape = state[0].shape
        shapes += [jax.ShapeDtypeStruct(shape, f32)] * 3 + [jax.ShapeDtypeStruct(shape, bf16)]
    shapes.append(jax.ShapeDtypeStruct((1, LANES), f32))
    return pl.pallas_call(
        renew_kernel,
        in_specs=[vmem] * 15,
        out_specs=[vmem] * len(shapes),
        out_shape=shapes,
        compiler_params=pltpu.CompilerParams(vmem_limit_bytes=VMEM),
        name="renew_matrices",
    )(spread, early, late, *[value for state in states for value in state])


def shards(
    patches,
    patch_pos,
    owner,
    local_row,
    counts,
    task,
    table,
    table_mom,
    table_avg,
    patch_w,
    patch_mom,
    patch_avg,
    attn_w,
    attn_mom,
    attn_avg,
    up_w,
    up_mom,
    up_avg,
    down_w,
    down_mom,
    down_avg,
    gains,
    gain_mom,
    gain_avg,
):
    groups, owners = lax.axis_size("dp"), lax.axis_size("mp")
    world = groups * owners
    tokens_here = patches.shape[0]
    rows_own = table.shape[0]
    rows_attn, rows_patch, rows_down = attn_w.shape[0], patch_w.shape[0], down_w.shape[0]
    cols_gain = gains.shape[1]
    place = lax.axis_index("dp") * owners + lax.axis_index("mp")

    table_low = table.astype(bf16)
    gain_row = jnp.pad(gains.astype(bf16).reshape(1, 3 * cols_gain), ((0, 0), (0, 4 * D - 3 * cols_gain)))
    patch_rows = jnp.pad(patch_w.astype(bf16), ((0, -rows_patch % 4), (0, 0)))
    early = jnp.concatenate([attn_w.astype(bf16), patch_rows.reshape(-1, 4 * D), gain_row], 0)
    late = jnp.concatenate(
        [
            up_w.astype(bf16),
            jnp.concatenate(
                [down_w[j : j + rows_attn] for j in range(0, rows_down, rows_attn)], 1
            ).astype(bf16),
        ],
        0,
    )
    early_all, late_all = (
        lax.all_gather(jnp.pad(w, ((0, -w.shape[0] % 8), (0, 0))), AXES, axis=0, tiled=False)
        for w in (early, late)
    )

    first_pieces = ring_hop(table_low, table_low)

    my_counts = lax.dynamic_slice_in_dim(counts, place, 1, 0)
    first_tok, alive = my_counts[0, 0], my_counts[0, 1]
    positions = jnp.arange(tokens_here, dtype=jnp.int32)
    is_patch = (positions < first_tok)[:, None]
    is_token = (positions >= first_tok) & (positions < first_tok + alive)
    target_owner = owner[:, 0]

    share = -(-3 * tokens_here // (2 * world) // 16) * 16
    identity = target_owner * (rows_own * groups) + local_row
    same = (identity[:, None] == identity[None, :]) & is_token[None, :]
    first_same = jnp.min(jnp.where(same, positions[None, :], tokens_here), 1)
    leads = is_token & (first_same == positions)
    dest = identity // rows_own
    leads_to = (dest[:, None] == jnp.arange(world)[None, :]) & leads[:, None]
    lead_rank = jnp.sum(jnp.where(leads_to, rank_before(leads_to), 0.0), 1).astype(jnp.int32)
    far_rank = jnp.max(
        jnp.where(first_same[:, None] == positions[None, :], lead_rank[None, :], 0), 1
    )
    far_row = identity - dest * rows_own
    most = jnp.max(jnp.sum(leads_to.astype(jnp.int32), 0))

    def far_slots(start, share, limit):
        within = far_rank - start
        fits = is_token & (within >= 0) & (within < limit)
        return jnp.where(fits, dest * share + within, -1)

    def far_ids(slots, extra, share):
        ids = placed(slots, far_row, world * share).reshape(world, share)
        ids = jnp.concatenate([ids, jnp.full((world, 1), extra, jnp.int32)], 1)
        return lax.all_to_all(ids, ("mp", "dp"), split_axis=0, concat_axis=0, tiled=True)

    first_slots = far_slots(0, share, share - 1)
    first_ids = far_ids(first_slots, most, share)
    few = 16
    turns = (jnp.max(first_ids[:, share]) - (share - 1) + few - 1) // few

    def far_fetch(slots, ids, share):
        spread = one_hot(ids[:, :share].reshape(-1), rows_own)
        rows = jnp.dot(spread, table_low, preferred_element_type=f32).astype(bf16)
        rows = lax.optimization_barrier((rows, *first_pieces))[0]
        return lax.all_to_all(
            rows.reshape(world, share, D), ("mp", "dp"), split_axis=0, concat_axis=0, tiled=True
        ).reshape(world * share, D)

    def far_spread(slots, arrived, share):
        return jnp.dot(one_hot(slots, world * share), arrived, preferred_element_type=f32)

    def far_pack(slots, values, share, extra=None):
        rows = jnp.dot(one_hot(slots, world * share).T, values, preferred_element_type=f32)
        if extra is not None:
            spare = lax.broadcasted_iota(jnp.int32, (world * share, 1), 0) % share == share - 1
            rows = jnp.where(spare, extra, rows)
        return rows.astype(bf16)

    def far_send(packed, share):
        return lax.all_to_all(
            packed.reshape(world, share, D),
            ("mp", "dp"), split_axis=0, concat_axis=0, tiled=True,
        ).reshape(world * share, D)

    def far_add(arrived, ids, share):
        spread = one_hot(ids[:, :share].reshape(-1), rows_own)
        return tn(spread, arrived)


    def columns(gathered, low, high):
        return gathered[:, :rows_attn, low * D : high * D].reshape(-1, (high - low) * D)

    w_q, w_kv, w_out = columns(early_all, 0, 1), columns(early_all, 1, 3), columns(early_all, 3, 4)
    gain_at = rows_attn + patch_rows.shape[0] // 4
    w_patch = (
        early_all[:, rows_attn:gain_at].reshape(world, -1, D)[:, :rows_patch].reshape(-1, D)
    )
    gain_all = (
        early_all[:, gain_at, : 3 * cols_gain]
        .reshape(world, 3, cols_gain).transpose(1, 0, 2).reshape(3, D).astype(f32)
    )
    scored_all = counts[:, 2].astype(f32)
    per_task = (task[:, None] == jnp.arange(TASKS)[None, :]).astype(f32)
    task_total = jnp.sum(per_task * scored_all[:, None], 0)
    present = jnp.sum((task_total > 0).astype(f32))
    inverse_seq = jnp.sum(per_task / jnp.maximum(task_total, 1.0)[None, :], 1)
    row_live = (jnp.arange(LOSS)[None, :] < counts[:, 2:3]).astype(f32) * inverse_seq[:, None]
    head_weight = (row_live / present).reshape(-1, 1, HEAD_BLOCK)

    arrived = far_fetch(first_slots, first_ids, share)
    arrived, head_weight = lax.optimization_barrier((arrived, head_weight, w_kv, w_q, w_patch))[:2]
    looked = far_spread(first_slots, arrived, share)

    def fetch_turn(turn, total):
        slots = far_slots(share - 1 + turn * few, few, few)
        return total + far_spread(slots, far_fetch(slots, far_ids(slots, 0, few), few), few)

    looked = lax.fori_loop(0, turns, fetch_turn, looked)

    w_up = columns(late_all, 0, 4)
    w_down = jnp.concatenate(
        [late_all[:, rows_attn : 2 * rows_attn, j : j + D] for j in range(0, 4 * D, D)], 1
    ).reshape(world * rows_down, D)

    def patch_rows_of(pixels):
        position_code = (patch_pos[:, None] == jnp.arange(POSN)[None, :]).astype(bf16)
        return jnp.concatenate([pixels, position_code], 1)

    patch_in = patch_rows_of(patches)
    from_patch = jnp.dot(patch_in, w_patch, preferred_element_type=f32)
    embed_scale = math.sqrt(D)
    embedded = jnp.where(is_patch, from_patch, 0.0) + embed_scale * looked
    normed_first = layer_norm(embedded, gain_all[0]).astype(bf16)
    key_values = jnp.dot(normed_first, w_kv, preferred_element_type=f32).astype(bf16)

    pick = first_tok - 1
    pick_at = jnp.reshape(pick, (1,))

    def picked_rows(values, start=pick):
        return lax.dynamic_slice_in_dim(values, start, LOSS, 0)

    normed_pick = picked_rows(normed_first)
    query_pick = jnp.dot(normed_pick, w_q, preferred_element_type=f32).astype(bf16)
    attended_pick, lse_pick = attention_pick(pick_at, query_pick, key_values)
    branch_pick = jnp.dot(attended_pick, w_out, preferred_element_type=f32)
    middle_pick = picked_rows(embedded) + branch_pick
    normed_mid, mid_back = jax.vjp(layer_norm, middle_pick, gain_all[1])
    normed_mid = normed_mid.astype(bf16)
    query_all = jnp.dot(normed_first, w_q, preferred_element_type=f32).astype(bf16)
    attended = attention_all(after(query_all, attended_pick), key_values)
    normed_mid = after(normed_mid, attended)
    hidden_pick = jnp.dot(normed_mid, w_up, preferred_element_type=f32)
    active_f32, gelu_back = jax.vjp(gelu_tanh, hidden_pick)
    active_pick = active_f32.astype(bf16)
    result_pick = middle_pick + jnp.dot(active_pick, w_down, preferred_element_type=f32)
    final_rows, final_back = jax.vjp(layer_norm, result_pick, gain_all[2])
    own_rows = final_rows.astype(bf16)
    chunks = [table_low, *first_pieces, *ring_middle(first_pieces, (arrived, attended))]
    half = rows_own // 32 * 16
    last_up, last_down = after(chunks[-2], own_rows)[:half], after(chunks[-1], own_rows)[half:]
    chunks += ring_hop(last_up, last_down)
    target_rows = picked_rows(looked, first_tok)

    chips = owners // 2
    line = jnp.stack([own_rows] + [along_x(own_rows, step) for step in range(1, chips)])
    group_rows = jnp.stack([line, other_core(line)])
    group_rows = group_rows.reshape(-1, D)
    carry = head_scan(after(group_rows, last_up, last_down), chunks[:5], last=False)
    rows_sent = after(own_rows, carry[0], chunks[-1], chunks[-2])
    mine, theirs = head_scan(group_rows, chunks[5:], carry)
    (line,) = merge([mine, other_core(theirs)])
    mean_own, own_total = merge(
        [line[:LOSS]]
        + [along_x(line[step * LOSS : (step + 1) * LOSS], -step) for step in range(1, chips)],
        last=True,
    )
    own_total = own_total[:, 0]

    picked = jnp.sum(own_rows.astype(f32) * target_rows, 1)
    own_weight = lax.dynamic_slice_in_dim(row_live, place, 1, 0)[0]
    loss_part = jnp.sum(own_weight * (own_total - picked))

    rows_all = lax.all_gather(rows_sent, AXES, axis=0, tiled=True)
    high = lax.reduce_precision(own_total, 8, 7)
    low = lax.reduce_precision(own_total - high, 8, 7)
    total_row = jnp.concatenate([high, low, own_total - high - low])[None, :]

    scaled_weight = (own_weight / present)[:, None]
    grad_rows = scaled_weight * (mean_own - target_rows)
    grad_result, grad_gain_last = final_back(grad_rows)
    grad_second = grad_result.astype(bf16)
    grad_hidden = gelu_back(nt(grad_second, w_down))[0].astype(bf16)
    grad_middle, grad_gain_mid = mid_back(nt(grad_hidden, w_up))
    grad_middle = grad_result + grad_middle
    grad_branch = grad_middle.astype(bf16)
    late_mine, late_theirs = grad_pack(
        [(normed_mid, grad_hidden), (active_pick, grad_second), (attended_pick, grad_branch)],
        [], world,
    )
    grad_attended = after(nt(grad_branch, w_out).astype(bf16), late_theirs)
    grad_q, grad_k, grad_v = attention_back(
        pick_at, query_pick, key_values, attended_pick, grad_attended, lse_pick
    )
    late_sum = RingSum(late_mine, late_theirs, gate=grad_q)
    late_sum.ready()
    grad_patch_rows, grad_looked, grad_gain_first = first_back(
        jnp.reshape(first_tok, (1,)), after(grad_k, late_sum.upward), grad_v, w_kv, grad_q, w_q,
        embedded, gain_all[0:1], grad_middle, -scaled_weight * own_rows.astype(f32),
    )
    late_sum.hop(grad_looked)
    packed = far_pack(first_slots, after(grad_looked, late_sum.upward), share, total_row)
    grad_arrived = far_send(packed, share)
    grad_gain = jnp.stack([grad_gain_first[0], grad_gain_mid, grad_gain_last])
    early_mine, early_theirs = grad_pack(
        [
            (normed_pick, grad_q),
            (normed_first, grad_k),
            (normed_first, grad_v),
            (patch_rows_of(after(patches, packed)), after(grad_patch_rows, packed)),
        ],
        [grad_gain], world,
    )

    lane = lax.broadcasted_iota(jnp.int32, (1, LANES), 1)
    row = layer_stats(
        jnp.reshape(first_tok + alive, (1,)), after(attended, early_theirs), embedded, w_out, w_up,
        w_down, gain_all[1:2], jnp.where(lane == 1, loss_part, 0.0),
    )

    early_sum = RingSum(early_mine, early_theirs, True, gate=row)
    grad_arrived = after(grad_arrived, early_sum.terms[0])
    late_sum.hop(grad_arrived)
    spare_rows = grad_arrived.reshape(owners, groups, share, D)[:, :, share - 1].astype(f32)
    total_all = spare_rows[..., :LOSS] + spare_rows[..., LOSS : 2 * LOSS] + spare_rows[..., 2 * LOSS :]
    total_all = total_all.transpose(1, 0, 2)
    early_sum.ready(late_sum.upward)
    head_first = head_grad(
        table_low, after(rows_all, late_sum.upward, early_sum.upward), total_all, head_weight, 0
    )
    late_sum.hop(head_first)
    early_sum.hop(late_sum.upward)
    table_head = head_grad(
        table_low, after(rows_all, late_sum.upward, early_sum.upward), total_all, head_weight, 1,
        (head_first,),
    )
    late_sum.hop(table_head)
    early_sum.hop(late_sum.upward)
    grad_table = table_head + far_add(
        after(grad_arrived, late_sum.upward, early_sum.upward), first_ids, share
    )
    late_terms = late_sum.total()
    (summed_early,) = early_sum.total()

    def next_turn(turn, total):
        slots = far_slots(share - 1 + turn * few, few, few)
        return total + far_add(
            far_send(far_pack(slots, grad_looked, few), few), far_ids(slots, 0, few), few
        )

    grad_table = lax.fori_loop(0, turns, next_turn, grad_table)

    edge = 3 * rows_attn + rows_patch
    summed_gain = lax.dynamic_slice_in_dim(
        summed_early[edge : edge + 3], place * cols_gain, cols_gain, 1
    )
    squares = [
        jnp.sum(part * part, keepdims=True) for part in (grad_table, summed_early[:edge], summed_gain)
    ]
    summed_late, spread = finish_sum(late_terms, [row, *squares], world)
    spread = lax.all_to_all(spread, AXES, 0, 0, tiled=True)
    *matrices, totals = renew_matrices(
        spread, summed_early, summed_late,
        (
            (patch_w, patch_mom, patch_avg),
            (attn_w, attn_mom, attn_avg),
            (up_w, up_mom, up_avg),
            (down_w, down_mom, down_avg),
        ),
    )
    factor = clip_factor(jnp.sum(spread, 0, keepdims=True))[0, 0]
    table_new = renew(table, table_mom, table_avg, grad_table, factor)
    gains_new = renew(gains, gain_mom, gain_avg, summed_gain, factor)
    clip_norm = jnp.sqrt(totals[0, 0])
    loss_total = totals[0, 1]
    valid_total = jnp.sum(counts[:, :2].astype(f32))
    rms_stats = jnp.sqrt(totals[0, 2:6] / valid_total)
    return (
        *table_new, table_new[0].astype(bf16), *matrices, *gains_new,
        loss_total, present, clip_norm, rms_stats,
    )


def solution(mesh):
    whole, split = P(), P(AXES)
    rows, vocab, columns = P(AXES, None), P(("mp", "dp"), None), P(None, AXES)
    in_specs = (rows, split, rows, split, whole, whole) + (vocab,) * 3 + (rows,) * 12 + (columns,) * 3
    out_specs = (vocab,) * 4 + (rows,) * 16 + (columns,) * 3 + (whole,) * 4
    return jax.shard_map(shards, mesh=mesh, in_specs=in_specs, out_specs=out_specs, check_vma=False)
```

```python
import math

import jax
import jax.numpy as jnp
from jax import lax
from jax.experimental import pallas as pl
from jax.experimental.pallas import tpu as pltpu
from jax.sharding import PartitionSpec as P

D = 768
HEADS = 24
HDIM = 32
POSN = 128
SEQ_LEN = 1024
LOSS = 256
TASKS = 32

NORM_EPS = 1e-05
STEP_RATE = 5000.0
MOMENTUM = 0.5
AVERAGE_DECAY = 0.5
CLIP_LIMIT = 0.02

AXES = ("dp", "mp")
LANES = 128
GROUP = LANES // HDIM
TILES = D // LANES
SCALE = HDIM ** (-0.5)
SCALE_LOG2 = SCALE * math.log2(math.e)
VMEM = 56 * 2**20
HEAD_BLOCK = 2048
SMALL_COST = pl.CostEstimate(flops=1, bytes_accessed=1, transcendentals=0)
bf16 = jnp.bfloat16
f32 = jnp.float32


def contract(left, right, left_dim, right_dim):
    return lax.dot_general(
        left, right, (((left_dim,), (right_dim,)), ((), ())), preferred_element_type=f32
    )


def nn(left, right):
    return contract(left, right, 1, 0)


def nt(left, right):
    return contract(left, right, 1, 1)


def tn(left, right):
    return contract(left, right, 0, 0)


def layer_norm(values, gain):
    row_mean = jnp.mean(values, -1, keepdims=True)
    centred = values - row_mean
    spread = jnp.mean(centred * centred, -1, keepdims=True)
    return centred * lax.rsqrt(spread + NORM_EPS) * gain


def gelu_tanh(values):
    return jax.nn.gelu(values, approximate=True)


def head_masks():
    lane = lax.broadcasted_iota(jnp.int32, (1, LANES), 1) // HDIM
    return [lane == head for head in range(GROUP)]


def only(mask, block):
    return jnp.where(mask, block, jnp.zeros((), block.dtype))


def attention_all_kernel(q_ref, k_ref, v_ref, o_ref, *, block):
    length = q_ref.shape[0]
    masks = head_masks()
    row = lax.broadcasted_iota(jnp.int32, (block, block), 0)
    col = lax.broadcasted_iota(jnp.int32, (block, block), 1)
    triangle = col <= row
    for index in range(length // block):
        start, end = index * block, (index + 1) * block
        q = q_ref[start:end, :]
        k, v = k_ref[0:end, :], v_ref[0:end, :]
        joined = jnp.zeros((block, LANES), f32)
        for mask in masks:
            scores = nt(only(mask, q), k)
            diagonal = jnp.where(triangle, scores[:, start:], -1e30)
            scores = jnp.concatenate([scores[:, :start], diagonal], 1) if index else diagonal
            top = jnp.max(scores, 1, keepdims=True) * SCALE_LOG2
            power = jnp.exp2(scores * SCALE_LOG2 - top)
            total = jnp.sum(power, 1, keepdims=True)
            joined = jnp.where(mask, nn(power.astype(bf16), v) / total, joined)
        o_ref[start:end, :] = joined.astype(bf16)


def attention_all(queries, key_values):
    length = queries.shape[0]
    return pl.pallas_call(
        lambda *refs: attention_all_kernel(*refs, block=512),
        grid=(TILES,),
        in_specs=[
            pl.BlockSpec((length, LANES), lambda g: (0, g)),
            pl.BlockSpec((length, LANES), lambda g: (0, g)),
            pl.BlockSpec((length, LANES), lambda g: (0, TILES + g)),
        ],
        out_specs=pl.BlockSpec((length, LANES), lambda g: (0, g)),
        out_shape=jax.ShapeDtypeStruct((length, D), bf16),
        compiler_params=pltpu.CompilerParams(vmem_limit_bytes=VMEM),
        cost_estimate=pl.CostEstimate(
            flops=2 * 2 * HEADS * length * length * LANES, bytes_accessed=8 * length * D,
            transcendentals=HEADS * length * length,
        ),
        name="attention_all",
    )(queries, key_values, key_values)


def attention_pick_kernel(first_ref, q_ref, k_ref, v_ref, o_ref, lse_ref):
    rows, length = q_ref.shape[0], k_ref.shape[0]
    masks = head_masks()
    row = lax.broadcasted_iota(jnp.int32, (rows, length), 0)
    col = lax.broadcasted_iota(jnp.int32, (rows, length), 1)
    allowed = col <= row + first_ref[0]
    lane = lax.broadcasted_iota(jnp.int32, (1, LANES), 1)
    q, k, v = q_ref[...], k_ref[...], v_ref[...]
    joined = jnp.zeros((rows, LANES), f32)
    stat = jnp.zeros((rows, LANES), f32)
    for head, mask in enumerate(masks):
        scores = jnp.where(allowed, nt(only(mask, q), k), -1e30)
        top = jnp.max(scores, 1, keepdims=True) * SCALE_LOG2
        power = jnp.exp2(scores * SCALE_LOG2 - top)
        total = jnp.sum(power, 1, keepdims=True)
        joined = jnp.where(mask, nn(power.astype(bf16), v) / total, joined)
        stat = jnp.where(lane == head, top + jnp.log2(total), stat)
    o_ref[...] = joined.astype(bf16)
    lse_ref[0] = stat.T[0:8, :]


def attention_pick(first, queries, key_values):
    rows, length = queries.shape[0], key_values.shape[0]
    return pl.pallas_call(
        attention_pick_kernel,
        grid_spec=pltpu.PrefetchScalarGridSpec(
            num_scalar_prefetch=1,
            grid=(TILES,),
            in_specs=[
                pl.BlockSpec((rows, LANES), lambda g, s: (0, g)),
                pl.BlockSpec((length, LANES), lambda g, s: (0, g)),
                pl.BlockSpec((length, LANES), lambda g, s: (0, TILES + g)),
            ],
            out_specs=[
                pl.BlockSpec((rows, LANES), lambda g, s: (0, g)),
                pl.BlockSpec((1, 8, rows), lambda g, s: (g, 0, 0)),
            ],
        ),
        out_shape=[
            jax.ShapeDtypeStruct((rows, D), bf16),
            jax.ShapeDtypeStruct((TILES, 8, rows), f32),
        ],
        compiler_params=pltpu.CompilerParams(vmem_limit_bytes=VMEM),
        cost_estimate=pl.CostEstimate(
            flops=2 * 2 * HEADS * rows * length * LANES, bytes_accessed=6 * length * D,
            transcendentals=HEADS * rows * length,
        ),
        name="attention_pick",
    )(first, queries, key_values, key_values)


def attention_back_kernel(
    first_ref, q_ref, k_ref, v_ref, o_ref, do_ref, lse_ref, dq_ref, dk_ref, dv_ref
):
    rows, length = q_ref.shape[0], k_ref.shape[0]
    masks = head_masks()
    key = lax.broadcasted_iota(jnp.int32, (length, rows), 0)
    query = lax.broadcasted_iota(jnp.int32, (length, rows), 1)
    allowed = key <= query + first_ref[0]
    q, k, v, do = q_ref[...], k_ref[...], v_ref[...], do_ref[...]
    share = (
        lax.broadcasted_iota(jnp.int32, (8, LANES), 0)
        == lax.broadcasted_iota(jnp.int32, (8, LANES), 1) // HDIM
    ).astype(f32)
    inner = lax.dot_general(
        share, do.astype(f32) * o_ref[...].astype(f32), (((1,), (1,)), ((), ())),
        preferred_element_type=f32, precision=lax.Precision.HIGHEST,
    )
    lse = lse_ref[0]
    dq = jnp.zeros((rows, LANES), f32)
    dk = jnp.zeros((length, LANES), f32)
    dv = jnp.zeros((length, LANES), f32)
    for head, mask in enumerate(masks):
        k_head = only(mask, k)
        scores = nt(k_head, q)
        chance = jnp.where(
            allowed, jnp.exp2(scores * SCALE_LOG2 - lse[head : head + 1, :]), 0.0
        )
        d_chance = nt(only(mask, v), do)
        d_scores = (chance * (d_chance - inner[head : head + 1, :])).astype(bf16)
        dv = jnp.where(mask, nn(chance.astype(bf16), do), dv)
        dk = jnp.where(mask, nn(d_scores, q), dk)
        dq = dq + tn(d_scores, k_head)
    dq_ref[...] = (dq * SCALE).astype(bf16)
    dk_ref[...] = (dk * SCALE).astype(bf16)
    dv_ref[...] = dv.astype(bf16)


def attention_back(first, queries, key_values, attended, grad_attended, lse):
    rows, length = queries.shape[0], key_values.shape[0]
    rows_spec = pl.BlockSpec((rows, LANES), lambda g, s: (0, g))
    all_spec = pl.BlockSpec((length, LANES), lambda g, s: (0, g))
    return pl.pallas_call(
        attention_back_kernel,
        grid_spec=pltpu.PrefetchScalarGridSpec(
            num_scalar_prefetch=1,
            grid=(TILES,),
            in_specs=[
                rows_spec,
                all_spec,
                pl.BlockSpec((length, LANES), lambda g, s: (0, TILES + g)),
                rows_spec,
                rows_spec,
                pl.BlockSpec((1, 8, rows), lambda g, s: (g, 0, 0)),
            ],
            out_specs=[rows_spec, all_spec, all_spec],
        ),
        out_shape=[
            jax.ShapeDtypeStruct((rows, D), bf16),
            jax.ShapeDtypeStruct((length, D), bf16),
            jax.ShapeDtypeStruct((length, D), bf16),
        ],
        compiler_params=pltpu.CompilerParams(vmem_limit_bytes=VMEM),
        cost_estimate=pl.CostEstimate(
            flops=5 * 2 * HEADS * rows * length * LANES, bytes_accessed=10 * length * D,
            transcendentals=HEADS * rows * length,
        ),
        name="attention_back",
    )(first, queries, key_values, key_values, attended, grad_attended, lse)


def layer_stats_kernel(
    valid_ref, attended_ref, x_ref, wout_ref, wup_ref, wdown_ref, gain_ref, row_ref, out_ref
):
    block = x_ref.shape[0]
    step = pl.program_id(0)
    embedded = x_ref[...]
    branch = nn(attended_ref[...], wout_ref[...])
    middle = embedded + branch
    normed = layer_norm(middle, gain_ref[...]).astype(bf16)
    active = gelu_tanh(nn(normed, wup_ref[...])).astype(bf16)
    second = nn(active, wdown_ref[...])
    valid = step * block + lax.broadcasted_iota(jnp.int32, (block, 1), 0) < valid_ref[0]
    lane = lax.broadcasted_iota(jnp.int32, (1, LANES), 1)
    sums = jnp.zeros((1, LANES), f32)
    for at, values in enumerate((embedded, branch, second, middle + second)):
        mean = jnp.where(valid, jnp.mean(values * values, 1, keepdims=True), 0.0)
        sums = jnp.where(lane == at + 2, jnp.sum(mean, 0, keepdims=True), sums)

    @pl.when(step == 0)
    def _():
        out_ref[...] = row_ref[...] + sums

    @pl.when(step > 0)
    def _():
        out_ref[...] += sums


def layer_stats(valid, attended, embedded, w_out, w_up, w_down, gain, row):
    length, block = embedded.shape[0], 256
    blocked = pl.BlockSpec((block, D), lambda i, s: (i, 0))

    def whole(value):
        return pl.BlockSpec(value.shape, lambda i, s: (0, 0), pipeline_mode=pl.Buffered(1))

    return pl.pallas_call(
        layer_stats_kernel,
        grid_spec=pltpu.PrefetchScalarGridSpec(
            num_scalar_prefetch=1,
            grid=(length // block,),
            in_specs=[blocked, blocked] + [whole(v) for v in (w_out, w_up, w_down, gain, row)],
            out_specs=pl.BlockSpec((1, LANES), lambda i, s: (0, 0)),
        ),
        out_shape=jax.ShapeDtypeStruct((1, LANES), f32),
        compiler_params=pltpu.CompilerParams(vmem_limit_bytes=VMEM),
        cost_estimate=SMALL_COST,
        name="layer_stats",
    )(valid, attended, embedded, w_out, w_up, w_down, gain, row)


def first_back_kernel(
    bounds_ref, k_ref, v_ref, wkv_ref, q_ref, wq_ref, x_ref, gain_ref, middle_ref, target_ref,
    patch_ref, looked_ref, dgain_ref, normed, residual, pulled,
):
    length, block = x_ref.shape[0], 128
    first = bounds_ref[0]
    normed[0:length, :] = nt(k_ref[...], wkv_ref[:, :D]) + nt(v_ref[...], wkv_ref[:, D:])
    residual[...] = jnp.zeros_like(residual)
    pulled[...] = jnp.zeros_like(pulled)

    def place(ref, rows, start):
        base = pl.multiple_of(start // 8 * 8, 8)
        padded = jnp.concatenate([rows, jnp.zeros((8, D), f32)], 0)
        turned = pltpu.roll(padded, start - base, 0)
        at = pl.ds(base, rows.shape[0] + 8)
        ref[at, :] = ref[at, :] + turned

    place(normed, nt(q_ref[...], wq_ref[...]), first - 1)
    place(residual, middle_ref[...], first - 1)
    place(pulled, target_ref[...], first)
    gain = gain_ref[...]
    dgain = jnp.zeros((1, D), f32)
    for start in range(0, length, block):
        at = slice(start, start + block)
        x, grad = x_ref[at, :], normed[at, :]
        centred = x - jnp.mean(x, 1, keepdims=True)
        spread = lax.rsqrt(jnp.mean(centred * centred, 1, keepdims=True) + NORM_EPS)
        unit = centred * spread
        dgain = dgain + jnp.sum(grad * unit, 0, keepdims=True)
        scaled = grad * gain
        inner = jnp.mean(scaled * unit, 1, keepdims=True)
        back = spread * (scaled - jnp.mean(scaled, 1, keepdims=True) - unit * inner)
        back = back + residual[at, :]
        row = start + lax.broadcasted_iota(jnp.int32, (block, 1), 0)
        patch_ref[at, :] = jnp.where(row < first, back, 0.0).astype(bf16)
        looked_ref[at, :] = (math.sqrt(D) * back + pulled[at, :]).astype(bf16)
    dgain_ref[...] = dgain


def first_back(first, grad_k, grad_v, w_kv, grad_q, w_q, embedded, gain, middle, target):
    length = embedded.shape[0]
    wide = jax.ShapeDtypeStruct((length, D), bf16)
    return pl.pallas_call(
        first_back_kernel,
        in_specs=[pl.BlockSpec(memory_space=pltpu.SMEM)]
        + [pl.BlockSpec(memory_space=pltpu.VMEM)] * 9,
        out_specs=[pl.BlockSpec(memory_space=pltpu.VMEM)] * 3,
        out_shape=[wide, wide, jax.ShapeDtypeStruct((1, D), f32)],
        scratch_shapes=[pltpu.VMEM((length + 16, D), f32)] * 3,
        compiler_params=pltpu.CompilerParams(vmem_limit_bytes=VMEM),
        cost_estimate=pl.CostEstimate(
            flops=2 * length * 2 * D * D, bytes_accessed=16 * length * D, transcendentals=0
        ),
        name="first_back",
    )(first, grad_k, grad_v, w_kv, grad_q, w_q, embedded, gain, middle, target)


def write_with_lse(ref, mean, lse):
    ref[:, :D] = mean.astype(bf16)
    high = lse.astype(bf16).astype(f32)
    low = (lse - high).astype(bf16).astype(f32)
    rest = lse - high - low
    lane = lax.broadcasted_iota(jnp.int32, (1, LANES), 1)
    tail = jnp.where(lane == 0, high, jnp.where(lane == 1, low, jnp.where(lane == 2, rest, 0.0)))
    ref[:, D:] = tail.astype(bf16)


def merge_kernel(*refs, count, last):
    means, sums = [], []
    for ref in refs[:count]:
        means.append(ref[:, :D].astype(f32))
        tail = ref[:, D:].astype(f32)
        sums.append(tail[:, 0:1] + tail[:, 1:2] + tail[:, 2:3])
    top = sums[0]
    for value in sums[1:]:
        top = jnp.maximum(top, value)
    powers = [jnp.exp(value - top) for value in sums]
    total = sum(powers[1:], powers[0])
    mean = sum((m * p for m, p in zip(means[1:], powers[1:])), means[0] * powers[0]) / total
    lse = top + jnp.log(total)
    if last:
        refs[count][...], refs[count + 1][...] = mean, lse
    else:
        write_with_lse(refs[count], mean, lse)


def merge(parts, last=False):
    rows = parts[0].shape[0]
    shapes = [jax.ShapeDtypeStruct((rows, D + LANES), bf16)]
    if last:
        shapes = [jax.ShapeDtypeStruct((rows, D), f32), jax.ShapeDtypeStruct((rows, 1), f32)]
    return pl.pallas_call(
        lambda *refs: merge_kernel(*refs, count=len(parts), last=last),
        in_specs=[pl.BlockSpec(memory_space=pltpu.VMEM)] * len(parts),
        out_specs=[pl.BlockSpec(memory_space=pltpu.VMEM)] * len(shapes),
        out_shape=shapes,
        compiler_params=pltpu.CompilerParams(vmem_limit_bytes=VMEM),
        name="merge",
    )(*parts)


def head_scan_kernel(rows_ref, *refs, carried, last):
    refs, outs = refs[:-2], refs[-2:]
    rows = rows_ref[...]
    top = total = mixed = None
    if carried:
        mixed, top = refs[0][...].astype(f32), refs[1][...]
        total = jnp.ones_like(top)
        refs = refs[2:]
    for at in range(0, len(refs), 2):
        chunk = refs[at][...]
        if at + 1 < len(refs):
            chunk = jnp.concatenate([chunk, refs[at + 1][...]], 0)
        logits = nt(rows, chunk)
        here = jnp.max(logits, 1, keepdims=True)
        if top is None:
            top = here
            power = jnp.exp(logits - top)
            total = jnp.sum(power, 1, keepdims=True)
            mixed = nn(power.astype(bf16), chunk)
        else:
            joint = jnp.maximum(top, here)
            shrink = jnp.exp(top - joint)
            power = jnp.exp(logits - joint)
            total = total * shrink + jnp.sum(power, 1, keepdims=True)
            mixed = mixed * shrink + nn(power.astype(bf16), chunk)
            top = joint
    lse = top + jnp.log(total)
    if not last:
        outs[0][...], outs[1][...] = mixed / total, lse
    else:
        for part in range(2):

            @pl.when(pl.program_id(0) == part)
            def _():
                write_with_lse(outs[part], mixed / total, lse)


def head_scan(rows, chunks, carry=(), last=True):
    count, block = rows.shape[0], rows.shape[0] // 2
    vocab = sum(chunk.shape[0] for chunk in chunks)
    wide = pl.BlockSpec((block, D), lambda i: (i, 0))
    thin = pl.BlockSpec((block, 1), lambda i: (i, 0))
    if last:
        out_specs = [pl.BlockSpec((block, D + LANES), lambda i: (0, 0))] * 2
        out_shape = [jax.ShapeDtypeStruct((block, D + LANES), bf16)] * 2
    else:
        out_specs = [wide, thin]
        out_shape = [jax.ShapeDtypeStruct((count, D), f32), jax.ShapeDtypeStruct((count, 1), f32)]
    return pl.pallas_call(
        lambda *refs: head_scan_kernel(*refs, carried=bool(carry), last=last),
        grid=(count // block,),
        in_specs=[wide]
        + [wide, thin][: len(carry)]
        + [
            pl.BlockSpec(chunk.shape, lambda i: (0, 0), pipeline_mode=pl.Buffered(1))
            for chunk in chunks
        ],
        out_specs=out_specs,
        out_shape=out_shape,
        compiler_params=pltpu.CompilerParams(vmem_limit_bytes=VMEM),
        cost_estimate=pl.CostEstimate(
            flops=4 * count * vocab * D, bytes_accessed=2 * vocab * D + 4 * count * D,
            transcendentals=count * vocab,
        ),
        name="head_scan",
    )(rows, *carry, *chunks)


def head_grad_kernel(table_ref, rows_ref, lse_ref, weight_ref, *refs):
    out_ref = refs[-1]
    rows = rows_ref[...]
    logits = nt(table_ref[...], rows)
    grad = (jnp.exp(logits - lse_ref[0]) * weight_ref[0]).astype(bf16)
    part = nn(grad, rows)

    @pl.when(pl.program_id(0) == 0)
    def _():
        out_ref[...] = part if len(refs) == 1 else refs[0][...] + part

    @pl.when(pl.program_id(0) > 0)
    def _():
        out_ref[...] += part


def head_grad(table_low, rows, lse, weight, first, quarters, carry=()):
    vocab, count, block = table_low.shape[0], rows.shape[0], HEAD_BLOCK
    steps = count // block
    start, part = steps * first // 4, steps * quarters // 4
    stat = pl.BlockSpec((1, 1, block), lambda i: (i + start, 0, 0))
    whole = pl.BlockSpec((vocab, D), lambda i: (0, 0))
    return pl.pallas_call(
        head_grad_kernel,
        grid=(part,),
        in_specs=[whole, pl.BlockSpec((block, D), lambda i: (i + start, 0)), stat, stat]
        + [whole] * len(carry),
        out_specs=whole,
        out_shape=jax.ShapeDtypeStruct((vocab, D), f32),
        compiler_params=pltpu.CompilerParams(vmem_limit_bytes=VMEM),
        cost_estimate=pl.CostEstimate(
            flops=quarters * count * vocab * D, bytes_accessed=count * D + 6 * vocab * D,
            transcendentals=quarters * count * vocab // 4,
        ),
        name="head_grad",
    )(table_low, rows, lse.reshape(steps, 1, block), weight, *carry)


def permute(value, axis, target):
    return lax.ppermute(value, axis, [(i, target(i)) for i in range(lax.axis_size(axis))])


def other_core(value):
    return permute(value, "mp", lambda i: i ^ 1)


def along_x(value, step):
    chips = lax.axis_size("mp") // 2
    return permute(value, "mp", lambda i: (i // 2 + step) % chips * 2 + i % 2)


def ring_order(count):
    return list(range(0, count, 2)) + list(range(count - 1, 0, -2))


def after(value, *others):
    return lax.optimization_barrier((value, *others))[0]


def ring_hop(upward, downward):
    count = lax.axis_size("dp")
    order = ring_order(count)
    spot = [order.index(i) for i in range(count)]
    return (
        permute(upward, "dp", lambda i: order[(spot[i] + 1) % count]),
        permute(downward, "dp", lambda i: order[(spot[i] - 1) % count]),
    )


def ring_middle(first, gates):
    upward, downward = first
    pieces = []
    for step in range(2, lax.axis_size("dp") // 2):
        upward, downward, _ = lax.optimization_barrier(
            (upward, downward, gates[min(step - 2, len(gates) - 1)])
        )
        upward, downward = ring_hop(upward, downward)
        pieces += [upward, downward]
    return pieces


def one_hot(index, count):
    return (index[:, None] == jnp.arange(count, dtype=jnp.int32)[None, :]).astype(bf16)


def placed(index, values, count):
    hit = index[None, :] == jnp.arange(count, dtype=jnp.int32)[:, None]
    return jnp.max(jnp.where(hit, values[None, :], -1), 1)


def rank_before(choice):
    count = choice.shape[0]
    earlier = (
        jnp.arange(count)[None, :] < jnp.arange(count)[:, None]
    ).astype(bf16)
    return jnp.dot(earlier, choice.astype(bf16), preferred_element_type=f32)


def grad_pack_kernel(core_ref, *refs, plan, rows_of, world):
    refs = dict(enumerate(refs))
    for left, right, held in plan:
        refs[held][...] = tn(refs[left][...], refs[right][...])
    mine_ref, theirs_ref = refs[rows_of[-1][0]], refs[rows_of[-1][0] + 1]
    second = core_ref[0] == 1
    total = mine_ref.shape[1]
    for j in range(world // 2):
        mine, theirs, filled = [], [], 0
        for held, rows, column in rows_of[:-1]:
            if column is None:
                mine.append(refs[held][...])
                theirs.append(mine[-1])
                filled += rows
                continue
            low = refs[held][2 * j * rows : (2 * j + 1) * rows, column : column + D]
            high = refs[held][(2 * j + 1) * rows : (2 * j + 2) * rows, column : column + D]
            mine.append(jnp.where(second, high, low))
            theirs.append(jnp.where(second, low, high))
            filled += rows
        if filled < total:
            mine.append(jnp.zeros((total - filled, D), f32))
            theirs.append(mine[-1])
        mine_ref[j] = jnp.concatenate(mine, 0).astype(bf16)
        theirs_ref[j] = jnp.concatenate(theirs, 0).astype(bf16)


def grad_pack(products, rows, world):
    core = jnp.reshape(lax.axis_index("mp") % 2, (1,)).astype(jnp.int32)
    operands = [value for product in products for value in product] + list(rows)
    inputs, count = len(operands), len(products)
    plan = [(2 * i, 2 * i + 1, inputs + 2 + i) for i in range(count)]
    pieces, scratch, flops = [], [], 0
    for i, (left, right) in enumerate(products):
        flops += 2 * left.shape[0] * left.shape[1] * right.shape[1]
        scratch.append(pltpu.VMEM((left.shape[1], right.shape[1]), f32))
        for column in range(0, right.shape[1], D):
            pieces.append((inputs + 2 + i, left.shape[1] // world, column))
    for i, value in enumerate(rows):
        pieces.append((2 * count + i, value.shape[0], None))
    total = -(-sum(piece[1] for piece in pieces) // 16) * 16
    pieces.append((inputs, 0, 0))
    shape = jax.ShapeDtypeStruct((world // 2, total, D), bf16)
    return pl.pallas_call(
        lambda *refs: grad_pack_kernel(*refs, plan=plan, rows_of=pieces, world=world),
        in_specs=[pl.BlockSpec(memory_space=pltpu.SMEM)]
        + [pl.BlockSpec(memory_space=pltpu.VMEM)] * inputs,
        out_specs=[pl.BlockSpec(memory_space=pltpu.VMEM)] * 2,
        out_shape=[shape, shape],
        scratch_shapes=scratch,
        compiler_params=pltpu.CompilerParams(vmem_limit_bytes=VMEM),
        cost_estimate=SMALL_COST,
        name="grad_pack",
    )(core, *operands)


class RingSum:

    def __init__(self, mine, theirs, x_first=False, gate=None):
        self.count = lax.axis_size("dp")
        self.chips = lax.axis_size("mp") // 2
        self.x_first = x_first
        shape = (self.count, self.chips, -1, D)
        got = other_core(theirs)
        got = (got if gate is None else after(got, gate)).reshape(shape)
        self.terms = [mine.reshape(shape), got]
        if x_first:
            chip = lax.axis_index("mp") // 2

            def for_chip(index):
                return sum(
                    lax.dynamic_index_in_dim(term, index, 1, keepdims=False).astype(f32)
                    for term in self.terms
                ).astype(bf16)

            self.terms = [for_chip(chip)] + [
                along_x(for_chip((chip + step) % self.chips), step)
                for step in range(1, self.chips)
            ]
        side, at = lax.axis_index("dp") % 2, lax.axis_index("dp") // 2
        self.here = jnp.where(side == 0, at, self.count - 1 - at)
        self.up_steps, self.down_steps = self.count // 2, (self.count - 1) // 2
        self.upward = self.downward = None
        self.step = 0

    def ready(self, *gates):
        if gates:
            self.terms[-1] = after(self.terms[-1], *gates)
        self.upward = self.part(self.up_steps).astype(bf16)
        self.downward = self.part(-self.down_steps).astype(bf16)

    def part(self, step):
        spot = lax.rem(self.here + step + self.count, self.count)
        at = jnp.where(2 * spot < self.count, 2 * spot, 2 * (self.count - 1 - spot) + 1)
        return sum(
            lax.dynamic_index_in_dim(term, at, 0, keepdims=False).astype(f32)
            for term in self.terms
        )

    def hop(self, gate=None):
        self.step += 1
        step, down = self.step, self.downward
        self.upward, down = ring_hop(self.upward, down)
        if gate is not None:
            self.upward, down, _ = lax.optimization_barrier((self.upward, down, gate))
        if step <= self.down_steps:
            self.downward = down
        if step < self.up_steps:
            self.upward = (self.upward.astype(f32) + self.part(self.up_steps - step)).astype(bf16)
        if step < self.down_steps:
            self.downward = (self.downward.astype(f32) + self.part(step - self.down_steps)).astype(
                bf16
            )

    def wait(self, gate):
        self.upward, self.downward, _ = lax.optimization_barrier((self.upward, self.downward, gate))

    def total(self):
        while self.step < self.up_steps:
            self.hop()
        line = self.part(0) + self.upward.astype(f32) + self.downward.astype(f32)
        if self.x_first:
            return [line]
        line = line.astype(bf16)
        chip = lax.axis_index("mp") // 2
        terms = [lax.dynamic_index_in_dim(line, chip, 0, keepdims=False)]
        for step in range(1, self.chips):
            going = lax.dynamic_index_in_dim(line, (chip + step) % self.chips, 0, keepdims=False)
            terms.append(along_x(going, step))
        return terms


def renew(weight, moment, average, gradient, factor):
    clipped = gradient * factor
    moment_new = MOMENTUM * moment + clipped
    weight_new = weight - STEP_RATE * (clipped + MOMENTUM * moment_new)
    average_new = AVERAGE_DECAY * average + (1.0 - AVERAGE_DECAY) * weight_new
    return (weight_new, moment_new, average_new)


def finish_sum_kernel(*refs, count):
    (row_ref, *square_refs), terms, (total_ref, spread_ref) = (
        refs[:count], refs[count:-2], refs[-2:]
    )
    total = sum((term[...].astype(f32) for term in terms[1:]), terms[0][...].astype(f32))
    total_ref[...] = total
    squares = jnp.sum(jnp.sum(total * total, 0, keepdims=True), 1, keepdims=True)
    lane = lax.broadcasted_iota(jnp.int32, (1, LANES), 1)
    for ref in square_refs:
        squares = squares + ref[...]
    row = row_ref[...] + jnp.where(lane == 0, squares, 0.0)
    spread_ref[...] = jnp.broadcast_to(row, spread_ref.shape)


def finish_sum(terms, numbers, world):
    vmem = pl.BlockSpec(memory_space=pltpu.VMEM)
    return pl.pallas_call(
        lambda *refs: finish_sum_kernel(*refs, count=len(numbers)),
        in_specs=[vmem] * (len(numbers) + len(terms)),
        out_specs=[vmem] * 2,
        out_shape=[
            jax.ShapeDtypeStruct(terms[0].shape, f32),
            jax.ShapeDtypeStruct((world, LANES), f32),
        ],
        compiler_params=pltpu.CompilerParams(vmem_limit_bytes=VMEM),
        name="finish_sum",
    )(*numbers, *terms)


def clip_factor(totals):
    return jnp.minimum(1.0, CLIP_LIMIT / jnp.sqrt(totals[:, 0:1]))


def renew_kernel(spread_ref, early_ref, late_ref, *refs):
    states, outs = [refs[i : i + 3] for i in range(0, 12, 3)], refs[12:]
    totals = jnp.sum(spread_ref[...], 0, keepdims=True)
    outs[-1][...] = totals
    factor = clip_factor(totals)
    rows = states[1][0].shape[0]
    rows_patch, rows_down = states[0][0].shape[0], states[3][0].shape[0]
    attn = [(early_ref, j * rows, rows) for j in range(3)]
    attn.append((late_ref, 4 * rows + rows_down, rows))
    pieces = (
        [(early_ref, 3 * rows, rows_patch)],
        attn,
        [(late_ref, j * rows, rows) for j in range(4)],
        [(late_ref, 4 * rows, rows_down)],
    )
    for index, (state, parts) in enumerate(zip(states, pieces)):
        new = outs[4 * index : 4 * index + 4]
        for j, (ref, start, count) in enumerate(parts):
            at = slice(j * D, (j + 1) * D)
            gradient = ref[start : start + count, :]
            results = renew(
                state[0][:, at], state[1][:, at], state[2][:, at], gradient, factor
            )
            for out, value in zip(new, results):
                out[:, at] = value
            new[3][:, at] = results[0].astype(bf16)


def renew_matrices(spread, early, late, states):
    vmem = pl.BlockSpec(memory_space=pltpu.VMEM)
    shapes = []
    for state in states:
        shape = state[0].shape
        shapes += [jax.ShapeDtypeStruct(shape, f32)] * 3 + [jax.ShapeDtypeStruct(shape, bf16)]
    shapes.append(jax.ShapeDtypeStruct((1, LANES), f32))
    return pl.pallas_call(
        renew_kernel,
        in_specs=[vmem] * 15,
        out_specs=[vmem] * len(shapes),
        out_shape=shapes,
        compiler_params=pltpu.CompilerParams(vmem_limit_bytes=VMEM),
        name="renew_matrices",
    )(spread, early, late, *[value for state in states for value in state])


def shards(
    patches,
    patch_pos,
    owner,
    local_row,
    counts,
    task,
    table,
    table_mom,
    table_avg,
    patch_w,
    patch_mom,
    patch_avg,
    attn_w,
    attn_mom,
    attn_avg,
    up_w,
    up_mom,
    up_avg,
    down_w,
    down_mom,
    down_avg,
    gains,
    gain_mom,
    gain_avg,
):
    groups, owners = lax.axis_size("dp"), lax.axis_size("mp")
    world = groups * owners
    tokens_here = patches.shape[0]
    rows_own = table.shape[0]
    rows_attn, rows_patch, rows_down = attn_w.shape[0], patch_w.shape[0], down_w.shape[0]
    cols_gain = gains.shape[1]
    place = lax.axis_index("dp") * owners + lax.axis_index("mp")

    table_low = table.astype(bf16)
    gain_row = jnp.pad(gains.astype(bf16).reshape(1, 3 * cols_gain), ((0, 0), (0, 4 * D - 3 * cols_gain)))
    patch_rows = jnp.pad(patch_w.astype(bf16), ((0, -rows_patch % 4), (0, 0)))
    early = jnp.concatenate([attn_w.astype(bf16), patch_rows.reshape(-1, 4 * D), gain_row], 0)
    late = jnp.concatenate(
        [
            up_w.astype(bf16),
            jnp.concatenate(
                [down_w[j : j + rows_attn] for j in range(0, rows_down, rows_attn)], 1
            ).astype(bf16),
        ],
        0,
    )
    early_all, late_all = (
        lax.all_gather(jnp.pad(w, ((0, -w.shape[0] % 8), (0, 0))), AXES, axis=0, tiled=False)
        for w in (early, late)
    )

    first_pieces = ring_hop(table_low, table_low)

    my_counts = lax.dynamic_slice_in_dim(counts, place, 1, 0)
    first_tok, alive = my_counts[0, 0], my_counts[0, 1]
    positions = jnp.arange(tokens_here, dtype=jnp.int32)
    is_patch = (positions < first_tok)[:, None]
    is_token = (positions >= first_tok) & (positions < first_tok + alive)
    target_owner = owner[:, 0]

    share = -(-3 * tokens_here // (2 * world) // 16) * 16
    identity = target_owner * (rows_own * groups) + local_row
    same = (identity[:, None] == identity[None, :]) & is_token[None, :]
    first_same = jnp.min(jnp.where(same, positions[None, :], tokens_here), 1)
    leads = is_token & (first_same == positions)
    dest = identity // rows_own
    leads_to = (dest[:, None] == jnp.arange(world)[None, :]) & leads[:, None]
    lead_rank = jnp.sum(jnp.where(leads_to, rank_before(leads_to), 0.0), 1).astype(jnp.int32)
    far_rank = jnp.max(
        jnp.where(first_same[:, None] == positions[None, :], lead_rank[None, :], 0), 1
    )
    far_row = identity - dest * rows_own
    most = jnp.max(jnp.sum(leads_to.astype(jnp.int32), 0))

    def far_slots(start, share):
        within = far_rank - start
        fits = is_token & (within >= 0) & (within < share)
        return jnp.where(fits, dest * share + within, -1)

    def far_ids(slots, extra, share):
        ids = placed(slots, far_row, world * share).reshape(world, share)
        ids = jnp.concatenate([ids, jnp.full((world, 1), extra, jnp.int32)], 1)
        return lax.all_to_all(ids, ("mp", "dp"), split_axis=0, concat_axis=0, tiled=True)

    first_slots = far_slots(0, share)
    first_ids = far_ids(first_slots, most, share)
    few = 16
    turns = (jnp.max(first_ids[:, share]) - share + few - 1) // few

    def far_fetch(slots, ids, share):
        spread = one_hot(ids[:, :share].reshape(-1), rows_own)
        rows = jnp.dot(spread, table_low, preferred_element_type=f32).astype(bf16)
        rows = lax.optimization_barrier((rows, *first_pieces))[0]
        return lax.all_to_all(
            rows.reshape(world, share, D), ("mp", "dp"), split_axis=0, concat_axis=0, tiled=True
        ).reshape(world * share, D)

    def far_spread(slots, arrived, share):
        return jnp.dot(one_hot(slots, world * share), arrived, preferred_element_type=f32)

    def far_pack(slots, values, share):
        return jnp.dot(
            one_hot(slots, world * share).T, values, preferred_element_type=f32
        ).astype(bf16)

    def far_send(packed, share):
        return lax.all_to_all(
            packed.reshape(world, share, D),
            ("mp", "dp"), split_axis=0, concat_axis=0, tiled=True,
        ).reshape(world * share, D)

    def far_add(arrived, ids, share):
        spread = one_hot(ids[:, :share].reshape(-1), rows_own)
        return tn(spread, arrived)


    def columns(gathered, low, high):
        return gathered[:, :rows_attn, low * D : high * D].reshape(-1, (high - low) * D)

    w_q, w_kv, w_out = columns(early_all, 0, 1), columns(early_all, 1, 3), columns(early_all, 3, 4)
    gain_at = rows_attn + patch_rows.shape[0] // 4
    w_patch = (
        early_all[:, rows_attn:gain_at].reshape(world, -1, D)[:, :rows_patch].reshape(-1, D)
    )
    gain_all = (
        early_all[:, gain_at, : 3 * cols_gain]
        .reshape(world, 3, cols_gain).transpose(1, 0, 2).reshape(3, D).astype(f32)
    )
    scored_all = counts[:, 2].astype(f32)
    per_task = (task[:, None] == jnp.arange(TASKS)[None, :]).astype(f32)
    task_total = jnp.sum(per_task * scored_all[:, None], 0)
    present = jnp.sum((task_total > 0).astype(f32))
    inverse_seq = jnp.sum(per_task / jnp.maximum(task_total, 1.0)[None, :], 1)
    row_live = (jnp.arange(LOSS)[None, :] < counts[:, 2:3]).astype(f32) * inverse_seq[:, None]
    head_weight = (row_live / present).reshape(-1, 1, HEAD_BLOCK)

    arrived = far_fetch(first_slots, first_ids, share)
    arrived, head_weight = lax.optimization_barrier((arrived, head_weight, w_kv, w_q, w_patch))[:2]
    looked = far_spread(first_slots, arrived, share)

    def fetch_turn(turn, total):
        slots = far_slots(share + turn * few, few)
        return total + far_spread(slots, far_fetch(slots, far_ids(slots, 0, few), few), few)

    looked = lax.fori_loop(0, turns, fetch_turn, looked)

    w_up = columns(late_all, 0, 4)
    w_down = jnp.concatenate(
        [late_all[:, rows_attn : 2 * rows_attn, j : j + D] for j in range(0, 4 * D, D)], 1
    ).reshape(world * rows_down, D)

    def patch_rows_of(pixels):
        position_code = (patch_pos[:, None] == jnp.arange(POSN)[None, :]).astype(bf16)
        return jnp.concatenate([pixels, position_code], 1)

    patch_in = patch_rows_of(patches)
    from_patch = jnp.dot(patch_in, w_patch, preferred_element_type=f32)
    embed_scale = math.sqrt(D)
    embedded = jnp.where(is_patch, from_patch, 0.0) + embed_scale * looked
    normed_first = layer_norm(embedded, gain_all[0]).astype(bf16)
    key_values = jnp.dot(normed_first, w_kv, preferred_element_type=f32).astype(bf16)

    pick = first_tok - 1
    pick_at = jnp.reshape(pick, (1,))

    def picked_rows(values, start=pick):
        return lax.dynamic_slice_in_dim(values, start, LOSS, 0)

    normed_pick = picked_rows(normed_first)
    query_pick = jnp.dot(normed_pick, w_q, preferred_element_type=f32).astype(bf16)
    attended_pick, lse_pick = attention_pick(pick_at, query_pick, key_values)
    branch_pick = jnp.dot(attended_pick, w_out, preferred_element_type=f32)
    middle_pick = picked_rows(embedded) + branch_pick
    normed_mid, mid_back = jax.vjp(layer_norm, middle_pick, gain_all[1])
    normed_mid = normed_mid.astype(bf16)
    query_all = jnp.dot(normed_first, w_q, preferred_element_type=f32).astype(bf16)
    attended = attention_all(after(query_all, attended_pick), key_values)
    normed_mid = after(normed_mid, attended)
    hidden_pick = jnp.dot(normed_mid, w_up, preferred_element_type=f32)
    active_f32, gelu_back = jax.vjp(gelu_tanh, hidden_pick)
    active_pick = active_f32.astype(bf16)
    result_pick = middle_pick + jnp.dot(active_pick, w_down, preferred_element_type=f32)
    final_rows, final_back = jax.vjp(layer_norm, result_pick, gain_all[2])
    own_rows = final_rows.astype(bf16)
    chunks = [table_low, *first_pieces, *ring_middle(first_pieces, (arrived, attended))]
    half = rows_own // 32 * 16
    last_up, last_down = after(chunks[-2], own_rows)[:half], after(chunks[-1], own_rows)[half:]
    chunks += ring_hop(last_up, last_down)
    target_rows = picked_rows(looked, first_tok)

    chips = owners // 2
    line = jnp.stack([own_rows] + [along_x(own_rows, step) for step in range(1, chips)])
    group_rows = jnp.stack([line, other_core(line)])
    group_rows = group_rows.reshape(-1, D)
    carry = head_scan(after(group_rows, last_up, last_down), chunks[:5], last=False)
    rows_sent = after(own_rows, carry[0], chunks[-1], chunks[-2])
    mine, theirs = head_scan(group_rows, chunks[5:], carry)
    (line,) = merge([mine, other_core(theirs)])
    mean_own, own_total = merge(
        [line[:LOSS]]
        + [along_x(line[step * LOSS : (step + 1) * LOSS], -step) for step in range(1, chips)],
        last=True,
    )
    own_total = own_total[:, 0]

    picked = jnp.sum(own_rows.astype(f32) * target_rows, 1)
    own_weight = lax.dynamic_slice_in_dim(row_live, place, 1, 0)[0]
    loss_part = jnp.sum(own_weight * (own_total - picked))

    rows_all = lax.all_gather(rows_sent, AXES, axis=0, tiled=True)
    total_all = lax.all_to_all(
        jnp.broadcast_to(own_total[None, :], (world, LOSS)), AXES, 0, 0, tiled=True
    )

    scaled_weight = (own_weight / present)[:, None]
    grad_rows = scaled_weight * (mean_own - target_rows)
    grad_result, grad_gain_last = final_back(grad_rows)
    grad_second = grad_result.astype(bf16)
    grad_hidden = gelu_back(nt(grad_second, w_down))[0].astype(bf16)
    grad_middle, grad_gain_mid = mid_back(nt(grad_hidden, w_up))
    grad_middle = grad_result + grad_middle
    grad_branch = grad_middle.astype(bf16)
    late_mine, late_theirs = grad_pack(
        [(normed_mid, grad_hidden), (active_pick, grad_second), (attended_pick, grad_branch)],
        [], world,
    )
    grad_attended = after(nt(grad_branch, w_out).astype(bf16), late_theirs)
    grad_q, grad_k, grad_v = attention_back(
        pick_at, query_pick, key_values, attended_pick, grad_attended, lse_pick
    )
    late_sum = RingSum(late_mine, late_theirs, gate=grad_q)
    late_sum.ready()
    grad_patch_rows, grad_looked, grad_gain_first = first_back(
        jnp.reshape(first_tok, (1,)), after(grad_k, late_sum.upward, total_all), grad_v, w_kv, grad_q, w_q,
        embedded, gain_all[0:1], grad_middle, -scaled_weight * own_rows.astype(f32),
    )
    late_sum.hop(grad_looked)
    packed = far_pack(first_slots, after(grad_looked, late_sum.upward), share)
    grad_arrived = far_send(packed, share)
    grad_gain = jnp.stack([grad_gain_first[0], grad_gain_mid, grad_gain_last])
    early_mine, early_theirs = grad_pack(
        [
            (normed_pick, grad_q),
            (normed_first, grad_k),
            (normed_first, grad_v),
            (patch_rows_of(after(patches, packed)), after(grad_patch_rows, packed)),
        ],
        [grad_gain], world,
    )

    lane = lax.broadcasted_iota(jnp.int32, (1, LANES), 1)
    row = layer_stats(
        jnp.reshape(first_tok + alive, (1,)), after(attended, early_theirs), embedded, w_out, w_up,
        w_down, gain_all[1:2], jnp.where(lane == 1, loss_part, 0.0),
    )

    early_sum = RingSum(early_mine, early_theirs, True, gate=row)
    head_part = head_grad(
        table_low, after(rows_all, early_sum.terms[0]), total_all, head_weight, 0, 2
    )
    grad_arrived = after(grad_arrived, head_part)
    late_sum.hop(grad_arrived)
    head_part = head_part + far_add(after(grad_arrived, late_sum.upward), first_ids, share)
    early_sum.ready(head_part)
    head_part = head_grad(
        table_low, after(rows_all, late_sum.upward, early_sum.upward), total_all, head_weight, 2, 1,
        (head_part,),
    )
    late_sum.hop(head_part)
    early_sum.hop(late_sum.upward)
    table_head = head_grad(
        table_low, after(rows_all, late_sum.upward, early_sum.upward), total_all, head_weight, 3, 1,
        (head_part,),
    )
    late_sum.hop(table_head)
    early_sum.hop(late_sum.upward)
    grad_table = table_head
    late_terms = late_sum.total()
    (summed_early,) = early_sum.total()

    def next_turn(turn, total):
        slots = far_slots(share + turn * few, few)
        return total + far_add(
            far_send(far_pack(slots, grad_looked, few), few), far_ids(slots, 0, few), few
        )

    grad_table = lax.fori_loop(0, turns, next_turn, grad_table)

    edge = 3 * rows_attn + rows_patch
    summed_gain = lax.dynamic_slice_in_dim(
        summed_early[edge : edge + 3], place * cols_gain, cols_gain, 1
    )
    squares = [
        jnp.sum(part * part, keepdims=True) for part in (grad_table, summed_early[:edge], summed_gain)
    ]
    summed_late, spread = finish_sum(late_terms, [row, *squares], world)
    spread = lax.all_to_all(spread, AXES, 0, 0, tiled=True)
    *matrices, totals = renew_matrices(
        spread, summed_early, summed_late,
        (
            (patch_w, patch_mom, patch_avg),
            (attn_w, attn_mom, attn_avg),
            (up_w, up_mom, up_avg),
            (down_w, down_mom, down_avg),
        ),
    )
    factor = clip_factor(jnp.sum(spread, 0, keepdims=True))[0, 0]
    table_new = renew(table, table_mom, table_avg, grad_table, factor)
    gains_new = renew(gains, gain_mom, gain_avg, summed_gain, factor)
    clip_norm = jnp.sqrt(totals[0, 0])
    loss_total = totals[0, 1]
    valid_total = jnp.sum(counts[:, :2].astype(f32))
    rms_stats = jnp.sqrt(totals[0, 2:6] / valid_total)
    return (
        *table_new, table_new[0].astype(bf16), *matrices, *gains_new,
        loss_total, present, clip_norm, rms_stats,
    )


def solution(mesh):
    whole, split = P(), P(AXES)
    rows, vocab, columns = P(AXES, None), P(("mp", "dp"), None), P(None, AXES)
    in_specs = (rows, split, rows, split, whole, whole) + (vocab,) * 3 + (rows,) * 12 + (columns,) * 3
    out_specs = (vocab,) * 4 + (rows,) * 16 + (columns,) * 3 + (whole,) * 4
    return jax.shard_map(shards, mesh=mesh, in_specs=in_specs, out_specs=out_specs, check_vma=False)
```
